128 devices in a mesh: dp: 8 (over x, y_hi), ctx: 16 (over z, y_lo, core).
Axes of the slice: x: 4, y: 4 (y_hi: 2, y_lo: 2; y = y_hi * 2 + y_lo), z: 4, core: 2. Of those that a mesh axis runs over, the one named last changes fastest.
Arguments:
- q_raw: bfloat16 [8, 8192, 1024], P('dp', 'ctx'), may hold values from -6 to 6
- k_raw: bfloat16 [8, 8192, 128], P('dp', 'ctx'), may hold values from -6 to 6
- values: bfloat16 [8, 8192, 128], P('dp', 'ctx'), may hold values from -6 to 6
- d_out: bfloat16 [8, 8192, 1024], P('dp', 'ctx'), may hold values from -160 to 160
- q_gain: float32 [128], replicated, may hold values from 0.5 to 7
- k_gain: float32 [128], replicated, may hold values from 0.5 to 7
- resp_len: int32 [8, 8], P('dp'), may hold values from 1 to 1408, as said below
- block_parent: int32 [8, 64], P('dp'), may hold values from -1 to 62, as said below
- block_from: int32 [8, 64], P('dp', 'ctx'), may hold values from 0 to 63, as said below
Outputs:
- grad_q: bfloat16 [8, 8192, 1024], P('dp', 'ctx')
- grad_k: bfloat16 [8, 8192, 128], P('dp', 'ctx')
- grad_v: bfloat16 [8, 8192, 128], P('dp', 'ctx')
- q_gain_grad: float32 [128], replicated
- k_gain_grad: float32 [128], replicated
The draws below stay inside these ranges and needn't reach their ends.
Inputs may be any that keep to these rules, and one draw needn't show every extreme that they name: The responses of a tree follow the prompt's 16 blocks in order and fill its 64 blocks exactly; response r takes ceil(resp_len[t, r] / 128) blocks; the last response of each tree has exactly 11 blocks, all tokens live, and none has more. `block_parent`: block 0 has parent -1; prompt block b > 0 has parent b - 1; the first block of a response has parent 16 - 1 and its other blocks the block before. No block has more than 26 ancestors. Each block number appears once in a tree, and block_from[t, j] // 4 == j // 4.
All inputs are finite; a program needn't handle non-finite values.
Results may differ from the reference program's by a relative error of at most 0.035.
The reference program's roundings to bfloat16 on the way (of `d_tree`, `d_mask`, `chances_b` and `d_scores`) count: a program that leaves them out, or rounds other values in their place, can miss the bound.
Values may be sent and summed in bfloat16 or wider, within the bound.
A program may use at most 128 MiB of HBM per device.

```python
import math
import jax
import jax.numpy as jnp
from jax import lax

HD = 128
QH = 8
BLK = 128
RESP = 8
TREES = 8
TREE = 8192
NBLK = 64
BPD = 4
RBASE = 6
PBLK = 16
DEPTH = 27


def response_counts(key):

    def per_tree(tree_key):
        first_key, second_key = jax.random.split(tree_key)
        shuffled = jax.random.permutation(first_key, RESP).astype(jnp.int32)
        where_last = jnp.argmax(shuffled == RESP - 1)
        shuffled = shuffled.at[where_last].set(shuffled[0]).at[0].set(RESP - 1)
        moved = jax.random.randint(second_key, (RESP // 2,), 0, RBASE)
        moved = moved.at[0].set(RBASE - 1)
        counts = jnp.full((RESP,), RBASE, jnp.int32)
        counts = counts.at[shuffled[0::2]].add(moved).at[shuffled[1::2]].add(-moved)
        return (counts, shuffled[0])
    return jax.vmap(per_tree)(jax.random.split(key, TREES))


def drawn_base(key):
    first_key = jax.random.fold_in(key, 0)
    key_drawn = jax.random.truncated_normal(first_key, -5.0, 5.0, (TREES, TREE, HD))
    return key_drawn


def draw_resp_len(key, part):
    counts, longest = response_counts(key)
    key = jax.random.fold_in(key, 11)
    last_fill = jax.random.randint(key, (TREES, RESP), 1, BLK + 1)
    lengths = BLK * (counts - 1) + last_fill
    full = jnp.arange(RESP, dtype=jnp.int32)[None, :] == longest[:, None]
    return jnp.where(full, BLK * counts, lengths).astype(jnp.int32)


def draw_block_parent(key, part):
    counts, longest = response_counts(key)
    block_ends = PBLK + jnp.cumsum(counts, axis=1, dtype=jnp.int32)
    block_starts = block_ends - counts
    blocks = jnp.arange(NBLK, dtype=jnp.int32)
    opening = jnp.any(blocks[None, :, None] == block_starts[:, None, :], axis=2)
    return jnp.where(opening, PBLK - 1, blocks[None, :] - 1).astype(jnp.int32)


def draw_block_from(key, part):
    key = jax.random.fold_in(key, 13)
    groups = NBLK // BPD
    tree_keys = jax.random.split(key, TREES * groups)
    shuffles = jax.vmap(lambda group_key: jax.random.permutation(group_key, BPD))(tree_keys)
    shuffles = shuffles.reshape(TREES, NBLK).astype(jnp.int32)
    group_base = jnp.arange(NBLK, dtype=jnp.int32) // BPD * BPD
    return shuffles + group_base[None, :]


def draw_k_raw(key, part):
    key_drawn = drawn_base(key)
    result = key_drawn
    return result.astype(jnp.bfloat16)


def draw_q_raw(key, part):
    key = jax.random.fold_in(key, 19)
    queries = jax.random.truncated_normal(key, -5.0, 5.0, (TREES, TREE, QH, HD))
    return queries.reshape(TREES, TREE, QH * HD).astype(jnp.bfloat16)


def draw_d_out(key, part):
    key = jax.random.fold_in(key, 31)
    first_key = jax.random.fold_in(key, 0)
    position = jnp.arange(TREE, dtype=jnp.float32) / max(TREE - 1, 1)
    tree_ramp = jnp.arange(TREES, dtype=jnp.float32) / max(TREES - 1, 1)
    row_ramp = ((1.0 + 2.0 * tree_ramp)[:, None] * (1.0 + 2.0 * position)[None, :])[:, :, None]
    entries = jax.random.truncated_normal(first_key, -4.0, 4.0, (TREES, TREE, QH * HD))
    return (entries * row_ramp).astype(jnp.bfloat16)


def draw_q_gain(key, part):
    key = jax.random.fold_in(key, 23)
    return jnp.exp(jax.random.uniform(key, (HD,), minval=math.log(0.5), maxval=math.log(2.5)))


def draw_k_gain(key, part):
    key = jax.random.fold_in(key, 29)
    return jnp.exp(jax.random.uniform(key, (HD,), minval=math.log(0.5), maxval=math.log(2.5)))


def steps_of(stream_key, extent, cuts, smallest, top_value):
    factor_of = 1.0
    for axis_at, blocks in cuts:
        steps = jax.random.uniform(jax.random.fold_in(jax.random.fold_in(stream_key, 6), axis_at), (blocks,), jnp.float32, smallest / len(cuts), top_value / len(cuts))
        factor_of = factor_of * jnp.repeat(jnp.exp(steps), extent[axis_at] // blocks).reshape((-1,) + (1,) * (len(extent) - 1 - axis_at))
    return factor_of


def scatter_about(key, shape, deviation, most, pieces=(), kind=jnp.bfloat16):
    values = deviation * jax.random.normal(key, shape, jnp.float32)
    if pieces:
        values = values * steps_of(key, shape, pieces, -0.22, 0.18)
    return jnp.clip(values, -most, most).astype(kind)


def setup_inputs(seed: int = 0) -> dict:
    arg_keys = jax.random.split(jax.random.key(seed), 10)
    q_raw = draw_q_raw(jax.random.fold_in(arg_keys[9], 71), 0)
    k_raw = draw_k_raw(jax.random.fold_in(arg_keys[9], 71), 0)
    values = scatter_about(arg_keys[2], (TREES, TREE, HD), 1.0, 6.0, ((0, 8), (1, 16)))
    d_out = draw_d_out(jax.random.fold_in(arg_keys[9], 71), 0)
    q_gain = draw_q_gain(jax.random.fold_in(arg_keys[9], 71), 0)
    k_gain = draw_k_gain(jax.random.fold_in(arg_keys[9], 71), 0)
    resp_len = draw_resp_len(jax.random.fold_in(arg_keys[9], 71), 0)
    block_parent = draw_block_parent(jax.random.fold_in(arg_keys[9], 71), 0)
    block_from = draw_block_from(jax.random.fold_in(arg_keys[9], 71), 0)
    return dict(q_raw=q_raw, k_raw=k_raw, values=values, d_out=d_out, q_gain=q_gain, k_gain=k_gain, resp_len=resp_len, block_parent=block_parent, block_from=block_from)


def contract_last(left, right):
    return lax.dot_general(left, right, (((1,), (1,)), ((), ())), preferred_element_type=jnp.float32)

def contract_first(left, right):
    return lax.dot_general(left, right, (((0,), (0,)), ((), ())), preferred_element_type=jnp.float32)

def live_tokens(resp_len, block_total, prompt_blocks):
    counts = (resp_len + BLK - 1) // BLK
    block_ends = prompt_blocks + jnp.cumsum(counts, dtype=jnp.int32)
    block_starts = block_ends - counts
    blocks = jnp.arange(block_total, dtype=jnp.int32)
    inside = (blocks[:, None] >= block_starts[None, :]) & (blocks[:, None] < block_ends[None, :])
    first_block = lax.optimization_barrier(jnp.sum(jnp.where(inside, block_starts[None, :], 0), axis=1))
    length = lax.optimization_barrier(jnp.sum(jnp.where(inside, resp_len[None, :], 0), axis=1))
    offset = (blocks - first_block)[:, None] * BLK + jnp.arange(BLK, dtype=jnp.int32)[None, :]
    alive_mask = (blocks[:, None] < prompt_blocks) | (offset < length[:, None])
    return alive_mask.reshape(-1)

def ancestors(block_parent, chain_depth):
    anchor = jnp.arange(block_parent.shape[0], dtype=jnp.int32)

    def climb(current, unused):
        parent_now = jnp.where(current >= 0, block_parent[jnp.maximum(current, 0)], -1)
        return (parent_now, parent_now)
    unused_last, climbed = lax.scan(climb, anchor, None, length=chain_depth - 1)
    return jnp.concatenate([anchor[None, :], climbed], axis=0).T

def normalize(raw, gain):
    values_f = raw.astype(jnp.float32)
    inverse_rms = lax.rsqrt(lax.optimization_barrier(jnp.mean(values_f * values_f, axis=-1, keepdims=True)) + 1e-06)
    unit_vec = values_f * inverse_rms
    return (unit_vec, inverse_rms, (unit_vec * gain).astype(jnp.bfloat16))

def unnormalize(gradient, unit_vec, inverse_rms, gain):
    scaled = gradient * gain
    return inverse_rms * (scaled - unit_vec * lax.optimization_barrier(jnp.mean(scaled * unit_vec, axis=-1, keepdims=True)))

def attend(q_blk, d_blk, keys_win, vals_win, allowed, score_scale):
    scores = contract_last(q_blk, keys_win) * score_scale
    scores = jnp.where(allowed, scores, -jnp.inf)
    row_top = lax.optimization_barrier(jnp.max(scores, axis=1, keepdims=True))
    weights = jnp.exp(scores - row_top)
    chances = weights / lax.optimization_barrier(jnp.sum(weights, axis=1, keepdims=True))
    chances_b = chances.astype(jnp.bfloat16)
    attn_out = jnp.dot(chances_b, vals_win, preferred_element_type=jnp.float32)
    row_delta = lax.optimization_barrier(jnp.sum(d_blk.astype(jnp.float32) * attn_out, axis=1, keepdims=True))
    d_chances = contract_last(d_blk, vals_win)
    d_scores = (chances * (d_chances - row_delta)).astype(jnp.bfloat16)
    query_grad = jnp.dot(d_scores, keys_win, preferred_element_type=jnp.float32) * score_scale
    key_grad = contract_first(d_scores, q_blk) * score_scale
    value_grad = contract_first(chances_b, d_blk)
    return (query_grad, key_grad, value_grad)

def block_pass(key_store, offsets, ancestry, live_all, q_blocks, d_blocks, score_scale):
    head_size = key_store.shape[2]
    head_rows = q_blocks.shape[1]
    head_count = head_rows // BLK
    chain_depth = ancestry.shape[1]
    width = chain_depth * BLK
    arange_b = jnp.arange(BLK, dtype=jnp.int32)
    later_block = jnp.arange(chain_depth, dtype=jnp.int32)[None, :, None] > 0
    earlier_col = arange_b[None, None, :] <= arange_b[:, None, None]

    def step(gradients, inputs):
        q_blk, d_blk, block_offsets, links = inputs
        key_rows = (block_offsets[:, None] + arange_b[None, :]).reshape(-1)
        window = key_store[:, key_rows]
        key_live = live_all[jnp.maximum(links, 0)[:, None] * BLK + arange_b[None, :]]
        visible = (links >= 0)[:, None] & key_live
        allowed = visible[None, :, :] & (later_block | earlier_col)
        allowed = jnp.broadcast_to(allowed.reshape(BLK, 1, width), (BLK, head_count, width)).reshape(head_rows, width)
        query_grad, key_grad, value_grad = attend(q_blk, d_blk, window[0], window[1], allowed, score_scale)
        gradients = gradients.at[:, key_rows].add(jnp.stack([key_grad, value_grad]))
        return (gradients, query_grad)
    start_grads = jnp.zeros((2, key_store.shape[1], head_size), jnp.float32)
    return lax.scan(step, start_grads, (q_blocks, d_blocks, offsets, ancestry))

def tree_pass(q_gain, k_gain, inputs):
    q_raw, k_raw, values, d_out, resp_len, block_parent, block_from = inputs
    tree_len = k_raw.shape[0]
    head_size = k_raw.shape[1]
    head_count = q_raw.shape[1] // head_size
    block_total = tree_len // BLK
    score_scale = 1.0 / math.sqrt(head_size)
    live_all = live_tokens(resp_len, block_total, PBLK)
    ancestry = ancestors(block_parent, DEPTH)
    d_blocks = d_out.reshape(block_total, BLK, head_count * head_size)
    d_tree = jnp.zeros_like(d_blocks).at[block_from].set(d_blocks).reshape(tree_len, head_count * head_size)
    d_mask = d_tree * live_all[:, None].astype(jnp.bfloat16)
    q_unit, q_inverse, q_norm = normalize(q_raw.reshape(tree_len, head_count, head_size), q_gain)
    k_unit, k_inverse, k_norm = normalize(k_raw, k_gain)
    key_store = jnp.stack([k_norm, values])
    offsets = jnp.maximum(ancestry, 0) * BLK
    gradients, query_grad = block_pass(key_store, offsets, ancestry, live_all, q_norm.reshape(block_total, BLK * head_count, head_size), d_mask.reshape(block_total, BLK * head_count, head_size), score_scale)
    d_qnorm = query_grad.reshape(tree_len, head_count, head_size)
    q_part = lax.optimization_barrier(jnp.sum(d_qnorm * q_unit, axis=(0, 1)))
    k_part = lax.optimization_barrier(jnp.sum(gradients[0] * k_unit, axis=0))
    grad_q = unnormalize(d_qnorm, q_unit, q_inverse, q_gain).astype(jnp.bfloat16).reshape(tree_len, head_count * head_size)
    grad_k = unnormalize(gradients[0], k_unit, k_inverse, k_gain).astype(jnp.bfloat16)
    grad_v = gradients[1].astype(jnp.bfloat16)
    return (grad_q, grad_k, grad_v, q_part, k_part)

def reference(q_raw, k_raw, values, d_out, q_gain, k_gain, resp_len, block_parent, block_from):

    def per_tree(inputs):
        return tree_pass(q_gain, k_gain, inputs)
    grad_q, grad_k, grad_v, q_parts, k_parts = lax.map(per_tree, (q_raw, k_raw, values, d_out, resp_len, block_parent, block_from))
    return (grad_q, grad_k, grad_v, lax.optimization_barrier(jnp.sum(q_parts, axis=0)), lax.optimization_barrier(jnp.sum(k_parts, axis=0)))
```

```python
import functools, math
import jax, jax.numpy as jnp
from jax import lax
from jax.experimental import pallas as pl
from jax.experimental.pallas import tpu as pltpu
from jax.sharding import PartitionSpec as P

BLK = 128
HEADS = 8
PROMPT = 16
REACH = 10
SLOTS = 30
OWN = PROMPT + REACH
POS = 27
RT = 1024
CBP = 8
CBL = 10
HT = RT // BLK
CS = 256
TPB = HEADS // HT
LOW = -1e30
F32 = jnp.float32
BF = jnp.bfloat16
SCALE = 1.0 / math.sqrt(128.0)
LOG2E = 1.4426950408889634
SL2 = SCALE * LOG2E


def nt(a, b):
    return lax.dot_general(a, b, (((1,), (1,)), ((), ())), preferred_element_type=F32)


def nn(a, b):
    return jnp.dot(a, b, preferred_element_type=F32)


def attend_kernel(dev_ref, len_ref, from_ref, qg_ref, q_ref, do_ref, kv_ref,
           gq_ref, away_ref, mine_ref, qpart_ref,
           qn, qt, dn, dt, kt, w_s, dp_s, m_s, s_s, f_s, dq_s, dk_ref, dv_ref):
    d = dev_ref[0]
    first = d * 4
    dk_ref[...] = jnp.zeros_like(dk_ref)
    dv_ref[...] = jnp.zeros_like(dv_ref)
    m_s[...] = jnp.full_like(m_s, LOW)
    s_s[...] = jnp.zeros_like(s_s)
    qpart_ref[...] = jnp.zeros_like(qpart_ref)
    gain = qg_ref[...]

    def slot_t(s, _):
        kt[s] = kv_ref[pl.ds(pl.multiple_of(s * BLK, BLK), BLK), 0:BLK].T
        return 0

    lax.fori_loop(0, SLOTS, slot_t, 0)

    def facts(i):
        b = first + i
        start = jnp.int32(PROMPT)
        off = jnp.int32(0)
        live = jnp.int32(BLK)
        for r in range(8):
            n = len_ref[r]
            c = (n + BLK - 1) // BLK
            inside = (b >= start) & (b < start + c)
            off = jnp.where(inside, b - start, off)
            live = jnp.where(inside, jnp.minimum(n - (b - start) * BLK, BLK), live)
            start = start + c
        return b, off, live

    def prep(i, _):
        b, off, live = facts(i)
        src = jnp.int32(0)
        for j in range(4):
            src = jnp.where(from_ref[j] == b, j, src)
        rows = pl.ds(pl.multiple_of(i * BLK, BLK), BLK)
        srow = pl.ds(pl.multiple_of(src * BLK, BLK), BLK)
        alive = (lax.broadcasted_iota(jnp.int32, (BLK, BLK), 0) < live).astype(F32)
        for h in range(HEADS):
            cols = pl.ds(h * BLK, BLK)
            x = q_ref[rows, cols].astype(F32)
            r = lax.rsqrt(jnp.mean(x * x, axis=-1, keepdims=True) + 1e-6)
            y = (x * r * gain).astype(BF)
            z = (do_ref[srow, cols].astype(F32) * alive).astype(BF)
            t = i * TPB + h // HT
            e = pl.ds((h % HT) * BLK, BLK)
            qn[t, e, :] = y
            qt[t, :, e] = y.T
            dn[t, e, :] = z
            dt[t, :, e] = z.T
        return 0

    lax.fori_loop(0, 4, prep, 0)

    def per_block(i, _):
        b, off, live = facts(i)
        n_prompt = jnp.minimum(b, PROMPT)
        n_prev = jnp.clip(b - PROMPT, 0, REACH)
        pc = (n_prompt + CBP - 1) // CBP
        lc = (REACH - n_prev) // CBL
        keyi = lax.broadcasted_iota(jnp.int32, (BLK, RT), 0)
        toki = lax.rem(lax.broadcasted_iota(jnp.int32, (BLK, RT), 1), BLK)
        bias = jnp.where((keyi <= toki) & (keyi < live), 0.0, LOW)

        def seen(pos):
            return jnp.where(pos < PROMPT, pos < n_prompt, pos - PROMPT >= REACH - off)

        def per_tile(g, _):
            t = i * TPB + g

            def row0(pos):
                return pl.multiple_of(jnp.where(pos < PROMPT, pos, pos + i) * BLK, BLK)

            def first_pass(pos, nb, diag):
                r0 = row0(pos)
                kc = kv_ref[pl.ds(r0, nb * BLK), 0:BLK]
                for x in range(0, RT, CS):
                    cs = slice(x, x + CS)
                    s = nn(kc, qt[t, :, cs])
                    for u in range(nb):
                        su = s[u * BLK:(u + 1) * BLK]
                        if diag:
                            su = su + bias[:, cs]
                        su = su.reshape(BLK // 8, 8, CS)
                        m = jnp.max(su, axis=0) * SL2
                        w = jnp.exp2(su * SL2 - m[None])
                        s_s[pos + u, :, cs] = jnp.sum(w, axis=0)
                        if diag:
                            m_s[pos + u, :, cs] = m
                        else:
                            m_s[pos + u, :, cs] = jnp.where(seen(pos + u), m, LOW)
                        w_s[pos + u, :, cs] = w.reshape(BLK, CS)

            def over(body, init):
                init = lax.fori_loop(0, pc, lambda c, x: body(c * CBP, CBP, False, x), init)
                init = lax.fori_loop(lc, REACH // CBL, lambda c, x: body(PROMPT + c * CBL, CBL, False, x), init)
                return body(POS - 1, 1, True, init)

            def p1(pos, nb, diag, x):
                first_pass(pos, nb, diag)
                return x

            over(p1, 0)
            m = m_s[...]
            top = jnp.max(jnp.max(m, axis=0), axis=0, keepdims=True)
            f = jnp.exp2(m - top[None])
            tot = jnp.sum(jnp.sum(f * s_s[...], axis=0), axis=0, keepdims=True)
            f_s[...] = f * (1.0 / tot)[None]

            drows = dn[t]
            def p3(pos, nb, diag, acc):
                r0 = row0(pos)
                vc = kv_ref[pl.ds(r0, nb * BLK), BLK:2 * BLK]
                accs, ps = [], []
                for x in range(0, RT, CS):
                    cs = slice(x, x + CS)
                    dp = nn(vc, dt[t, :, cs])
                    a = acc[:, cs]
                    pu = []
                    for u in range(nb):
                        du = dp[u * BLK:(u + 1) * BLK]
                        ch = (w_s[pos + u, :, cs].reshape(BLK // 8, 8, CS) * f_s[pos + u, :, cs][None]).reshape(BLK, CS)
                        chb = ch.astype(BF)
                        w_s[pos + u, :, cs] = ch
                        dp_s[pos + u, :, cs] = du
                        a = a + jnp.sum((chb.astype(F32) * du).reshape(BLK // 8, 8, CS), axis=0)
                        pu.append(chb)
                    accs.append(a)
                    ps.append(jnp.concatenate(pu, axis=0))
                p = jnp.concatenate(ps, axis=1)
                rows = pl.ds(r0, nb * BLK)
                dv_ref[rows, :] += nn(p, drows)
                return jnp.concatenate(accs, axis=1)

            delta = over(p3, jnp.zeros((8, RT), F32))
            delta = jnp.sum(delta, axis=0, keepdims=True)
            qrows = qn[t]

            def p4(pos, nb, diag, dq):
                r0 = row0(pos)
                dss = []
                for u in range(nb):
                    ch = w_s[pos + u]
                    dss.append((ch * (dp_s[pos + u] - delta)).astype(BF))
                ds = jnp.concatenate(dss, axis=0) if nb > 1 else dss[0]
                rows = pl.ds(r0, nb * BLK)
                dk_ref[rows, :] += nn(ds, qrows)
                slot = r0 // BLK
                ktc = jnp.concatenate([kt[slot + u] for u in range(nb)], axis=1) if nb > 1 else kt[slot]
                dq_s[...] += nn(ktc, ds)
                return 0

            dq_s[...] = jnp.zeros_like(dq_s)
            over(p4, 0)
            dqt = dq_s[...]
            dq = dqt.T * SCALE
            rows = pl.ds(pl.multiple_of(i * BLK, BLK), BLK)
            part = jnp.zeros((8, BLK), F32)
            for u in range(HT):
                cols = pl.ds(pl.multiple_of((g * HT + u) * BLK, BLK), BLK)
                x = q_ref[rows, cols].astype(F32)
                r = lax.rsqrt(jnp.mean(x * x, axis=-1, keepdims=True) + 1e-6)
                unit = x * r
                dqu = dq[u * BLK:(u + 1) * BLK]
                both = dqu * unit
                part = part + jnp.sum(both.reshape(BLK // 8, 8, BLK), axis=0)
                mean = jnp.mean(both * gain, axis=-1, keepdims=True)
                gq_ref[rows, cols] = (r * (dqu * gain - unit * mean)).astype(BF)
            qpart_ref[...] += part
            return 0

        lax.fori_loop(0, TPB, per_tile, 0)
        return 0

    lax.fori_loop(0, 4, per_block, 0)

    def hand_over(s, _):
        rows = pl.ds(pl.multiple_of(s * BLK, BLK), BLK)
        away_ref[rows, 0:BLK] = dk_ref[rows, :].astype(BF)
        away_ref[rows, BLK:2 * BLK] = dv_ref[rows, :].astype(BF)
        return 0

    lax.fori_loop(0, OWN, hand_over, 0)
    mine_ref[:, 0:BLK] = dk_ref[OWN * BLK:, :]
    mine_ref[:, BLK:2 * BLK] = dv_ref[OWN * BLK:, :]


VM = pl.BlockSpec(memory_space=pltpu.VMEM)
SM = pl.BlockSpec(memory_space=pltpu.SMEM)


def attend(dev, lens, frm, qg, q, do, kv):
    rows = SLOTS * BLK
    return pl.pallas_call(
        attend_kernel,
        out_shape=(
            jax.ShapeDtypeStruct((512, 1024), BF),
            jax.ShapeDtypeStruct((OWN * BLK, 2 * BLK), BF),
            jax.ShapeDtypeStruct((4 * BLK, 2 * BLK), F32),
            jax.ShapeDtypeStruct((8, BLK), F32),
        ),
        in_specs=[SM, SM, SM, VM, VM, VM, VM],
        out_specs=(VM, VM, VM, VM),
        scratch_shapes=[
            pltpu.VMEM((4096 // RT, RT, BLK), BF),
            pltpu.VMEM((4096 // RT, BLK, RT), BF),
            pltpu.VMEM((4096 // RT, RT, BLK), BF),
            pltpu.VMEM((4096 // RT, BLK, RT), BF),
            pltpu.VMEM((SLOTS, BLK, BLK), BF),
            pltpu.VMEM((POS, BLK, RT), F32),
            pltpu.VMEM((POS, BLK, RT), F32),
            pltpu.VMEM((POS, 8, RT), F32),
            pltpu.VMEM((POS, 8, RT), F32),
            pltpu.VMEM((POS, 8, RT), F32),
            pltpu.VMEM((BLK, RT), F32),
            pltpu.VMEM((rows, BLK), F32),
            pltpu.VMEM((rows, BLK), F32),
        ],
        compiler_params=pltpu.CompilerParams(vmem_limit_bytes=60 * 1024 * 1024),
    )(dev, lens, frm, qg, q, do, kv)


MESH = pl.DeviceIdType.MESH
GRP = 512


def copy_to(src, dst, send, recv, dp, ctx):
    return pltpu.make_async_remote_copy(
        src_ref=src, dst_ref=dst, send_sem=send, recv_sem=recv,
        device_id=(dp, ctx), device_id_type=MESH)


def greet(dp, me, others):
    barrier = pltpu.get_barrier_semaphore()
    for ctx_off in range(1, 16):
        pl.semaphore_signal(barrier, inc=1, device_id=(dp, lax.rem(me + ctx_off, 16)), device_id_type=MESH)
    for dp_off in range(1, 8 if others else 1):
        pl.semaphore_signal(barrier, inc=1, device_id=(lax.rem(dp + dp_off, 8), me), device_id_type=MESH)
    pl.semaphore_wait(barrier, 22 if others else 15)


def spread_kernel(kg_ref, k_ref, v_ref, kv_ref, send_p, recv_p, send_l, recv_l):
    dp = lax.axis_index("dp")
    me = lax.axis_index("ctx")
    kv_ref[PROMPT * BLK:OWN * BLK, :] = jnp.zeros((REACH * BLK, 2 * BLK), BF)
    x = k_ref[...].astype(F32)
    r = lax.rsqrt(jnp.mean(x * x, axis=-1, keepdims=True) + 1e-6)
    mine = kv_ref.at[pl.ds(OWN * BLK, GRP)]
    kv_ref[OWN * BLK:, 0:BLK] = (x * r * kg_ref[...]).astype(BF)
    kv_ref[OWN * BLK:, BLK:2 * BLK] = v_ref[...]
    greet(dp, me, False)

    def slot(g):
        return kv_ref.at[pl.ds(pl.multiple_of(g * GRP, GRP), GRP)]

    def to_all(o):
        return copy_to(mine, slot(me), send_p.at[o], recv_p.at[me], dp, lax.rem(me + o, 16))

    locals_ = []
    for k in (1, 2, 3):
        n = 4 if k < 3 else 2
        src = kv_ref.at[pl.ds((OWN + 4 - n) * BLK, n * BLK)]
        dst = kv_ref.at[pl.ds((OWN + 4 - 4 * k - n) * BLK, n * BLK)]
        locals_.append(copy_to(src, dst, send_l.at[k - 1], recv_l.at[k - 1], dp, lax.rem(me + k, 16)))

    @pl.when(me < 4)
    def _():
        for o in range(15, 0, -1):
            to_all(o).start()
        kv_ref[pl.ds(pl.multiple_of(me * GRP, GRP), GRP), :] = kv_ref[OWN * BLK:, :]

    for k in (1, 2, 3):
        @pl.when((me >= 4) & (me + k < 16))
        def _(k=k):
            locals_[k - 1].start()
    for k in (1, 2, 3):
        @pl.when(me - k >= 4)
        def _(k=k):
            locals_[k - 1].wait_recv()
    for g in range(4):
        @pl.when(me != g)
        def _(g=g):
            copy_to(mine, slot(g), send_p.at[0], recv_p.at[g], dp, lax.rem(me + 1, 16)).wait_recv()
    for k in (1, 2, 3):
        @pl.when((me >= 4) & (me + k < 16))
        def _(k=k):
            locals_[k - 1].wait_send()

    @pl.when(me < 4)
    def _():
        for o in range(1, 16):
            to_all(o).wait_send()


def spread(kg, k, v):
    return pl.pallas_call(
        spread_kernel,
        out_shape=jax.ShapeDtypeStruct((SLOTS * BLK, 2 * BLK), BF),
        in_specs=[VM, VM, VM],
        out_specs=VM,
        scratch_shapes=[pltpu.SemaphoreType.DMA((16,)), pltpu.SemaphoreType.DMA((4,)),
                        pltpu.SemaphoreType.DMA((3,)), pltpu.SemaphoreType.DMA((3,))],
        compiler_params=pltpu.CompilerParams(collective_id=0, has_side_effects=True),
    )(kg, k, v)


def collect_kernel(kg_ref, k_ref, away_ref, mine_ref, qpart_ref, gk_ref, gv_ref, gain_ref,
                   bufa, bufb, bufc, bufl, sa, sb, tot, gown, gall, gdp,
                   send_a, recv_a, send_b, recv_b, send_c, recv_c, send_l, recv_l, send_g, recv_g):
    dp = lax.axis_index("dp")
    me = lax.axis_index("ctx")
    z = me // 4
    y = lax.rem(me // 2, 2)
    c = lax.rem(me, 2)
    greet(dp, me, True)
    sib = me + 1 - 2 * c
    yny = me + 2 - 4 * y

    def group(ref, g):
        return ref.at[pl.ds(pl.multiple_of(g * GRP, GRP), GRP)]

    ca = [copy_to(group(away_ref, 2 * j + 1 - c), bufa.at[j], send_a.at[j], recv_a.at[j], dp, sib) for j in range(2)]
    for x in ca:
        x.start()
    lo = []
    for k in (1, 2, 3):
        n = 4 if k < 3 else 2
        src = away_ref.at[pl.ds((OWN + 4 - 4 * k - n) * BLK, n * BLK)]
        lo.append(copy_to(src, bufl.at[k - 1, pl.ds(0, n * BLK)], send_l.at[k - 1], recv_l.at[k - 1], dp, lax.rem(me + 16 - k, 16)))
        @pl.when(me - k >= 4)
        def _(k=k):
            lo[k - 1].start()
    for x in ca:
        x.wait_recv()
    far = group(away_ref, 2 * (1 - y) + c)
    near = group(away_ref, 2 * y + c)
    sa[...] = (far[...].astype(F32) + bufa[1 - y].astype(F32)).astype(BF)
    cb = copy_to(sa, bufb, send_b, recv_b, dp, yny)
    cb.start()
    tot[...] = near[...].astype(F32) + bufa[y].astype(F32)
    cb.wait_recv()
    tot[...] += bufb[...].astype(F32)

    def zto(zz):
        return zz * 4 + 2 * y + c

    def half(h):
        return pl.ds(h * 256, 256)

    def leg(h, target):
        return copy_to(sb.at[half(h)], bufc.at[h], send_c.at[h], recv_c.at[h], dp, zto(target))

    for h, (src, mid, last) in ((0, (3, 2, 1)), (1, (1, 2, 3))):
        @pl.when(z == src)
        def _(h=h, src=src):
            sb[half(h), :] = tot[half(h), :].astype(BF)
            leg(h, 2).start()
    for h, (src, mid, last) in ((0, (3, 2, 1)), (1, (1, 2, 3))):
        for stage, nxt in ((mid, last), (last, 0)):
            @pl.when(z == stage)
            def _(h=h, nxt=nxt):
                leg(h, nxt).wait_recv()
                sb[half(h), :] = (tot[half(h), :] + bufc[h].astype(F32)).astype(BF)
                leg(h, nxt).start()

    @pl.when(z == 0)
    def _():
        for h in (0, 1):
            leg(h, 0).wait_recv()
            tot[half(h), :] += bufc[h].astype(F32)

    @pl.when(z != 0)
    def _():
        tot[...] = mine_ref[...]
        for h in (0, 1):
            leg(h, 0).wait_send()
    @pl.when(z == 0)
    def _():
        tot[...] += mine_ref[...]

    for k in (1, 2, 3):
        @pl.when((me >= 4) & (me + k < 16))
        def _(k=k):
            n = 4 if k < 3 else 2
            lo[k - 1].wait_recv()
            tot[(4 - n) * BLK:, :] += bufl[k - 1, 0:n * BLK].astype(F32)

    x = k_ref[...].astype(F32)
    r = lax.rsqrt(jnp.mean(x * x, axis=-1, keepdims=True) + 1e-6)
    unit = x * r
    dk = tot[:, 0:BLK] * SCALE
    both = dk * unit
    gown[...] = jnp.zeros_like(gown)
    gown[0:1, :] = jnp.sum(qpart_ref[...], axis=0, keepdims=True)
    gown[1:2, :] = jnp.sum(both, axis=0, keepdims=True)
    cg = [copy_to(gown, gall.at[me], send_g.at[o - 1], recv_g.at[me], dp, lax.rem(me + o, 16)) for o in range(1, 16)]
    for q in cg:
        q.start()
    gall[me] = gown[...]
    gain = kg_ref[...]
    mean = jnp.mean(both * gain, axis=-1, keepdims=True)
    gk_ref[...] = (r * (dk * gain - unit * mean)).astype(BF)
    gv_ref[...] = tot[:, BLK:2 * BLK].astype(BF)
    for o in range(1, 16):
        p = lax.rem(me + o, 16)
        copy_to(gown, gall.at[p], send_g.at[o - 1], recv_g.at[p], dp, p).wait_recv()
    total = gall[0]
    for o in range(1, 16):
        total = total + gall[o]
    for q in cg:
        q.wait_send()
    gown[...] = total
    ch = [copy_to(gown, gdp.at[dp], send_g.at[14 + o], recv_g.at[16 + dp], lax.rem(dp + o, 8), me) for o in range(1, 8)]
    for q in ch:
        q.start()
    gdp[dp] = total
    for o in range(1, 8):
        p = lax.rem(dp + o, 8)
        copy_to(gown, gdp.at[p], send_g.at[14 + o], recv_g.at[16 + p], p, me).wait_recv()
    total = gdp[0]
    for o in range(1, 8):
        total = total + gdp[o]
    gain_ref[...] = total
    for q in ch:
        q.wait_send()
    for q in ca:
        q.wait_send()
    cb.wait_send()
    for k in (1, 2, 3):
        @pl.when(me - k >= 4)
        def _(k=k):
            lo[k - 1].wait_send()


def collect(kg, k, away, mine, qpart):
    dma = pltpu.SemaphoreType.DMA
    return pl.pallas_call(
        collect_kernel,
        out_shape=(
            jax.ShapeDtypeStruct((GRP, BLK), BF),
            jax.ShapeDtypeStruct((GRP, BLK), BF),
            jax.ShapeDtypeStruct((8, BLK), F32),
        ),
        in_specs=[VM] * 5,
        out_specs=(VM, VM, VM),
        scratch_shapes=[
            pltpu.VMEM((2, GRP, 2 * BLK), BF),
            pltpu.VMEM((GRP, 2 * BLK), BF),
            pltpu.VMEM((2, 256, 2 * BLK), BF),
            pltpu.VMEM((3, GRP, 2 * BLK), BF),
            pltpu.VMEM((GRP, 2 * BLK), BF),
            pltpu.VMEM((GRP, 2 * BLK), BF),
            pltpu.VMEM((GRP, 2 * BLK), F32),
            pltpu.VMEM((8, BLK), F32),
            pltpu.VMEM((16, 8, BLK), F32),
            pltpu.VMEM((8, 8, BLK), F32),
            dma((2,)), dma((2,)), dma, dma, dma((2,)), dma((2,)),
            dma((3,)), dma((3,)), dma((22,)), dma((24,)),
        ],
        compiler_params=pltpu.CompilerParams(collective_id=1, has_side_effects=True, vmem_limit_bytes=32 * 1024 * 1024),
    )(kg, k, away, mine, qpart)


def body(q_raw, k_raw, values, d_out, q_gain, k_gain, resp_len, block_parent, block_from):
    dev = lax.axis_index("ctx").astype(jnp.int32).reshape(1)
    kg = k_gain.reshape(1, BLK)
    kv = spread(kg, k_raw[0], values[0])
    gq, away, mine, qpart = attend(dev, resp_len[0], block_from[0], q_gain.reshape(1, BLK), q_raw[0], d_out[0], kv)
    gk, gv, gains = collect(kg, k_raw[0], away, mine, qpart)
    return gq[None], gk[None], gv[None], gains[0], gains[1]


def solution(mesh):
    tok = P("dp", "ctx", None)
    return jax.shard_map(
        body,
        mesh=mesh,
        in_specs=(tok, tok, tok, tok, P(), P(), P("dp", None), P("dp", None), P("dp", "ctx")),
        out_specs=(tok, tok, tok, P(), P()),
        check_vma=False,
    )
```

```python
import functools, math
import jax, jax.numpy as jnp
from jax import lax
from jax.experimental import pallas as pl
from jax.experimental.pallas import tpu as pltpu
from jax.sharding import PartitionSpec as P

BLK = 128
HEADS = 8
PROMPT = 16
REACH = 10
SLOTS = 30
OWN = PROMPT + REACH
POS = 27
RT = 1024
CBP = 8
CBL = 10
HT = RT // BLK
CS = 256
TPB = HEADS // HT
LOW = -1e30
F32 = jnp.float32
BF = jnp.bfloat16
SCALE = 1.0 / math.sqrt(128.0)
LOG2E = 1.4426950408889634
SL2 = SCALE * LOG2E
VM = pl.BlockSpec(memory_space=pltpu.VMEM)
SM = pl.BlockSpec(memory_space=pltpu.SMEM)


def nt(a, b):
    return lax.dot_general(a, b, (((1,), (1,)), ((), ())), preferred_element_type=F32)


def nn(a, b):
    return jnp.dot(a, b, preferred_element_type=F32)


MESH = pl.DeviceIdType.MESH
GRP = 512


def copy_to(src, dst, send, recv, dp, ctx):
    return pltpu.make_async_remote_copy(
        src_ref=src, dst_ref=dst, send_sem=send, recv_sem=recv,
        device_id=(dp, ctx), device_id_type=MESH)


def greet(dp, me, wide):
    barrier = pltpu.get_barrier_semaphore()
    c = lax.rem(me, 2)
    y = lax.rem(me // 2, 2)
    if wide:
        targets = [(dp, lax.rem(me + o, 16)) for o in range(1, 16)]
        targets += [(lax.rem(dp + o, 8), me) for o in range(1, 8)]
    else:
        targets = [(dp, me + 1 - 2 * c), (dp, me + 2 - 4 * y)]
        targets += [(dp, lax.rem(me + o, 16)) for o in (4, 12, 2, 14, 3, 13)]
    for t in targets:
        pl.semaphore_signal(barrier, inc=1, device_id=t, device_id_type=MESH)
    pl.semaphore_wait(barrier, len(targets))


def fused_kernel(len_ref, from_ref, qg_ref, kg_ref, q_ref, do_ref, k_ref, v_ref,
                 gq_ref, gk_ref, gv_ref, gain_ref,
                 kv_ref, qn, qt, dn, dt, kt, w_s, dp_s, m_s, s_s, f_s, dq_s, dk_ref, dv_ref, qpart,
                 away, bufa, bufb, bufc, bufl, bufs, sa, sb, sl, tot, gown, gall, gdp,
                 send_z, recv_z, send_y, recv_y, send_s, recv_s, fsend_l, frecv_l,
                 send_a, recv_a, send_b, recv_b, send_c, recv_c, send_l, recv_l, send_g, recv_g):
    dp = lax.axis_index("dp")
    me = lax.axis_index("ctx")
    z = me // 4
    y = lax.rem(me // 2, 2)
    c = lax.rem(me, 2)
    n = me // 2
    first = me * 4
    sib = me + 1 - 2 * c
    yny = me + 2 - 4 * y
    kv_ref[PROMPT * BLK:OWN * BLK, :] = jnp.zeros((REACH * BLK, 2 * BLK), BF)
    x = k_ref[...].astype(F32)
    r = lax.rsqrt(jnp.mean(x * x, axis=-1, keepdims=True) + 1e-6)
    kv_ref[OWN * BLK:, 0:BLK] = (x * r * kg_ref[...]).astype(BF)
    kv_ref[OWN * BLK:, BLK:2 * BLK] = v_ref[...]

    @pl.when(z == 0)
    def _():
        kv_ref[pl.ds(pl.multiple_of(me * GRP, GRP), GRP), :] = kv_ref[OWN * BLK:, :]

    greet(dp, me, True)
    chain = 2 * y + c
    other = 2 * (1 - y) + c

    def krows(g, h):
        return kv_ref.at[pl.ds(pl.multiple_of(g * GRP + h * 256, 256), 256)]

    def kblocks(first, count):
        return kv_ref.at[pl.ds(first * BLK, count * BLK)]

    def kv_z(h, zz, k):
        return copy_to(krows(chain, h), krows(chain, h), send_z.at[k], recv_z.at[h], dp, zz * 4 + chain)

    def kv_y(h):
        return copy_to(krows(chain, h), krows(chain, h), send_y.at[h], recv_y.at[h], dp, yny)

    def kv_s(j, h):
        g = chain if j == 0 else other
        return copy_to(krows(g, h), krows(g, h), send_s.at[2 * j + h], recv_s.at[2 * j + h], dp, sib)

    has_next = (n >= 2) & (n + 1 <= 7)
    has_prev = n >= 3
    ahead = copy_to(kblocks(OWN, 4),kblocks(PROMPT + 2, 4), fsend_l.at[0], frecv_l.at[0], dp, lax.rem(me + 2, 16))
    own_sib = copy_to(kblocks(OWN, 4),kblocks(PROMPT + 6, 4), fsend_l.at[1], frecv_l.at[1], dp, sib)
    kfar = copy_to(kblocks(OWN + 2, 2),kblocks(PROMPT, 2), fsend_l.at[2], frecv_l.at[2], dp, lax.rem(me + 3, 16))
    relay_full = copy_to(kblocks(PROMPT + 2, 4),kblocks(PROMPT + 6, 4), fsend_l.at[3], frecv_l.at[1], dp, sib)
    relay_half = copy_to(kblocks(PROMPT + 4, 2),kblocks(PROMPT, 2), fsend_l.at[4], frecv_l.at[2], dp, sib)
    sends_kfar = (c == 1) & (n >= 2) & (n + 2 <= 7)
    gets_kfar = (c == 0) & (n >= 4)

    @pl.when(z == 0)
    def _():
        kv_z(0, 1, 0).start()
        kv_z(1, 3, 1).start()
        kv_z(1, 1, 2).start()
        kv_z(0, 3, 3).start()
        for h in (0, 1):
            kv_y(h).start()
            kv_s(0, h).start()

    @pl.when((c == 0) & (n >= 2))
    def _():
        own_sib.start()

    @pl.when(has_next)
    def _():
        ahead.start()

    @pl.when(sends_kfar)
    def _():
        kfar.start()

    early = jnp.where(z == 1, 1, 0)
    order = (early, 1 - early)

    def half(h):
        return pl.ds(pl.multiple_of(h * 256, 256), 256)

    def rows(g, h):
        return pl.ds(pl.multiple_of(g * GRP + h * 256, 256), 256)

    def blocks(first, count):
        return pl.ds(first * BLK, count * BLK)

    def cp_a(j, h):
        return copy_to(away.at[rows(2 * j + 1 - c, h)], bufa.at[j, half(h)],
                       send_a.at[2 * j + h], recv_a.at[2 * j + h], dp, sib)

    def cp_b(h):
        return copy_to(sa.at[half(h)], bufb.at[half(h)], send_b.at[h], recv_b.at[h], dp, yny)

    def cp_c(h, slot, zz):
        return copy_to(sb.at[half(h)], bufc.at[slot, half(h)], send_c.at[h], recv_c.at[2 * slot + h],
                       dp, zz * 4 + 2 * y + c)

    has_prev = n >= 3
    from_next = (n >= 2) & (n + 1 <= 7)
    hand_full = copy_to(away.at[blocks(PROMPT + 6, 4)], bufs, send_l.at[0], recv_l.at[0], dp, sib)
    hand_half = copy_to(away.at[blocks(PROMPT, 2)], bufs.at[pl.ds(0, 2 * BLK)], send_l.at[1], recv_l.at[0], dp, sib)
    back = copy_to(sl, bufl.at[0], send_l.at[2], recv_l.at[1], dp, lax.rem(me + 14, 16))
    near_back = copy_to(away.at[blocks(PROMPT + 6, 4)], bufl.at[1], send_l.at[3], recv_l.at[2], dp, sib)
    far_back = copy_to(away.at[blocks(PROMPT, 2)], bufl.at[2, pl.ds(0, 2 * BLK)], send_l.at[4], recv_l.at[3],
                       dp, lax.rem(me + 13, 16))
    sends_near = (c == 1) & (n >= 2)
    gets_near = (c == 0) & (n >= 2)
    sends_far = (c == 0) & (n >= 4)
    gets_far = (c == 1) & (n >= 2) & (n + 2 <= 7)

    def hand_over(s, _):
        rr = pl.ds(pl.multiple_of(s * BLK, BLK), BLK)
        away[rr, 0:BLK] = dk_ref[rr, :].astype(BF)
        away[rr, BLK:2 * BLK] = dv_ref[rr, :].astype(BF)
        return 0

    def local_sends():
        @pl.when(has_prev & (c == 0))
        def _():
            hand_full.start()

        @pl.when(has_prev & (c == 1))
        def _():
            hand_half.start()

        @pl.when(sends_near)
        def _():
            near_back.start()

        @pl.when(sends_far)
        def _():
            far_back.start()

    dk_ref[...] = jnp.zeros_like(dk_ref)
    dv_ref[...] = jnp.zeros_like(dv_ref)
    m_s[...] = jnp.full_like(m_s, LOW)
    s_s[...] = jnp.zeros_like(s_s)
    qpart[...] = jnp.zeros_like(qpart)
    gain = qg_ref[...]

    def facts(i):
        b = first + i
        start = jnp.int32(PROMPT)
        off = jnp.int32(0)
        live = jnp.int32(BLK)
        for r in range(8):
            n = len_ref[r]
            c = (n + BLK - 1) // BLK
            inside = (b >= start) & (b < start + c)
            off = jnp.where(inside, b - start, off)
            live = jnp.where(inside, jnp.minimum(n - (b - start) * BLK, BLK), live)
            start = start + c
        return b, off, live

    def prep(i, _):
        b, off, live = facts(i)
        src = jnp.int32(0)
        for j in range(4):
            src = jnp.where(from_ref[j] == b, j, src)
        rows = pl.ds(pl.multiple_of(i * BLK, BLK), BLK)
        srcv = jnp.full((BLK, BLK), src, jnp.int32)
        alive = (lax.broadcasted_iota(jnp.int32, (BLK, BLK), 0) < live).astype(F32)
        for h in range(HEADS):
            cols = pl.ds(h * BLK, BLK)
            x = q_ref[rows, cols].astype(F32)
            r = lax.rsqrt(jnp.mean(x * x, axis=-1, keepdims=True) + 1e-6)
            y = (x * r * gain).astype(BF)
            z = do_ref[0:BLK, cols].astype(F32)
            for j in range(1, 4):
                z = jnp.where(srcv == j, do_ref[j * BLK:(j + 1) * BLK, cols].astype(F32), z)
            z = (z * alive).astype(BF)
            t = i * TPB + h // HT
            e = pl.ds((h % HT) * BLK, BLK)
            qn[t, e, :] = y
            qt[t, :, e] = y.T
            dn[t, e, :] = z
            dt[t, :, e] = z.T
        return 0

    lax.fori_loop(0, 2, prep, 0)
    def got(h):
        kv_z(h, 0, 0).wait_recv()
        kv_y(h).start()
        kv_s(0, h).start()

    @pl.when(z == 1)
    def _():
        kv_z(0, 2, 0).wait_recv()
        kv_z(0, 2, 0).start()
        kv_y(0).start()
        kv_s(0, 0).start()
        got(1)

    @pl.when(z == 3)
    def _():
        kv_z(1, 2, 0).wait_recv()
        kv_z(1, 2, 0).start()
        kv_y(1).start()
        kv_s(0, 1).start()
        got(0)

    @pl.when(z == 2)
    def _():
        got(0)
        got(1)

    lax.fori_loop(2, 4, prep, 0)
    @pl.when(has_prev)
    def _():
        ahead.wait_recv()

    @pl.when(has_prev & (c == 1))
    def _():
        relay_full.start()

    @pl.when(has_prev & (c == 0))
    def _():
        relay_half.start()

    def y_got(h):
        copy_to(krows(other, h), krows(other, h), send_y.at[h], recv_y.at[h], dp, yny).wait_recv()
        kv_s(1, h).start()

    @pl.when(z != 3)
    def _():
        y_got(0)
        y_got(1)

    @pl.when(z == 3)
    def _():
        y_got(1)
        y_got(0)

    for j in (0, 1):
        for h in (0, 1):
            g = (2 * y + 1 - c) if j == 0 else (2 * (1 - y) + 1 - c)
            copy_to(krows(g, h), krows(g, h), send_s.at[2 * j + h], recv_s.at[2 * j + h], dp, sib).wait_recv()

    @pl.when(((c == 1) & (n >= 2)) | ((c == 0) & has_prev))
    def _():
        own_sib.wait_recv()

    @pl.when(gets_kfar | ((c == 1) & has_prev))
    def _():
        kfar.wait_recv()

    def slot_t(s, _):
        kt[s] = kv_ref[pl.ds(pl.multiple_of(s * BLK, BLK), BLK), 0:BLK].T
        return 0

    lax.fori_loop(0, SLOTS, slot_t, 0)

    def per_block(i, _):
        b, off, live = facts(i)
        n_prompt = jnp.minimum(b, PROMPT)
        n_prev = jnp.clip(b - PROMPT, 0, REACH)
        pc = (n_prompt + CBP - 1) // CBP
        lc = (REACH - n_prev) // CBL
        keyi = lax.broadcasted_iota(jnp.int32, (BLK, RT), 0)
        toki = lax.rem(lax.broadcasted_iota(jnp.int32, (BLK, RT), 1), BLK)
        bias = jnp.where((keyi <= toki) & (keyi < live), 0.0, LOW)

        offv = jnp.full((8, CS), off, jnp.int32)

        def seen(pos):
            prompt = pos < PROMPT
            spare = jnp.where(prompt, n_prompt - 1 - pos, pos - PROMPT - REACH)
            return spare + offv * jnp.where(prompt, 0, 1) >= 0

        def per_tile(g, _):
            t = i * TPB + g

            def row0(pos):
                return pl.multiple_of(jnp.where(pos < PROMPT, pos, pos + i) * BLK, BLK)

            def first_pass(pos, nb, diag):
                r0 = row0(pos)
                kc = kv_ref[pl.ds(r0, nb * BLK), 0:BLK]
                for x in range(0, RT, CS):
                    cs = slice(x, x + CS)
                    s = nn(kc, qt[t, :, cs])
                    for u in range(nb):
                        su = s[u * BLK:(u + 1) * BLK]
                        if diag:
                            su = su + bias[:, cs]
                        su = su.reshape(BLK // 8, 8, CS)
                        m = jnp.max(su, axis=0) * SL2
                        w = jnp.exp2(su * SL2 - m[None])
                        s_s[pos + u, :, cs] = jnp.sum(w, axis=0)
                        if diag:
                            m_s[pos + u, :, cs] = m
                        else:
                            m_s[pos + u, :, cs] = jnp.where(seen(pos + u), m, LOW)
                        w_s[pos + u, :, cs] = w.reshape(BLK, CS)

            def over(body, init):
                init = lax.fori_loop(0, pc, lambda c, x: body(c * CBP, CBP, False, x), init)
                init = lax.fori_loop(lc, REACH // CBL, lambda c, x: body(PROMPT + c * CBL, CBL, False, x), init)
                return body(POS - 1, 1, True, init)

            def p1(pos, nb, diag, x):
                first_pass(pos, nb, diag)
                return x

            over(p1, 0)
            m = m_s[...]
            top = jnp.max(jnp.max(m, axis=0), axis=0, keepdims=True)
            f = jnp.exp2(m - top[None])
            tot = jnp.sum(jnp.sum(f * s_s[...], axis=0), axis=0, keepdims=True)
            f_s[...] = f * (1.0 / tot)[None]

            drows = dn[t]
            def p3(pos, nb, diag, acc):
                r0 = row0(pos)
                vc = kv_ref[pl.ds(r0, nb * BLK), BLK:2 * BLK]
                accs, ps = [], []
                for x in range(0, RT, CS):
                    cs = slice(x, x + CS)
                    dp = nn(vc, dt[t, :, cs])
                    a = acc[:, cs]
                    pu = []
                    for u in range(nb):
                        du = dp[u * BLK:(u + 1) * BLK]
                        ch = (w_s[pos + u, :, cs].reshape(BLK // 8, 8, CS) * f_s[pos + u, :, cs][None]).reshape(BLK, CS)
                        chb = ch.astype(BF)
                        w_s[pos + u, :, cs] = ch
                        dp_s[pos + u, :, cs] = du
                        a = a + jnp.sum((chb.astype(F32) * du).reshape(BLK // 8, 8, CS), axis=0)
                        pu.append(chb)
                    accs.append(a)
                    ps.append(jnp.concatenate(pu, axis=0))
                p = jnp.concatenate(ps, axis=1)
                rows = pl.ds(r0, nb * BLK)
                dv_ref[rows, :] += nn(p, drows)
                return jnp.concatenate(accs, axis=1)

            delta = over(p3, jnp.zeros((8, RT), F32))
            delta = jnp.sum(delta, axis=0, keepdims=True)
            qrows = qn[t]

            def p4(pos, nb, diag, dq):
                r0 = row0(pos)
                dss = []
                for u in range(nb):
                    ch = w_s[pos + u]
                    dss.append((ch * (dp_s[pos + u] - delta)).astype(BF))
                ds = jnp.concatenate(dss, axis=0) if nb > 1 else dss[0]
                rows = pl.ds(r0, nb * BLK)
                dk_ref[rows, :] += nn(ds, qrows)
                slot = r0 // BLK
                ktc = jnp.concatenate([kt[slot + u] for u in range(nb)], axis=1) if nb > 1 else kt[slot]
                dq_s[...] += nn(ktc, ds)
                return 0

            dq_s[...] = jnp.zeros_like(dq_s)
            p4(POS - 1, 1, True, 0)
            lax.fori_loop(lc, REACH // CBL, lambda c, x: p4(PROMPT + c * CBL, CBL, False, x), 0)

            @pl.when(i == 3)
            def _():
                lax.fori_loop(PROMPT, OWN, hand_over, 0)
                local_sends()

            def p4_prompt(j, _):
                @pl.when(j < pc)
                def _():
                    p4(j * CBP, CBP, False, 0)

                @pl.when(i == 3)
                def _():
                    lax.fori_loop(8 * j, 8 * j + 8, hand_over, 0)
                    for h in order:
                        cp_a(j, h).start()

                return 0

            lax.fori_loop(0, 2, p4_prompt, 0)
            dqt = dq_s[...]
            dq = dqt.T * SCALE
            rows = pl.ds(pl.multiple_of(i * BLK, BLK), BLK)
            part = jnp.zeros((8, BLK), F32)
            for u in range(HT):
                cols = pl.ds(pl.multiple_of((g * HT + u) * BLK, BLK), BLK)
                x = q_ref[rows, cols].astype(F32)
                r = lax.rsqrt(jnp.mean(x * x, axis=-1, keepdims=True) + 1e-6)
                unit = x * r
                dqu = dq[u * BLK:(u + 1) * BLK]
                both = dqu * unit
                part = part + jnp.sum(both.reshape(BLK // 8, 8, BLK), axis=0)
                mean = jnp.mean(both * gain, axis=-1, keepdims=True)
                gq_ref[rows, cols] = (r * (dqu * gain - unit * mean)).astype(BF)
            qpart[...] += part
            return 0

        lax.fori_loop(0, TPB, per_tile, 0)
        return 0

    lax.fori_loop(0, 4, per_block, 0)

    @pl.when(has_prev & (c == 1))
    def _():
        hand_full.wait_recv()
        sl[...] = (away[blocks(PROMPT + 2, 4), :].astype(F32) + bufs[...].astype(F32)).astype(BF)
        back.start()

    @pl.when(has_prev & (c == 0))
    def _():
        hand_half.wait_recv()
        sl[0:2 * BLK, :] = away[blocks(PROMPT + 2, 2), :]
        sl[2 * BLK:, :] = (away[blocks(PROMPT + 4, 2), :].astype(F32) + bufs[0:2 * BLK].astype(F32)).astype(BF)
        back.start()

    for h in order:
        cp_a(1 - y, h).wait_recv()
        sa[half(h), :] = (away[rows(2 * (1 - y) + c, h), :].astype(F32)
                          + bufa[1 - y, half(h), :].astype(F32)).astype(BF)
        cp_b(h).start()

    for step, h in enumerate(order):
        cp_a(y, h).wait_recv()
        tot[half(h), :] = away[rows(2 * y + c, h), :].astype(F32) + bufa[y, half(h), :].astype(F32)
        cp_b(h).wait_recv()
        tot[half(h), :] += bufb[half(h), :].astype(F32)

        @pl.when(z == 2)
        def _(h=h):
            sb[half(h), :] = tot[half(h), :].astype(BF)
            cp_c(h, 0, 1 + 2 * h).start()

        @pl.when((z == 1) | (z == 3))
        def _(h=h, step=step):
            if step == 1:
                cp_c(h, 0, 0).wait_recv()
                tot[half(h), :] += bufc[0, half(h), :].astype(F32)
            sb[half(h), :] = tot[half(h), :].astype(BF)
            cp_c(h, (z - 1) // 2, 0).start()

    @pl.when(z == 0)
    def _():
        for h in order:
            for slot in (0, 1):
                cp_c(h, slot, 1).wait_recv()
                tot[half(h), :] += bufc[slot, half(h), :].astype(F32)
        tot[:, 0:BLK] += dk_ref[OWN * BLK:, :]
        tot[:, BLK:2 * BLK] += dv_ref[OWN * BLK:, :]

    @pl.when(z != 0)
    def _():
        tot[:, 0:BLK] = dk_ref[OWN * BLK:, :]
        tot[:, BLK:2 * BLK] = dv_ref[OWN * BLK:, :]

    @pl.when(from_next)
    def _():
        back.wait_recv()
        tot[...] += bufl[0].astype(F32)

    @pl.when(gets_near)
    def _():
        near_back.wait_recv()
        tot[...] += bufl[1].astype(F32)

    @pl.when(gets_far)
    def _():
        far_back.wait_recv()
        tot[2 * BLK:, :] += bufl[2, 0:2 * BLK].astype(F32)

    x = k_ref[...].astype(F32)
    r = lax.rsqrt(jnp.mean(x * x, axis=-1, keepdims=True) + 1e-6)
    unit = x * r
    dk = tot[:, 0:BLK] * SCALE
    both = dk * unit
    gown[...] = jnp.zeros_like(gown)
    gown[0:1, :] = jnp.sum(qpart[...], axis=0, keepdims=True)
    gown[1:2, :] = jnp.sum(both, axis=0, keepdims=True)
    cg = [copy_to(gown, gall.at[me], send_g.at[o - 1], recv_g.at[me], dp, lax.rem(me + o, 16)) for o in range(1, 16)]
    for q in cg:
        q.start()
    gall[me] = gown[...]
    kgain = kg_ref[...]
    mean = jnp.mean(both * kgain, axis=-1, keepdims=True)
    gk_ref[...] = (r * (dk * kgain - unit * mean)).astype(BF)
    gv_ref[...] = tot[:, BLK:2 * BLK].astype(BF)
    for o in range(1, 16):
        p = lax.rem(me + o, 16)
        copy_to(gown, gall.at[p], send_g.at[o - 1], recv_g.at[p], dp, p).wait_recv()
    total = gall[0]
    for o in range(1, 16):
        total = total + gall[o]
    for q in cg:
        q.wait_send()
    gown[...] = total
    ch = [copy_to(gown, gdp.at[dp], send_g.at[14 + o], recv_g.at[16 + dp], lax.rem(dp + o, 8), me) for o in range(1, 8)]
    for q in ch:
        q.start()
    gdp[dp] = total
    for o in range(1, 8):
        p = lax.rem(dp + o, 8)
        copy_to(gown, gdp.at[p], send_g.at[14 + o], recv_g.at[16 + p], p, me).wait_recv()
    total = gdp[0]
    for o in range(1, 8):
        total = total + gdp[o]
    gain_ref[...] = total
    for q in ch:
        q.wait_send()
    for h in (0, 1):
        cp_a(0, h).wait_send()
        cp_a(1, h).wait_send()
        cp_b(h).wait_send()

    @pl.when(z != 0)
    def _():
        for h in (0, 1):
            cp_c(h, 0, 0).wait_send()

    @pl.when(has_prev & (c == 0))
    def _():
        hand_full.wait_send()

    @pl.when(has_prev & (c == 1))
    def _():
        hand_half.wait_send()

    @pl.when(has_prev)
    def _():
        back.wait_send()

    @pl.when(sends_near)
    def _():
        near_back.wait_send()

    @pl.when(sends_far)
    def _():
        far_back.wait_send()

    @pl.when(z == 0)
    def _():
        for k in range(4):
            kv_z(0, 1, k).wait_send()

    @pl.when((z == 1) | (z == 3))
    def _():
        kv_z(0, 1, 0).wait_send()

    for h in (0, 1):
        kv_y(h).wait_send()
        kv_s(0, h).wait_send()
        kv_s(1, h).wait_send()

    @pl.when((c == 0) & (n >= 2))
    def _():
        own_sib.wait_send()

    @pl.when(has_next)
    def _():
        ahead.wait_send()

    @pl.when(sends_kfar)
    def _():
        kfar.wait_send()

    @pl.when(has_prev & (c == 1))
    def _():
        relay_full.wait_send()

    @pl.when(has_prev & (c == 0))
    def _():
        relay_half.wait_send()


def fused(lens, frm, qg, kg, q, do, k, v):
    dma = pltpu.SemaphoreType.DMA
    rows = SLOTS * BLK
    tiles = 4096 // RT
    pair = pltpu.VMEM((GRP, 2 * BLK), BF)
    two = pltpu.VMEM((2, GRP, 2 * BLK), BF)
    return pl.pallas_call(
        fused_kernel,
        out_shape=(
            jax.ShapeDtypeStruct((512, 1024), BF),
            jax.ShapeDtypeStruct((GRP, BLK), BF),
            jax.ShapeDtypeStruct((GRP, BLK), BF),
            jax.ShapeDtypeStruct((8, BLK), F32),
        ),
        in_specs=[SM, SM, VM, VM, VM, VM, VM, VM],
        out_specs=(VM, VM, VM, VM),
        scratch_shapes=[
            pltpu.VMEM((rows, 2 * BLK), BF),
            pltpu.VMEM((tiles, RT, BLK), BF),
            pltpu.VMEM((tiles, BLK, RT), BF),
            pltpu.VMEM((tiles, RT, BLK), BF),
            pltpu.VMEM((tiles, BLK, RT), BF),
            pltpu.VMEM((SLOTS, BLK, BLK), BF),
            pltpu.VMEM((POS, BLK, RT), F32),
            pltpu.VMEM((POS, BLK, RT), F32),
            pltpu.VMEM((POS, 8, RT), F32),
            pltpu.VMEM((POS, 8, RT), F32),
            pltpu.VMEM((POS, 8, RT), F32),
            pltpu.VMEM((BLK, RT), F32),
            pltpu.VMEM((rows, BLK), F32),
            pltpu.VMEM((rows, BLK), F32),
            pltpu.VMEM((8, BLK), F32),
            pltpu.VMEM((OWN * BLK, 2 * BLK), BF),
            two, pair, two, pltpu.VMEM((3, GRP, 2 * BLK), BF), pair, pair, pair, pair,
            pltpu.VMEM((GRP, 2 * BLK), F32),
            pltpu.VMEM((8, BLK), F32),
            pltpu.VMEM((16, 8, BLK), F32),
            pltpu.VMEM((8, 8, BLK), F32),
        ] + [dma((m,)) for m in (4, 2, 2, 2, 4, 4, 5, 3, 4, 4, 2, 2, 2, 4, 5, 4, 22, 24)],
        compiler_params=pltpu.CompilerParams(
            collective_id=0, has_side_effects=True, vmem_limit_bytes=60 * 1024 * 1024),
    )(lens, frm, qg, kg, q, do, k, v)


PIECES = 4


def hand_out_kernel(gains_ref, gq_ref, gk_ref, gv_ref, oq_ref, ok_ref, ov_ref, gq_gain_ref, gk_gain_ref,
                    bq, bk, bv, sin, sout):
    step = bq.shape[0] // PIECES
    legs = [(gq_ref.at[pl.ds(j * step, step)], bq.at[pl.ds(j * step, step)], oq_ref.at[pl.ds(j * step, step)])
            for j in range(PIECES)]
    legs += [(gk_ref, bk, ok_ref), (gv_ref, bv, ov_ref)]
    into = [pltpu.make_async_copy(x, m, sin.at[j]) for j, (x, m, _) in enumerate(legs)]
    out = [pltpu.make_async_copy(m, o, sout.at[j]) for j, (_, m, o) in enumerate(legs)]
    for copy in into:
        copy.start()
    gq_gain_ref[...] = gains_ref[0, :]
    gk_gain_ref[...] = gains_ref[1, :]
    for j in range(len(legs)):
        into[j].wait()
        out[j].start()
    for copy in out:
        copy.wait()


def hand_out(gains, gq, gk, gv):
    anywhere = pl.BlockSpec(memory_space=pl.ANY)
    flat = jax.ShapeDtypeStruct((BLK,), F32)
    dma = pltpu.SemaphoreType.DMA
    return pl.pallas_call(
        hand_out_kernel,
        out_shape=tuple(jax.ShapeDtypeStruct(t.shape, t.dtype) for t in (gq, gk, gv)) + (flat, flat),
        in_specs=[VM, anywhere, anywhere, anywhere],
        out_specs=(anywhere, anywhere, anywhere, VM, VM),
        scratch_shapes=[pltpu.VMEM(t.shape, t.dtype) for t in (gq, gk, gv)] + [dma((PIECES + 2,)), dma((PIECES + 2,))],
    )(gains, gq, gk, gv)


def body(q_raw, k_raw, values, d_out, q_gain, k_gain, resp_len, block_parent, block_from):
    gq, gk, gv, gains = fused(resp_len[0], block_from[0], q_gain.reshape(1, BLK), k_gain.reshape(1, BLK),
                              q_raw[0], d_out[0], k_raw[0], values[0])
    gq, gk, gv, q_gain_grad, k_gain_grad = hand_out(gains, gq, gk, gv)
    return gq[None], gk[None], gv[None], q_gain_grad, k_gain_grad


def solution(mesh):
    tok = P("dp", "ctx", None)
    return jax.shard_map(
        body,
        mesh=mesh,
        in_specs=(tok, tok, tok, tok, P(), P(), P("dp", None), P("dp", None), P("dp", "ctx")),
        out_specs=(tok, tok, tok, P(), P()),
        check_vma=False,
    )
```

```python
import functools, math
import jax, jax.numpy as jnp
from jax import lax
from jax.experimental import pallas as pl
from jax.experimental.pallas import tpu as pltpu
from jax.sharding import PartitionSpec as P

BLK = 128
HEADS = 8
PROMPT = 16
REACH = 10
SLOTS = 30
OWN = PROMPT + REACH
POS = 27
RT = 1024
CBP = 8
CBL = 10
HT = RT // BLK
CS = 256
TPB = HEADS // HT
LOW = -1e30
F32 = jnp.float32
BF = jnp.bfloat16
SCALE = 1.0 / math.sqrt(128.0)
LOG2E = 1.4426950408889634
SL2 = SCALE * LOG2E
VM = pl.BlockSpec(memory_space=pltpu.VMEM)
SM = pl.BlockSpec(memory_space=pltpu.SMEM)


def nt(a, b):
    return lax.dot_general(a, b, (((1,), (1,)), ((), ())), preferred_element_type=F32)


def nn(a, b):
    return jnp.dot(a, b, preferred_element_type=F32)


MESH = pl.DeviceIdType.MESH
GRP = 512


def copy_to(src, dst, send, recv, dp, ctx):
    return pltpu.make_async_remote_copy(
        src_ref=src, dst_ref=dst, send_sem=send, recv_sem=recv,
        device_id=(dp, ctx), device_id_type=MESH)


def greet(dp, me, wide):
    barrier = pltpu.get_barrier_semaphore()
    c = lax.rem(me, 2)
    y = lax.rem(me // 2, 2)
    if wide:
        targets = [(dp, lax.rem(me + o, 16)) for o in range(1, 16)]
        targets += [(lax.rem(dp + o, 8), me) for o in range(1, 8)]
    else:
        targets = [(dp, me + 1 - 2 * c), (dp, me + 2 - 4 * y)]
        targets += [(dp, lax.rem(me + o, 16)) for o in (4, 12, 2, 14, 3, 13)]
    for t in targets:
        pl.semaphore_signal(barrier, inc=1, device_id=t, device_id_type=MESH)
    pl.semaphore_wait(barrier, len(targets))


def fused_kernel(len_ref, from_ref, qg_ref, kg_ref, q_ref, do_ref, k_ref, v_ref,
                 gq_ref, gk_ref, gv_ref, gain_ref,
                 kv_ref, qn, qt, dn, dt, kt, w_s, dp_s, m_s, s_s, f_s, dq_s, dk_ref, dv_ref, qpart,
                 away, bufa, bufb, bufc, bufl, bufs, sa, sb, sl, tot, gown, gsum, gall, gdp,
                 send_z, recv_z, send_y, recv_y, send_s, recv_s, fsend_l, frecv_l,
                 send_a, recv_a, send_b, recv_b, send_c, recv_c, send_l, recv_l, send_g, recv_g):
    dp = lax.axis_index("dp")
    me = lax.axis_index("ctx")
    z = me // 4
    y = lax.rem(me // 2, 2)
    c = lax.rem(me, 2)
    n = me // 2
    first = me * 4
    sib = me + 1 - 2 * c
    yny = me + 2 - 4 * y
    kv_ref[PROMPT * BLK:OWN * BLK, :] = jnp.zeros((REACH * BLK, 2 * BLK), BF)
    x = k_ref[...].astype(F32)
    r = lax.rsqrt(jnp.mean(x * x, axis=-1, keepdims=True) + 1e-6)
    kv_ref[OWN * BLK:, 0:BLK] = (x * r * kg_ref[...]).astype(BF)
    kv_ref[OWN * BLK:, BLK:2 * BLK] = v_ref[...]

    @pl.when(z == 0)
    def _():
        kv_ref[pl.ds(pl.multiple_of(me * GRP, GRP), GRP), :] = kv_ref[OWN * BLK:, :]

    greet(dp, me, True)
    chain = 2 * y + c
    other = 2 * (1 - y) + c

    def krows(g, h):
        return kv_ref.at[pl.ds(pl.multiple_of(g * GRP + h * 256, 256), 256)]

    def kblocks(first, count):
        return kv_ref.at[pl.ds(first * BLK, count * BLK)]

    def kv_z(h, zz, k):
        return copy_to(krows(chain, h), krows(chain, h), send_z.at[k], recv_z.at[h], dp, zz * 4 + chain)

    def kv_y(h):
        return copy_to(krows(chain, h), krows(chain, h), send_y.at[h], recv_y.at[h], dp, yny)

    def kv_s(j, h):
        g = chain if j == 0 else other
        return copy_to(krows(g, h), krows(g, h), send_s.at[2 * j + h], recv_s.at[2 * j + h], dp, sib)

    has_next = (n >= 2) & (n + 1 <= 7)
    has_prev = n >= 3
    ahead = copy_to(kblocks(OWN, 4),kblocks(PROMPT + 2, 4), fsend_l.at[0], frecv_l.at[0], dp, lax.rem(me + 2, 16))
    own_sib = copy_to(kblocks(OWN, 4),kblocks(PROMPT + 6, 4), fsend_l.at[1], frecv_l.at[1], dp, sib)
    kfar = copy_to(kblocks(OWN + 2, 2),kblocks(PROMPT, 2), fsend_l.at[2], frecv_l.at[2], dp, lax.rem(me + 3, 16))
    relay_full = copy_to(kblocks(PROMPT + 2, 4),kblocks(PROMPT + 6, 4), fsend_l.at[3], frecv_l.at[1], dp, sib)
    relay_half = copy_to(kblocks(PROMPT + 4, 2),kblocks(PROMPT, 2), fsend_l.at[4], frecv_l.at[2], dp, sib)
    sends_kfar = (c == 1) & (n >= 2) & (n + 2 <= 7)
    gets_kfar = (c == 0) & (n >= 4)

    @pl.when(z == 0)
    def _():
        kv_z(0, 1, 0).start()
        kv_z(1, 3, 1).start()
        kv_z(1, 1, 2).start()
        kv_z(0, 3, 3).start()
        for h in (0, 1):
            kv_y(h).start()
            kv_s(0, h).start()

    @pl.when((c == 0) & (n >= 2))
    def _():
        own_sib.start()

    @pl.when(has_next)
    def _():
        ahead.start()

    @pl.when(sends_kfar)
    def _():
        kfar.start()

    early = jnp.where(z == 1, 1, 0)
    order = (early, 1 - early)
    sums = (dv_ref, dk_ref)

    def half(h):
        return pl.ds(pl.multiple_of(h * 256, 256), 256)

    def rows(g, h):
        return pl.ds(pl.multiple_of(g * GRP + h * 256, 256), 256)

    def group(g):
        return pl.ds(pl.multiple_of(g * GRP, GRP), GRP)

    def blocks(first, count):
        return pl.ds(first * BLK, count * BLK)

    def cp_a(x, j):
        return copy_to(away.at[x, group(2 * j + 1 - c)], bufa.at[x, j],
                       send_a.at[2 * x + j], recv_a.at[2 * x + j], dp, sib)

    def cp_b(x, h):
        return copy_to(sa.at[x, half(h)], bufb.at[x, half(h)], send_b.at[2 * x + h], recv_b.at[2 * x + h], dp, yny)

    def cp_c(x, h, slot, zz):
        return copy_to(sb.at[x, half(h)], bufc.at[slot, x, half(h)], send_c.at[2 * x + h],
                       recv_c.at[4 * slot + 2 * x + h], dp, zz * 4 + 2 * y + c)

    from_next = (n >= 2) & (n + 1 <= 7)
    sends_near = (c == 1) & (n >= 2)
    gets_near = (c == 0) & (n >= 2)
    sends_far = (c == 0) & (n >= 4)
    gets_far = (c == 1) & (n >= 2) & (n + 2 <= 7)
    two_blocks = pl.ds(0, 2 * BLK)

    def leg(src, dst, k, x, to):
        return copy_to(src, dst, send_l.at[2 * k + x], recv_l.at[2 * k + x], dp, to)

    def hand_full(x):
        return leg(away.at[x, blocks(PROMPT + 6, 4)], bufs.at[x], 0, x, sib)

    def hand_half(x):
        return leg(away.at[x, blocks(PROMPT, 2)], bufs.at[x, two_blocks], 0, x, sib)

    def back(x):
        return leg(sl.at[x], bufl.at[0, x], 1, x, lax.rem(me + 14, 16))

    def near_back(x):
        return leg(away.at[x, blocks(PROMPT + 6, 4)], bufl.at[1, x], 2, x, sib)

    def far_back(x):
        return leg(away.at[x, blocks(PROMPT, 2)], bufl.at[2, x, two_blocks], 3, x, lax.rem(me + 13, 16))

    def hand_over(x, lo, hi):
        def one(s, _):
            rr = pl.ds(pl.multiple_of(s * BLK, BLK), BLK)
            away[x, rr, :] = sums[x][rr, :].astype(BF)
            return 0

        lax.fori_loop(lo, hi, one, 0)

    def local_start(x):
        @pl.when(has_prev & (c == 0))
        def _():
            hand_full(x).start()

        @pl.when(has_prev & (c == 1))
        def _():
            hand_half(x).start()

        @pl.when(sends_near)
        def _():
            near_back(x).start()

        @pl.when(sends_far)
        def _():
            far_back(x).start()

    def local_mid(x):
        @pl.when(has_prev & (c == 1))
        def _():
            hand_full(x).wait_recv()
            sl[x] = (away[x, blocks(PROMPT + 2, 4), :].astype(F32) + bufs[x].astype(F32)).astype(BF)
            back(x).start()

        @pl.when(has_prev & (c == 0))
        def _():
            hand_half(x).wait_recv()
            sl[x, 0:2 * BLK, :] = away[x, blocks(PROMPT + 2, 2), :]
            sl[x, 2 * BLK:, :] = (away[x, blocks(PROMPT + 4, 2), :].astype(F32)
                                  + bufs[x, 0:2 * BLK].astype(F32)).astype(BF)
            back(x).start()

    def local_end(x):
        @pl.when(from_next)
        def _():
            back(x).wait_recv()
            tot[x] += bufl[0, x].astype(F32)

        @pl.when(gets_near)
        def _():
            near_back(x).wait_recv()
            tot[x] += bufl[1, x].astype(F32)

        @pl.when(gets_far)
        def _():
            far_back(x).wait_recv()
            tot[x, 2 * BLK:, :] += bufl[2, x, 0:2 * BLK].astype(F32)

    def stage_b(x):
        cp_a(x, 1 - y).wait_recv()
        for h in order:
            sa[x, half(h), :] = (away[x, rows(2 * (1 - y) + c, h), :].astype(F32)
                                 + bufa[x, 1 - y, half(h), :].astype(F32)).astype(BF)
            cp_b(x, h).start()

    def stage_c(x):
        cp_a(x, y).wait_recv()
        for step, h in enumerate(order):
            tot[x, half(h), :] = (away[x, rows(2 * y + c, h), :].astype(F32)
                                  + bufa[x, y, half(h), :].astype(F32))
            cp_b(x, h).wait_recv()
            tot[x, half(h), :] += bufb[x, half(h), :].astype(F32)

            @pl.when(z == 2)
            def _(h=h):
                sb[x, half(h), :] = tot[x, half(h), :].astype(BF)
                cp_c(x, h, 0, 1 + 2 * h).start()

            if step == 0:
                @pl.when((z == 1) | (z == 3))
                def _(h=h):
                    sb[x, half(h), :] = tot[x, half(h), :].astype(BF)
                    cp_c(x, h, (z - 1) // 2, 0).start()

    def stage_d(x):
        h = 1 - early

        @pl.when((z == 1) | (z == 3))
        def _():
            cp_c(x, h, 0, 0).wait_recv()
            tot[x, half(h), :] += bufc[0, x, half(h), :].astype(F32)
            sb[x, half(h), :] = tot[x, half(h), :].astype(BF)
            cp_c(x, h, (z - 1) // 2, 0).start()

    def stage_e(x):
        own = sums[x][OWN * BLK:, :]

        @pl.when(z != 0)
        def _():
            tot[x] = own

        @pl.when(z == 0)
        def _():
            tot[x] += own
            for h in order:
                for slot in (0, 1):
                    cp_c(x, h, slot, 1).wait_recv()
                    tot[x, half(h), :] += bufc[slot, x, half(h), :].astype(F32)

    dk_ref[...] = jnp.zeros_like(dk_ref)
    dv_ref[...] = jnp.zeros_like(dv_ref)
    m_s[...] = jnp.full_like(m_s, LOW)
    s_s[...] = jnp.zeros_like(s_s)
    qpart[...] = jnp.zeros_like(qpart)
    gain = qg_ref[...]

    def facts(i):
        b = first + i
        start = jnp.int32(PROMPT)
        off = jnp.int32(0)
        live = jnp.int32(BLK)
        for r in range(8):
            n = len_ref[r]
            c = (n + BLK - 1) // BLK
            inside = (b >= start) & (b < start + c)
            off = jnp.where(inside, b - start, off)
            live = jnp.where(inside, jnp.minimum(n - (b - start) * BLK, BLK), live)
            start = start + c
        return b, off, live

    def prep(i, _):
        b, off, live = facts(i)
        src = jnp.int32(0)
        for j in range(4):
            src = jnp.where(from_ref[j] == b, j, src)
        rows = pl.ds(pl.multiple_of(i * BLK, BLK), BLK)
        srcv = jnp.full((BLK, BLK), src, jnp.int32)
        alive = (lax.broadcasted_iota(jnp.int32, (BLK, BLK), 0) < live).astype(F32)
        for h in range(HEADS):
            cols = pl.ds(h * BLK, BLK)
            x = q_ref[rows, cols].astype(F32)
            r = lax.rsqrt(jnp.mean(x * x, axis=-1, keepdims=True) + 1e-6)
            y = (x * r * gain).astype(BF)
            z = do_ref[0:BLK, cols].astype(F32)
            for j in range(1, 4):
                z = jnp.where(srcv == j, do_ref[j * BLK:(j + 1) * BLK, cols].astype(F32), z)
            z = (z * alive).astype(BF)
            t = i * TPB + h // HT
            e = pl.ds((h % HT) * BLK, BLK)
            qn[t, e, :] = y
            qt[t, :, e] = y.T
            dn[t, e, :] = z
            dt[t, :, e] = z.T
        return 0

    lax.fori_loop(0, 2, prep, 0)
    def got(h):
        kv_z(h, 0, 0).wait_recv()
        kv_y(h).start()
        kv_s(0, h).start()

    @pl.when(z == 1)
    def _():
        kv_z(0, 2, 0).wait_recv()
        kv_z(0, 2, 0).start()
        kv_y(0).start()
        kv_s(0, 0).start()
        got(1)

    @pl.when(z == 3)
    def _():
        kv_z(1, 2, 0).wait_recv()
        kv_z(1, 2, 0).start()
        kv_y(1).start()
        kv_s(0, 1).start()
        got(0)

    @pl.when(z == 2)
    def _():
        got(0)
        got(1)

    lax.fori_loop(2, 4, prep, 0)
    @pl.when(has_prev)
    def _():
        ahead.wait_recv()

    @pl.when(has_prev & (c == 1))
    def _():
        relay_full.start()

    @pl.when(has_prev & (c == 0))
    def _():
        relay_half.start()

    def y_got(h):
        copy_to(krows(other, h), krows(other, h), send_y.at[h], recv_y.at[h], dp, yny).wait_recv()
        kv_s(1, h).start()

    @pl.when(z != 3)
    def _():
        y_got(0)
        y_got(1)

    @pl.when(z == 3)
    def _():
        y_got(1)
        y_got(0)

    for j in (0, 1):
        for h in (0, 1):
            g = (2 * y + 1 - c) if j == 0 else (2 * (1 - y) + 1 - c)
            copy_to(krows(g, h), krows(g, h), send_s.at[2 * j + h], recv_s.at[2 * j + h], dp, sib).wait_recv()

    def slot_t(s, _):
        kt[s] = kv_ref[pl.ds(pl.multiple_of(s * BLK, BLK), BLK), 0:BLK].T
        return 0

    lax.fori_loop(0, PROMPT, slot_t, 0)
    lax.fori_loop(OWN, SLOTS, slot_t, 0)

    def local_arrive():
        @pl.when(((c == 1) & (n >= 2)) | ((c == 0) & has_prev))
        def _():
            own_sib.wait_recv()

        @pl.when(gets_kfar | ((c == 1) & has_prev))
        def _():
            kfar.wait_recv()

        lax.fori_loop(PROMPT, OWN, slot_t, 0)

    def per_block(i, _):
        b, off, live = facts(i)
        n_prompt = jnp.minimum(b, PROMPT)
        n_prev = jnp.clip(b - PROMPT, 0, REACH)
        pc = (n_prompt + CBP - 1) // CBP
        lc = (REACH - n_prev) // CBL
        keyi = lax.broadcasted_iota(jnp.int32, (BLK, RT), 0)
        toki = lax.rem(lax.broadcasted_iota(jnp.int32, (BLK, RT), 1), BLK)
        bias = jnp.where((keyi <= toki) & (keyi < live), 0.0, LOW)

        offv = jnp.full((8, CS), off, jnp.int32)

        def seen(pos):
            prompt = pos < PROMPT
            spare = jnp.where(prompt, n_prompt - 1 - pos, pos - PROMPT - REACH)
            return spare + offv * jnp.where(prompt, 0, 1) >= 0

        def per_tile(g, _):
            t = i * TPB + g

            def row0(pos):
                return pl.multiple_of(jnp.where(pos < PROMPT, pos, pos + i) * BLK, BLK)

            def first_pass(pos, nb, diag):
                r0 = row0(pos)
                kc = kv_ref[pl.ds(r0, nb * BLK), 0:BLK]
                for x in range(0, RT, CS):
                    cs = slice(x, x + CS)
                    s = nn(kc, qt[t, :, cs])
                    for u in range(nb):
                        su = s[u * BLK:(u + 1) * BLK]
                        if diag:
                            su = su + bias[:, cs]
                        su = su.reshape(BLK // 8, 8, CS)
                        m = jnp.max(su, axis=0) * SL2
                        w = jnp.exp2(su * SL2 - m[None])
                        s_s[pos + u, :, cs] = jnp.sum(w, axis=0)
                        if diag:
                            m_s[pos + u, :, cs] = m
                        else:
                            m_s[pos + u, :, cs] = jnp.where(seen(pos + u), m, LOW)
                        w_s[pos + u, :, cs] = w.reshape(BLK, CS)

            def over(body, init, between=None):
                init = lax.fori_loop(0, pc, lambda c, x: body(c * CBP, CBP, False, x), init)
                if between is not None:
                    between()
                init = lax.fori_loop(lc, REACH // CBL, lambda c, x: body(PROMPT + c * CBL, CBL, False, x), init)
                return body(POS - 1, 1, True, init)

            def p1(pos, nb, diag, x):
                first_pass(pos, nb, diag)
                return x

            def await_local():
                @pl.when(i == 0)
                def _():
                    local_arrive()

            over(p1, 0, await_local)
            m = m_s[...]
            top = jnp.max(jnp.max(m, axis=0), axis=0, keepdims=True)
            f = jnp.exp2(m - top[None])
            tot = jnp.sum(jnp.sum(f * s_s[...], axis=0), axis=0, keepdims=True)
            f_s[...] = f * (1.0 / tot)[None]

            drows = dn[t]
            def p3(pos, nb, diag, acc):
                r0 = row0(pos)
                vc = kv_ref[pl.ds(r0, nb * BLK), BLK:2 * BLK]
                accs, ps = [], []
                for x in range(0, RT, CS):
                    cs = slice(x, x + CS)
                    dp = nn(vc, dt[t, :, cs])
                    a = acc[:, cs]
                    pu = []
                    for u in range(nb):
                        du = dp[u * BLK:(u + 1) * BLK]
                        ch = (w_s[pos + u, :, cs].reshape(BLK // 8, 8, CS) * f_s[pos + u, :, cs][None]).reshape(BLK, CS)
                        chb = ch.astype(BF)
                        w_s[pos + u, :, cs] = ch
                        dp_s[pos + u, :, cs] = du
                        a = a + jnp.sum((chb.astype(F32) * du).reshape(BLK // 8, 8, CS), axis=0)
                        pu.append(chb)
                    accs.append(a)
                    ps.append(jnp.concatenate(pu, axis=0))
                p = jnp.concatenate(ps, axis=1)
                rows = pl.ds(r0, nb * BLK)
                dv_ref[rows, :] += nn(p, drows)
                return jnp.concatenate(accs, axis=1)

            delta = over(p3, jnp.zeros((8, RT), F32))
            @pl.when(i == 3)
            def _():
                hand_over(0, 0, OWN)
                for j in (0, 1):
                    cp_a(0, j).start()
                local_start(0)

            delta = jnp.sum(delta, axis=0, keepdims=True)
            qrows = qn[t]

            def p4(pos, nb, diag, dq):
                r0 = row0(pos)
                dss = []
                for u in range(nb):
                    ch = w_s[pos + u]
                    dss.append((ch * (dp_s[pos + u] - delta)).astype(BF))
                ds = jnp.concatenate(dss, axis=0) if nb > 1 else dss[0]
                rows = pl.ds(r0, nb * BLK)
                dk_ref[rows, :] += nn(ds, qrows)
                slot = r0 // BLK
                ktc = jnp.concatenate([kt[slot + u] for u in range(nb)], axis=1) if nb > 1 else kt[slot]
                dq_s[...] += nn(ktc, ds)
                return 0

            dq_s[...] = jnp.zeros_like(dq_s)
            p4(POS - 1, 1, True, 0)
            lax.fori_loop(lc, REACH // CBL, lambda c, x: p4(PROMPT + c * CBL, CBL, False, x), 0)

            @pl.when(i == 3)
            def _():
                hand_over(1, PROMPT, OWN)
                local_start(1)
                stage_b(0)
                local_mid(0)

            @pl.when(0 < pc)
            def _():
                p4(0, CBP, False, 0)

            @pl.when(i == 3)
            def _():
                hand_over(1, 0, 8)
                cp_a(1, 0).start()
                stage_c(0)

            @pl.when(1 < pc)
            def _():
                p4(CBP, CBP, False, 0)

            @pl.when(i == 3)
            def _():
                hand_over(1, 8, PROMPT)
                cp_a(1, 1).start()
                stage_d(0)

            dqt = dq_s[...]
            dq = dqt.T * SCALE
            rows = pl.ds(pl.multiple_of(i * BLK, BLK), BLK)
            part = jnp.zeros((8, BLK), F32)
            for u in range(HT):
                cols = pl.ds(pl.multiple_of((g * HT + u) * BLK, BLK), BLK)
                x = q_ref[rows, cols].astype(F32)
                r = lax.rsqrt(jnp.mean(x * x, axis=-1, keepdims=True) + 1e-6)
                unit = x * r
                dqu = dq[u * BLK:(u + 1) * BLK]
                both = dqu * unit
                part = part + jnp.sum(both.reshape(BLK // 8, 8, BLK), axis=0)
                mean = jnp.mean(both * gain, axis=-1, keepdims=True)
                gq_ref[rows, cols] = (r * (dqu * gain - unit * mean)).astype(BF)
            qpart[...] += part
            return 0

        lax.fori_loop(0, TPB, per_tile, 0)
        return 0

    lax.fori_loop(0, 4, per_block, 0)

    def key_part(k, acc):
        rr = pl.ds(pl.multiple_of(k * BLK, BLK), BLK)
        both = dk_ref[rr, :] * kv_ref[rr, 0:BLK].astype(F32)
        return acc + jnp.sum(both.reshape(BLK // 8, 8, BLK), axis=0)

    kpart = lax.fori_loop(0, SLOTS, key_part, jnp.zeros((8, BLK), F32))
    kgain = kg_ref[...]
    gown[...] = jnp.zeros_like(gown)
    gown[0:1, :] = jnp.sum(qpart[...], axis=0, keepdims=True)
    gown[1:2, :] = jnp.sum(kpart, axis=0, keepdims=True) * SCALE / kgain
    cg = [copy_to(gown, gall.at[me], send_g.at[o - 1], recv_g.at[me], dp, lax.rem(me + o, 16)) for o in range(1, 16)]
    ch = [copy_to(gsum, gdp.at[dp], send_g.at[14 + o], recv_g.at[16 + dp], lax.rem(dp + o, 8), me) for o in range(1, 8)]
    for q in cg:
        q.start()
    gall[me] = gown[...]
    stage_b(1)
    stage_e(0)
    for h in (0, 1):
        cp_b(1, h).wait_send()
    local_mid(1)
    stage_c(1)
    for o in range(1, 16):
        p = lax.rem(me + o, 16)
        copy_to(gown, gall.at[p], send_g.at[o - 1], recv_g.at[p], dp, p).wait_recv()
    total = gall[0]
    for o in range(1, 16):
        total = total + gall[o]
    gsum[...] = total
    for q in ch:
        q.start()
    gdp[dp] = total
    local_end(0)
    gv_ref[...] = tot[0].astype(BF)
    stage_d(1)
    stage_e(1)
    local_end(1)
    x = k_ref[...].astype(F32)
    r = lax.rsqrt(jnp.mean(x * x, axis=-1, keepdims=True) + 1e-6)
    unit = x * r
    dk = tot[1] * SCALE
    mean = jnp.mean(dk * unit * kgain, axis=-1, keepdims=True)
    gk_ref[...] = (r * (dk * kgain - unit * mean)).astype(BF)
    for o in range(1, 8):
        p = lax.rem(dp + o, 8)
        copy_to(gsum, gdp.at[p], send_g.at[14 + o], recv_g.at[16 + p], p, me).wait_recv()
    total = gdp[0]
    for o in range(1, 8):
        total = total + gdp[o]
    gain_ref[...] = total
    for q in cg + ch:
        q.wait_send()
    for x in (0, 1):
        for h in (0, 1):
            cp_a(x, h).wait_send()
            if x == 0:
                cp_b(x, h).wait_send()

        @pl.when(z != 0)
        def _(x=x):
            for h in (0, 1):
                cp_c(x, h, 0, 0).wait_send()

        @pl.when(has_prev & (c == 0))
        def _(x=x):
            hand_full(x).wait_send()

        @pl.when(has_prev & (c == 1))
        def _(x=x):
            hand_half(x).wait_send()

        @pl.when(has_prev)
        def _(x=x):
            back(x).wait_send()

        @pl.when(sends_near)
        def _(x=x):
            near_back(x).wait_send()

        @pl.when(sends_far)
        def _(x=x):
            far_back(x).wait_send()

    @pl.when(z == 0)
    def _():
        for k in range(4):
            kv_z(0, 1, k).wait_send()

    @pl.when((z == 1) | (z == 3))
    def _():
        kv_z(0, 1, 0).wait_send()

    for h in (0, 1):
        kv_y(h).wait_send()
        kv_s(0, h).wait_send()
        kv_s(1, h).wait_send()

    @pl.when((c == 0) & (n >= 2))
    def _():
        own_sib.wait_send()

    @pl.when(has_next)
    def _():
        ahead.wait_send()

    @pl.when(sends_kfar)
    def _():
        kfar.wait_send()

    @pl.when(has_prev & (c == 1))
    def _():
        relay_full.wait_send()

    @pl.when(has_prev & (c == 0))
    def _():
        relay_half.wait_send()


def fused(lens, frm, qg, kg, q, do, k, v):
    dma = pltpu.SemaphoreType.DMA
    rows = SLOTS * BLK
    tiles = 4096 // RT
    pair = pltpu.VMEM((2, GRP, BLK), BF)
    two = pltpu.VMEM((2, 2, GRP, BLK), BF)
    return pl.pallas_call(
        fused_kernel,
        out_shape=(
            jax.ShapeDtypeStruct((512, 1024), BF),
            jax.ShapeDtypeStruct((GRP, BLK), BF),
            jax.ShapeDtypeStruct((GRP, BLK), BF),
            jax.ShapeDtypeStruct((8, BLK), F32),
        ),
        in_specs=[SM, SM, VM, VM, VM, VM, VM, VM],
        out_specs=(VM, VM, VM, VM),
        scratch_shapes=[
            pltpu.VMEM((rows, 2 * BLK), BF),
            pltpu.VMEM((tiles, RT, BLK), BF),
            pltpu.VMEM((tiles, BLK, RT), BF),
            pltpu.VMEM((tiles, RT, BLK), BF),
            pltpu.VMEM((tiles, BLK, RT), BF),
            pltpu.VMEM((SLOTS, BLK, BLK), BF),
            pltpu.VMEM((POS, BLK, RT), F32),
            pltpu.VMEM((POS, BLK, RT), F32),
            pltpu.VMEM((POS, 8, RT), F32),
            pltpu.VMEM((POS, 8, RT), F32),
            pltpu.VMEM((POS, 8, RT), F32),
            pltpu.VMEM((BLK, RT), F32),
            pltpu.VMEM((rows, BLK), F32),
            pltpu.VMEM((rows, BLK), F32),
            pltpu.VMEM((8, BLK), F32),
            pltpu.VMEM((2, OWN * BLK, BLK), BF),
            two, pair, two, pltpu.VMEM((3, 2, GRP, BLK), BF), pair, pair, pair, pair,
            pltpu.VMEM((2, GRP, BLK), F32),
            pltpu.VMEM((8, BLK), F32),
            pltpu.VMEM((8, BLK), F32),
            pltpu.VMEM((16, 8, BLK), F32),
            pltpu.VMEM((8, 8, BLK), F32),
        ] + [dma((m,)) for m in (4, 2, 2, 2, 4, 4, 5, 3, 4, 4, 4, 4, 4, 8, 8, 8, 22, 24)],
        compiler_params=pltpu.CompilerParams(
            collective_id=0, has_side_effects=True, vmem_limit_bytes=60 * 1024 * 1024),
    )(lens, frm, qg, kg, q, do, k, v)


PIECES = 4


def hand_out_kernel(gains_ref, gq_ref, gk_ref, gv_ref, oq_ref, ok_ref, ov_ref, gq_gain_ref, gk_gain_ref,
                    bq, bk, bv, sin, sout):
    step = bq.shape[0] // PIECES
    legs = [(gq_ref.at[pl.ds(j * step, step)], bq.at[pl.ds(j * step, step)], oq_ref.at[pl.ds(j * step, step)])
            for j in range(PIECES)]
    legs += [(gk_ref, bk, ok_ref), (gv_ref, bv, ov_ref)]
    into = [pltpu.make_async_copy(x, m, sin.at[j]) for j, (x, m, _) in enumerate(legs)]
    out = [pltpu.make_async_copy(m, o, sout.at[j]) for j, (_, m, o) in enumerate(legs)]
    for copy in into:
        copy.start()
    gq_gain_ref[...] = gains_ref[0, :]
    gk_gain_ref[...] = gains_ref[1, :]
    for j in range(len(legs)):
        into[j].wait()
        out[j].start()
    for copy in out:
        copy.wait()


def hand_out(gains, gq, gk, gv):
    anywhere = pl.BlockSpec(memory_space=pl.ANY)
    flat = jax.ShapeDtypeStruct((BLK,), F32)
    dma = pltpu.SemaphoreType.DMA
    return pl.pallas_call(
        hand_out_kernel,
        out_shape=tuple(jax.ShapeDtypeStruct(t.shape, t.dtype) for t in (gq, gk, gv)) + (flat, flat),
        in_specs=[VM, anywhere, anywhere, anywhere],
        out_specs=(anywhere, anywhere, anywhere, VM, VM),
        scratch_shapes=[pltpu.VMEM(t.shape, t.dtype) for t in (gq, gk, gv)] + [dma((PIECES + 2,)), dma((PIECES + 2,))],
    )(gains, gq, gk, gv)


def body(q_raw, k_raw, values, d_out, q_gain, k_gain, resp_len, block_parent, block_from):
    gq, gk, gv, gains = fused(resp_len[0], block_from[0], q_gain.reshape(1, BLK), k_gain.reshape(1, BLK),
                              q_raw[0], d_out[0], k_raw[0], values[0])
    gq, gk, gv, q_gain_grad, k_gain_grad = hand_out(gains, gq, gk, gv)
    return gq[None], gk[None], gv[None], q_gain_grad, k_gain_grad


def solution(mesh):
    tok = P("dp", "ctx", None)
    return jax.shard_map(
        body,
        mesh=mesh,
        in_specs=(tok, tok, tok, tok, P(), P(), P("dp", None), P("dp", None), P("dp", "ctx")),
        out_specs=(tok, tok, tok, P(), P()),
        check_vma=False,
    )
```

```python
import functools, math
import jax, jax.numpy as jnp
from jax import lax
from jax.experimental import pallas as pl
from jax.experimental.pallas import tpu as pltpu
from jax.sharding import PartitionSpec as P

BLK = 128
HEADS = 8
PROMPT = 16
REACH = 10
SLOTS = 30
OWN = PROMPT + REACH
POS = 27
RT = 1024
CBP = 8
MG = 64
NG = BLK // MG
CBL = 10
HT = RT // BLK
CS = 256
TPB = HEADS // HT
LOW = -1e30
F32 = jnp.float32
BF = jnp.bfloat16
SCALE = 1.0 / math.sqrt(128.0)
LOG2E = 1.4426950408889634
SL2 = SCALE * LOG2E
VM = pl.BlockSpec(memory_space=pltpu.VMEM)
SM = pl.BlockSpec(memory_space=pltpu.SMEM)


def nt(a, b):
    return lax.dot_general(a, b, (((1,), (1,)), ((), ())), preferred_element_type=F32)


def nn(a, b):
    return jnp.dot(a, b, preferred_element_type=F32)


MESH = pl.DeviceIdType.MESH
GRP = 512


def copy_to(src, dst, send, recv, dp, ctx):
    return pltpu.make_async_remote_copy(
        src_ref=src, dst_ref=dst, send_sem=send, recv_sem=recv,
        device_id=(dp, ctx), device_id_type=MESH)


def greet(dp, me, wide):
    barrier = pltpu.get_barrier_semaphore()
    c = lax.rem(me, 2)
    y = lax.rem(me // 2, 2)
    if wide:
        targets = [(dp, lax.rem(me + o, 16)) for o in range(1, 16)]
        targets += [(lax.rem(dp + o, 8), me) for o in range(1, 8)]
    else:
        targets = [(dp, me + 1 - 2 * c), (dp, me + 2 - 4 * y)]
        targets += [(dp, lax.rem(me + o, 16)) for o in (4, 12, 2, 14, 3, 13)]
    for t in targets:
        pl.semaphore_signal(barrier, inc=1, device_id=t, device_id_type=MESH)
    pl.semaphore_wait(barrier, len(targets))


def fused_kernel(len_ref, from_ref, qg_ref, kg_ref, q_ref, do_ref, k_ref, v_ref,
                 gq_ref, gk_ref, gv_ref, gain_ref,
                 kv_ref, qn, qt, dn, dt, kt, w_s, dp_s, m_s, s_s, f_s, dq_s, dk_ref, dv_ref, qpart,
                 away, bufa, bufb, bufc, bufl, bufs, sa, sb, sl, tot, gown, gsum, gall, gdp,
                 send_z, recv_z, send_y, recv_y, send_s, recv_s, fsend_l, frecv_l,
                 send_a, recv_a, send_b, recv_b, send_c, recv_c, send_l, recv_l, send_g, recv_g):
    dp = lax.axis_index("dp")
    me = lax.axis_index("ctx")
    z = me // 4
    y = lax.rem(me // 2, 2)
    c = lax.rem(me, 2)
    n = me // 2
    first = me * 4
    sib = me + 1 - 2 * c
    yny = me + 2 - 4 * y
    kv_ref[PROMPT * BLK:OWN * BLK, :] = jnp.zeros((REACH * BLK, 2 * BLK), BF)
    x = k_ref[...].astype(F32)
    r = lax.rsqrt(jnp.mean(x * x, axis=-1, keepdims=True) + 1e-6)
    kv_ref[OWN * BLK:, 0:BLK] = (x * r * kg_ref[...]).astype(BF)
    kv_ref[OWN * BLK:, BLK:2 * BLK] = v_ref[...]

    @pl.when(z == 0)
    def _():
        kv_ref[pl.ds(pl.multiple_of(me * GRP, GRP), GRP), :] = kv_ref[OWN * BLK:, :]

    greet(dp, me, True)
    chain = 2 * y + c
    other = 2 * (1 - y) + c

    def krows(g, h):
        return kv_ref.at[pl.ds(pl.multiple_of(g * GRP + h * BLK, BLK), BLK)]

    def kblocks(first, count):
        return kv_ref.at[pl.ds(first * BLK, count * BLK)]

    def kv_z(h, zz, k):
        return copy_to(krows(chain, h), krows(chain, h), send_z.at[k], recv_z.at[h], dp, zz * 4 + chain)

    def kv_y(h):
        return copy_to(krows(chain, h), krows(chain, h), send_y.at[h], recv_y.at[h], dp, yny)

    def kv_s(j, h):
        g = chain if j == 0 else other
        return copy_to(krows(g, h), krows(g, h), send_s.at[4 * j + h], recv_s.at[4 * j + h], dp, sib)

    has_next = (n >= 2) & (n + 1 <= 7)
    has_prev = n >= 3
    ahead = copy_to(kblocks(OWN, 4),kblocks(PROMPT + 2, 4), fsend_l.at[0], frecv_l.at[0], dp, lax.rem(me + 2, 16))
    own_sib = copy_to(kblocks(OWN, 4),kblocks(PROMPT + 6, 4), fsend_l.at[1], frecv_l.at[1], dp, sib)
    kfar = copy_to(kblocks(OWN + 2, 2),kblocks(PROMPT, 2), fsend_l.at[2], frecv_l.at[2], dp, lax.rem(me + 3, 16))
    relay_full = copy_to(kblocks(PROMPT + 2, 4),kblocks(PROMPT + 6, 4), fsend_l.at[3], frecv_l.at[1], dp, sib)
    relay_half = copy_to(kblocks(PROMPT + 4, 2),kblocks(PROMPT, 2), fsend_l.at[4], frecv_l.at[2], dp, sib)
    sends_kfar = (c == 1) & (n >= 2) & (n + 2 <= 7)
    gets_kfar = (c == 0) & (n >= 4)

    shift = jnp.where(z >= 2, 2, 0)
    pieces = [lax.rem(p + shift, 4) for p in range(4)]

    @pl.when(z == 0)
    def _():
        for p in range(4):
            kv_z(p, 1, 2 * p).start()
            kv_z((p + 2) % 4, 3, 2 * p + 1).start()
        for p in range(4):
            kv_y(p).start()
            kv_s(0, p).start()

    @pl.when((c == 0) & (n >= 2))
    def _():
        own_sib.start()

    @pl.when(has_next)
    def _():
        ahead.start()

    @pl.when(sends_kfar)
    def _():
        kfar.start()

    early = jnp.where(z == 1, 1, 0)
    order = (early, 1 - early)
    sums = (dv_ref, dk_ref)

    def half(h):
        return pl.ds(pl.multiple_of(h * 256, 256), 256)

    def rows(g, h):
        return pl.ds(pl.multiple_of(g * GRP + h * 256, 256), 256)

    def group(g):
        return pl.ds(pl.multiple_of(g * GRP, GRP), GRP)

    def blocks(first, count):
        return pl.ds(first * BLK, count * BLK)

    def cp_a(x, j):
        return copy_to(away.at[x, group(2 * j + 1 - c)], bufa.at[x, j],
                       send_a.at[2 * x + j], recv_a.at[2 * x + j], dp, sib)

    def cp_b(x, h):
        return copy_to(sa.at[x, half(h)], bufb.at[x, half(h)], send_b.at[2 * x + h], recv_b.at[2 * x + h], dp, yny)

    def cp_c(x, h, slot, zz):
        return copy_to(sb.at[x, half(h)], bufc.at[slot, x, half(h)], send_c.at[2 * x + h],
                       recv_c.at[4 * slot + 2 * x + h], dp, zz * 4 + 2 * y + c)

    from_next = (n >= 2) & (n + 1 <= 7)
    sends_near = (c == 1) & (n >= 2)
    gets_near = (c == 0) & (n >= 2)
    sends_far = (c == 0) & (n >= 4)
    gets_far = (c == 1) & (n >= 2) & (n + 2 <= 7)
    two_blocks = pl.ds(0, 2 * BLK)

    def leg(src, dst, k, x, to):
        return copy_to(src, dst, send_l.at[2 * k + x], recv_l.at[2 * k + x], dp, to)

    def hand_full(x):
        return leg(away.at[x, blocks(PROMPT + 6, 4)], bufs.at[x], 0, x, sib)

    def hand_half(x):
        return leg(away.at[x, blocks(PROMPT, 2)], bufs.at[x, two_blocks], 0, x, sib)

    def back(x):
        return leg(sl.at[x], bufl.at[0, x], 1, x, lax.rem(me + 14, 16))

    def near_back(x):
        return leg(away.at[x, blocks(PROMPT + 6, 4)], bufl.at[1, x], 2, x, sib)

    def far_back(x):
        return leg(away.at[x, blocks(PROMPT, 2)], bufl.at[2, x, two_blocks], 3, x, lax.rem(me + 13, 16))

    def hand_over(x, lo, hi):
        def one(s, _):
            rr = pl.ds(pl.multiple_of(s * BLK, BLK), BLK)
            away[x, rr, :] = sums[x][rr, :].astype(BF)
            return 0

        lax.fori_loop(lo, hi, one, 0)

    def local_start(x):
        @pl.when(has_prev & (c == 0))
        def _():
            hand_full(x).start()

        @pl.when(has_prev & (c == 1))
        def _():
            hand_half(x).start()

        @pl.when(sends_near)
        def _():
            near_back(x).start()

        @pl.when(sends_far)
        def _():
            far_back(x).start()

    def local_mid(x):
        @pl.when(has_prev & (c == 1))
        def _():
            hand_full(x).wait_recv()
            sl[x] = (away[x, blocks(PROMPT + 2, 4), :].astype(F32) + bufs[x].astype(F32)).astype(BF)
            back(x).start()

        @pl.when(has_prev & (c == 0))
        def _():
            hand_half(x).wait_recv()
            sl[x, 0:2 * BLK, :] = away[x, blocks(PROMPT + 2, 2), :]
            sl[x, 2 * BLK:, :] = (away[x, blocks(PROMPT + 4, 2), :].astype(F32)
                                  + bufs[x, 0:2 * BLK].astype(F32)).astype(BF)
            back(x).start()

    def local_end(x):
        @pl.when(from_next)
        def _():
            back(x).wait_recv()
            tot[x] += bufl[0, x].astype(F32)

        @pl.when(gets_near)
        def _():
            near_back(x).wait_recv()
            tot[x] += bufl[1, x].astype(F32)

        @pl.when(gets_far)
        def _():
            far_back(x).wait_recv()
            tot[x, 2 * BLK:, :] += bufl[2, x, 0:2 * BLK].astype(F32)

    def stage_b(x):
        cp_a(x, 1 - y).wait_recv()
        for h in order:
            sa[x, half(h), :] = (away[x, rows(2 * (1 - y) + c, h), :].astype(F32)
                                 + bufa[x, 1 - y, half(h), :].astype(F32)).astype(BF)
            cp_b(x, h).start()

    def stage_c(x):
        cp_a(x, y).wait_recv()
        for step, h in enumerate(order):
            tot[x, half(h), :] = (away[x, rows(2 * y + c, h), :].astype(F32)
                                  + bufa[x, y, half(h), :].astype(F32))
            cp_b(x, h).wait_recv()
            tot[x, half(h), :] += bufb[x, half(h), :].astype(F32)

            @pl.when(z == 2)
            def _(h=h):
                sb[x, half(h), :] = tot[x, half(h), :].astype(BF)
                cp_c(x, h, 0, 1 + 2 * h).start()

            if step == 0:
                @pl.when((z == 1) | (z == 3))
                def _(h=h):
                    sb[x, half(h), :] = tot[x, half(h), :].astype(BF)
                    cp_c(x, h, (z - 1) // 2, 0).start()

    def stage_d(x):
        h = 1 - early

        @pl.when((z == 1) | (z == 3))
        def _():
            cp_c(x, h, 0, 0).wait_recv()
            tot[x, half(h), :] += bufc[0, x, half(h), :].astype(F32)
            sb[x, half(h), :] = tot[x, half(h), :].astype(BF)
            cp_c(x, h, (z - 1) // 2, 0).start()

    def stage_e(x):
        own = sums[x][OWN * BLK:, :]

        @pl.when(z != 0)
        def _():
            tot[x] = own

        @pl.when(z == 0)
        def _():
            tot[x] += own
            for h in order:
                for slot in (0, 1):
                    cp_c(x, h, slot, 1).wait_recv()
                    tot[x, half(h), :] += bufc[slot, x, half(h), :].astype(F32)

    dk_ref[...] = jnp.zeros_like(dk_ref)
    dv_ref[...] = jnp.zeros_like(dv_ref)
    m_s[...] = jnp.full_like(m_s, LOW)
    s_s[...] = jnp.zeros_like(s_s)
    qpart[...] = jnp.zeros_like(qpart)
    gain = qg_ref[...]

    def facts(i):
        b = first + i
        start = jnp.int32(PROMPT)
        off = jnp.int32(0)
        live = jnp.int32(BLK)
        for r in range(8):
            n = len_ref[r]
            c = (n + BLK - 1) // BLK
            inside = (b >= start) & (b < start + c)
            off = jnp.where(inside, b - start, off)
            live = jnp.where(inside, jnp.minimum(n - (b - start) * BLK, BLK), live)
            start = start + c
        return b, off, live

    def prep(i, _):
        b, off, live = facts(i)
        src = jnp.int32(0)
        for j in range(4):
            src = jnp.where(from_ref[j] == b, j, src)
        rows = pl.ds(pl.multiple_of(i * BLK, BLK), BLK)
        srcv = jnp.full((BLK, BLK), src, jnp.int32)
        alive = (lax.broadcasted_iota(jnp.int32, (BLK, BLK), 0) < live).astype(F32)
        for h in range(HEADS):
            cols = pl.ds(h * BLK, BLK)
            x = q_ref[rows, cols].astype(F32)
            r = lax.rsqrt(jnp.mean(x * x, axis=-1, keepdims=True) + 1e-6)
            y = (x * r * gain).astype(BF)
            z = do_ref[0:BLK, cols].astype(F32)
            for j in range(1, 4):
                z = jnp.where(srcv == j, do_ref[j * BLK:(j + 1) * BLK, cols].astype(F32), z)
            z = (z * alive).astype(BF)
            t = i * TPB + h // HT
            e = pl.ds((h % HT) * BLK, BLK)
            qn[t, e, :] = y
            qt[t, :, e] = y.T
            dn[t, e, :] = z
            dt[t, :, e] = z.T
        return 0

    lax.fori_loop(0, 2, prep, 0)
    @pl.when(z != 0)
    def _():
        for p in range(4):
            h = pieces[p]
            kv_z(h, 0, 0).wait_recv()
            if p < 2:
                @pl.when(z != 2)
                def _():
                    kv_z(h, 2, p).start()
            kv_y(h).start()
            kv_s(0, h).start()

    lax.fori_loop(2, 4, prep, 0)
    @pl.when(has_prev)
    def _():
        ahead.wait_recv()

    @pl.when(has_prev & (c == 1))
    def _():
        relay_full.start()

    @pl.when(has_prev & (c == 0))
    def _():
        relay_half.start()

    def chain_arrive():
        g = 2 * y + 1 - c
        for h in pieces:
            copy_to(krows(g, h), krows(g, h), send_s.at[h], recv_s.at[h], dp, sib).wait_recv()

    def rest_arrive():
        for h in pieces:
            copy_to(krows(other, h), krows(other, h), send_y.at[h], recv_y.at[h], dp, yny).wait_recv()
            kv_s(1, h).start()
        g = 2 * (1 - y) + 1 - c
        for h in pieces:
            copy_to(krows(g, h), krows(g, h), send_s.at[4 + h], recv_s.at[4 + h], dp, sib).wait_recv()
        lax.fori_loop(0, PROMPT, slot_t, 0)

    def slot_t(s, _):
        kt[s] = kv_ref[pl.ds(pl.multiple_of(s * BLK, BLK), BLK), 0:BLK].T
        return 0

    lax.fori_loop(OWN, SLOTS, slot_t, 0)

    def local_arrive():
        @pl.when(((c == 1) & (n >= 2)) | ((c == 0) & has_prev))
        def _():
            own_sib.wait_recv()

        @pl.when(gets_kfar | ((c == 1) & has_prev))
        def _():
            kfar.wait_recv()

        lax.fori_loop(PROMPT, OWN, slot_t, 0)

    def per_block(i, _):
        b, off, live = facts(i)
        n_prompt = jnp.minimum(b, PROMPT)
        n_prev = jnp.clip(b - PROMPT, 0, REACH)
        pc = (n_prompt + CBP - 1) // CBP
        lc = (REACH - n_prev) // CBL
        whole = jnp.minimum(n_prompt, 1)
        keyi = lax.broadcasted_iota(jnp.int32, (BLK, RT), 0)
        toki = lax.rem(lax.broadcasted_iota(jnp.int32, (BLK, RT), 1), BLK)
        bias = jnp.where((keyi <= toki) & (keyi < live), 0.0, LOW)

        offv = jnp.full((8, CS), off, jnp.int32)

        def seen(pos):
            prompt = pos < PROMPT
            spare = jnp.where(prompt, n_prompt - 1 - pos, pos - PROMPT - REACH)
            return spare + offv * jnp.where(prompt, 0, 1) >= 0

        def per_tile(g, _):
            t = i * TPB + g

            def row0(pos):
                return pl.multiple_of(jnp.where(pos < PROMPT, pos, pos + i) * BLK, BLK)

            def first_pass(pos, nb, diag):
                r0 = row0(pos)
                kc = kv_ref[pl.ds(r0, nb * BLK), 0:BLK]
                for x in range(0, RT, CS):
                    cs = slice(x, x + CS)
                    s = nn(kc, qt[t, :, cs])
                    for u in range(nb):
                        for q in range(NG):
                            lo = u * BLK + q * MG
                            su = s[lo:lo + MG]
                            if diag:
                                su = su + bias[q * MG:(q + 1) * MG, cs]
                            su = su.reshape(MG // 8, 8, CS)
                            m = jnp.max(su, axis=0) * SL2
                            w = jnp.exp2(su * SL2 - m[None])
                            s_s[(pos + u) * NG + q, :, cs] = jnp.sum(w, axis=0)
                            if diag:
                                m_s[(pos + u) * NG + q, :, cs] = m
                            else:
                                m_s[(pos + u) * NG + q, :, cs] = jnp.where(seen(pos + u), m, LOW)
                            w_s[pos + u, q * MG:(q + 1) * MG, cs] = w.reshape(MG, CS)

            def local(body, init):
                init = lax.fori_loop(lc, REACH // CBL, lambda c, x: body(PROMPT + c * CBL, CBL, False, x), init)
                return body(POS - 1, 1, True, init)

            def over(body, init):
                return local(body, lax.fori_loop(0, whole, lambda c, x: body(0, PROMPT, False, x), init))

            def p1(pos, nb, diag, x):
                first_pass(pos, nb, diag)
                return x

            @pl.when(i == 0)
            def _():
                local_arrive()
                local(p1, 0)
                chain_arrive()
                lax.fori_loop(0, whole, lambda c, x: p1(y * CBP, CBP, False, x), 0)
                rest_arrive()
                lax.fori_loop(0, whole, lambda c, x: p1((1 - y) * CBP, CBP, False, x), 0)

            @pl.when(i > 0)
            def _():
                over(p1, 0)

            m = m_s[...]
            top = jnp.max(jnp.max(m, axis=0), axis=0, keepdims=True)
            f = jnp.exp2(m - top[None])
            tot = jnp.sum(jnp.sum(f * s_s[...], axis=0), axis=0, keepdims=True)
            f_s[...] = f * (1.0 / tot)[None]

            drows = dn[t]
            def p3(pos, nb, diag, acc):
                r0 = row0(pos)
                vc = kv_ref[pl.ds(r0, nb * BLK), BLK:2 * BLK]
                accs, ps = [], []
                for x in range(0, RT, CS):
                    cs = slice(x, x + CS)
                    dp = nn(vc, dt[t, :, cs])
                    a = acc[:, cs]
                    pu = []
                    for u in range(nb):
                        du = dp[u * BLK:(u + 1) * BLK]
                        parts = []
                        for q in range(NG):
                            wq = w_s[pos + u, q * MG:(q + 1) * MG, cs].reshape(MG // 8, 8, CS)
                            parts.append((wq * f_s[(pos + u) * NG + q, :, cs][None]).reshape(MG, CS))
                        ch = jnp.concatenate(parts, axis=0)
                        chb = ch.astype(BF)
                        w_s[pos + u, :, cs] = ch
                        dp_s[pos + u, :, cs] = du
                        a = a + jnp.sum((chb.astype(F32) * du).reshape(BLK // 8, 8, CS), axis=0)
                        pu.append(chb)
                    accs.append(a)
                    ps.append(jnp.concatenate(pu, axis=0))
                p = jnp.concatenate(ps, axis=1)
                rows = pl.ds(r0, nb * BLK)
                dv_ref[rows, :] += nn(p, drows)
                return jnp.concatenate(accs, axis=1)

            delta = over(p3, jnp.zeros((8, RT), F32))
            @pl.when(i == 3)
            def _():
                hand_over(0, 0, OWN)
                for j in (0, 1):
                    cp_a(0, j).start()
                local_start(0)

            delta = jnp.sum(delta, axis=0, keepdims=True)
            qrows = qn[t]

            def p4(pos, nb, diag, dq):
                r0 = row0(pos)
                dss = []
                for u in range(nb):
                    ch = w_s[pos + u]
                    dss.append((ch * (dp_s[pos + u] - delta)).astype(BF))
                ds = jnp.concatenate(dss, axis=0) if nb > 1 else dss[0]
                rows = pl.ds(r0, nb * BLK)
                dk_ref[rows, :] += nn(ds, qrows)
                slot = r0 // BLK
                ktc = jnp.concatenate([kt[slot + u] for u in range(nb)], axis=1) if nb > 1 else kt[slot]
                dq_s[i] += nn(ktc, ds)
                return 0

            dq_s[i] = jnp.zeros((BLK, RT), F32)
            p4(POS - 1, 1, True, 0)
            lax.fori_loop(lc, REACH // CBL, lambda c, x: p4(PROMPT + c * CBL, CBL, False, x), 0)

            @pl.when(i == 3)
            def _():
                hand_over(1, PROMPT, OWN)
                local_start(1)
                stage_b(0)
                local_mid(0)

            @pl.when(0 < pc)
            def _():
                p4(0, CBP, False, 0)

            @pl.when(i == 3)
            def _():
                hand_over(1, 0, 8)
                cp_a(1, 0).start()
                stage_c(0)

            @pl.when(1 < pc)
            def _():
                p4(CBP, CBP, False, 0)

            @pl.when(i == 3)
            def _():
                hand_over(1, 8, PROMPT)
                cp_a(1, 1).start()
                stage_d(0)

            return 0

        lax.fori_loop(0, TPB, per_tile, 0)
        return 0

    lax.fori_loop(0, 4, per_block, 0)
    stage_b(1)

    def finish(i, _):
        dqt = dq_s[i]
        dq = dqt.T * SCALE
        rows = pl.ds(pl.multiple_of(i * BLK, BLK), BLK)
        part = jnp.zeros((8, BLK), F32)
        for u in range(HT):
            cols = pl.ds(pl.multiple_of(u * BLK, BLK), BLK)
            x = q_ref[rows, cols].astype(F32)
            r = lax.rsqrt(jnp.mean(x * x, axis=-1, keepdims=True) + 1e-6)
            unit = x * r
            dqu = dq[u * BLK:(u + 1) * BLK]
            both = dqu * unit
            part = part + jnp.sum(both.reshape(BLK // 8, 8, BLK), axis=0)
            mean = jnp.mean(both * gain, axis=-1, keepdims=True)
            gq_ref[rows, cols] = (r * (dqu * gain - unit * mean)).astype(BF)
        qpart[...] += part
        return 0

    lax.fori_loop(0, 4, finish, 0)

    def key_part(k, acc):
        rr = pl.ds(pl.multiple_of(k * BLK, BLK), BLK)
        both = dk_ref[rr, :] * kv_ref[rr, 0:BLK].astype(F32)
        return acc + jnp.sum(both.reshape(BLK // 8, 8, BLK), axis=0)

    kpart = lax.fori_loop(0, SLOTS, key_part, jnp.zeros((8, BLK), F32))
    kgain = kg_ref[...]
    gown[...] = jnp.zeros_like(gown)
    gown[0:1, :] = jnp.sum(qpart[...], axis=0, keepdims=True)
    gown[1:2, :] = jnp.sum(kpart, axis=0, keepdims=True) * SCALE / kgain
    cg = [copy_to(gown, gall.at[me], send_g.at[o - 1], recv_g.at[me], dp, lax.rem(me + o, 16)) for o in range(1, 16)]
    ch = [copy_to(gsum, gdp.at[dp], send_g.at[14 + o], recv_g.at[16 + dp], lax.rem(dp + o, 8), me) for o in range(1, 8)]
    for q in cg:
        q.start()
    gall[me] = gown[...]
    stage_e(0)
    for h in (0, 1):
        cp_b(1, h).wait_send()
    local_mid(1)
    stage_c(1)
    for o in range(1, 16):
        p = lax.rem(me + o, 16)
        copy_to(gown, gall.at[p], send_g.at[o - 1], recv_g.at[p], dp, p).wait_recv()
    total = gall[0]
    for o in range(1, 16):
        total = total + gall[o]
    gsum[...] = total
    for q in ch:
        q.start()
    gdp[dp] = total
    local_end(0)
    gv_ref[...] = tot[0].astype(BF)
    stage_d(1)
    stage_e(1)
    local_end(1)
    x = k_ref[...].astype(F32)
    r = lax.rsqrt(jnp.mean(x * x, axis=-1, keepdims=True) + 1e-6)
    unit = x * r
    dk = tot[1] * SCALE
    mean = jnp.mean(dk * unit * kgain, axis=-1, keepdims=True)
    gk_ref[...] = (r * (dk * kgain - unit * mean)).astype(BF)
    for o in range(1, 8):
        p = lax.rem(dp + o, 8)
        copy_to(gsum, gdp.at[p], send_g.at[14 + o], recv_g.at[16 + p], p, me).wait_recv()
    total = gdp[0]
    for o in range(1, 8):
        total = total + gdp[o]
    gain_ref[...] = total
    for q in cg + ch:
        q.wait_send()
    for x in (0, 1):
        for h in (0, 1):
            cp_a(x, h).wait_send()
            if x == 0:
                cp_b(x, h).wait_send()

        @pl.when(z != 0)
        def _(x=x):
            for h in (0, 1):
                cp_c(x, h, 0, 0).wait_send()

        @pl.when(has_prev & (c == 0))
        def _(x=x):
            hand_full(x).wait_send()

        @pl.when(has_prev & (c == 1))
        def _(x=x):
            hand_half(x).wait_send()

        @pl.when(has_prev)
        def _(x=x):
            back(x).wait_send()

        @pl.when(sends_near)
        def _(x=x):
            near_back(x).wait_send()

        @pl.when(sends_far)
        def _(x=x):
            far_back(x).wait_send()

    @pl.when(z == 0)
    def _():
        for k in range(8):
            kv_z(0, 1, k).wait_send()

    @pl.when((z == 1) | (z == 3))
    def _():
        for k in range(2):
            kv_z(0, 1, k).wait_send()

    for h in range(4):
        kv_y(h).wait_send()
        kv_s(0, h).wait_send()
        kv_s(1, h).wait_send()

    @pl.when((c == 0) & (n >= 2))
    def _():
        own_sib.wait_send()

    @pl.when(has_next)
    def _():
        ahead.wait_send()

    @pl.when(sends_kfar)
    def _():
        kfar.wait_send()

    @pl.when(has_prev & (c == 1))
    def _():
        relay_full.wait_send()

    @pl.when(has_prev & (c == 0))
    def _():
        relay_half.wait_send()


def fused(lens, frm, qg, kg, q, do, k, v):
    dma = pltpu.SemaphoreType.DMA
    rows = SLOTS * BLK
    tiles = 4096 // RT
    pair = pltpu.VMEM((2, GRP, BLK), BF)
    two = pltpu.VMEM((2, 2, GRP, BLK), BF)
    return pl.pallas_call(
        fused_kernel,
        out_shape=(
            jax.ShapeDtypeStruct((512, 1024), BF),
            jax.ShapeDtypeStruct((GRP, BLK), BF),
            jax.ShapeDtypeStruct((GRP, BLK), BF),
            jax.ShapeDtypeStruct((8, BLK), F32),
        ),
        in_specs=[SM, SM, VM, VM, VM, VM, VM, VM],
        out_specs=(VM, VM, VM, VM),
        scratch_shapes=[
            pltpu.VMEM((rows, 2 * BLK), BF),
            pltpu.VMEM((tiles, RT, BLK), BF),
            pltpu.VMEM((tiles, BLK, RT), BF),
            pltpu.VMEM((tiles, RT, BLK), BF),
            pltpu.VMEM((tiles, BLK, RT), BF),
            pltpu.VMEM((SLOTS, BLK, BLK), BF),
            pltpu.VMEM((POS, BLK, RT), F32),
            pltpu.VMEM((POS, BLK, RT), F32),
            pltpu.VMEM((POS * NG, 8, RT), F32),
            pltpu.VMEM((POS * NG, 8, RT), F32),
            pltpu.VMEM((POS * NG, 8, RT), F32),
            pltpu.VMEM((tiles, BLK, RT), F32),
            pltpu.VMEM((rows, BLK), F32),
            pltpu.VMEM((rows, BLK), F32),
            pltpu.VMEM((8, BLK), F32),
            pltpu.VMEM((2, OWN * BLK, BLK), BF),
            two, pair, two, pltpu.VMEM((3, 2, GRP, BLK), BF), pair, pair, pair, pair,
            pltpu.VMEM((2, GRP, BLK), F32),
            pltpu.VMEM((8, BLK), F32),
            pltpu.VMEM((8, BLK), F32),
            pltpu.VMEM((16, 8, BLK), F32),
            pltpu.VMEM((8, 8, BLK), F32),
        ] + [dma((m,)) for m in (8, 4, 4, 4, 8, 8, 5, 3, 4, 4, 4, 4, 4, 8, 8, 8, 22, 24)],
        compiler_params=pltpu.CompilerParams(
            collective_id=0, has_side_effects=True, vmem_limit_bytes=60 * 1024 * 1024),
    )(lens, frm, qg, kg, q, do, k, v)


PIECES = 4


def hand_out_kernel(gains_ref, gq_ref, gk_ref, gv_ref, oq_ref, ok_ref, ov_ref, gq_gain_ref, gk_gain_ref,
                    bq, bk, bv, sin, sout):
    step = bq.shape[0] // PIECES
    legs = [(gq_ref.at[pl.ds(j * step, step)], bq.at[pl.ds(j * step, step)], oq_ref.at[pl.ds(j * step, step)])
            for j in range(PIECES)]
    legs += [(gk_ref, bk, ok_ref), (gv_ref, bv, ov_ref)]
    into = [pltpu.make_async_copy(x, m, sin.at[j]) for j, (x, m, _) in enumerate(legs)]
    out = [pltpu.make_async_copy(m, o, sout.at[j]) for j, (_, m, o) in enumerate(legs)]
    for copy in into:
        copy.start()
    gq_gain_ref[...] = gains_ref[0, :]
    gk_gain_ref[...] = gains_ref[1, :]
    for j in range(len(legs)):
        into[j].wait()
        out[j].start()
    for copy in out:
        copy.wait()


def hand_out(gains, gq, gk, gv):
    anywhere = pl.BlockSpec(memory_space=pl.ANY)
    flat = jax.ShapeDtypeStruct((BLK,), F32)
    dma = pltpu.SemaphoreType.DMA
    return pl.pallas_call(
        hand_out_kernel,
        out_shape=tuple(jax.ShapeDtypeStruct(t.shape, t.dtype) for t in (gq, gk, gv)) + (flat, flat),
        in_specs=[VM, anywhere, anywhere, anywhere],
        out_specs=(anywhere, anywhere, anywhere, VM, VM),
        scratch_shapes=[pltpu.VMEM(t.shape, t.dtype) for t in (gq, gk, gv)] + [dma((PIECES + 2,)), dma((PIECES + 2,))],
    )(gains, gq, gk, gv)


def body(q_raw, k_raw, values, d_out, q_gain, k_gain, resp_len, block_parent, block_from):
    gq, gk, gv, gains = fused(resp_len[0], block_from[0], q_gain.reshape(1, BLK), k_gain.reshape(1, BLK),
                              q_raw[0], d_out[0], k_raw[0], values[0])
    gq, gk, gv, q_gain_grad, k_gain_grad = hand_out(gains, gq, gk, gv)
    return gq[None], gk[None], gv[None], q_gain_grad, k_gain_grad


def solution(mesh):
    tok = P("dp", "ctx", None)
    return jax.shard_map(
        body,
        mesh=mesh,
        in_specs=(tok, tok, tok, tok, P(), P(), P("dp", None), P("dp", None), P("dp", "ctx")),
        out_specs=(tok, tok, tok, P(), P()),
        check_vma=False,
    )
```

```python
import functools, math
import jax, jax.numpy as jnp
from jax import lax
from jax.experimental import pallas as pl
from jax.experimental.pallas import tpu as pltpu
from jax.sharding import PartitionSpec as P

BLK = 128
HEADS = 8
PROMPT = 16
REACH = 10
SLOTS = 30
OWN = PROMPT + REACH
POS = 27
RT = 1024
CBP = 8
MG = 64
NG = BLK // MG
CBL = 10
HT = RT // BLK
CS = 256
TPB = HEADS // HT
LOW = -1e30
F32 = jnp.float32
BF = jnp.bfloat16
SCALE = 1.0 / math.sqrt(128.0)
LOG2E = 1.4426950408889634
SL2 = SCALE * LOG2E
VM = pl.BlockSpec(memory_space=pltpu.VMEM)
SM = pl.BlockSpec(memory_space=pltpu.SMEM)


def nt(a, b):
    return lax.dot_general(a, b, (((1,), (1,)), ((), ())), preferred_element_type=F32)


def nn(a, b):
    return jnp.dot(a, b, preferred_element_type=F32)


MESH = pl.DeviceIdType.MESH
GRP = 512


def copy_to(src, dst, send, recv, dp, ctx):
    return pltpu.make_async_remote_copy(
        src_ref=src, dst_ref=dst, send_sem=send, recv_sem=recv,
        device_id=(dp, ctx), device_id_type=MESH)


def announce(dp, me):
    barrier = pltpu.get_barrier_semaphore()
    targets = [(dp, lax.rem(me + o, 16)) for o in range(1, 16)]
    targets += [(lax.rem(dp + o, 8), me) for o in range(1, 8)]
    for t in targets:
        pl.semaphore_signal(barrier, inc=1, device_id=t, device_id_type=MESH)


def fused_kernel(len_ref, from_ref, qg_ref, kg_ref, q_in, do_in, k_in, v_in,
                 gq_out, gk_ref, gv_ref, gain_ref,
                 q_ref, do_ref, k_ref, v_ref, gq_ref, in_sem, out_sem, kv_ref, qn, qt, dn, dt, kt, w_s, dp_s, m_s, s_s, f_s, dq_s, dk_ref, dv_ref, qpart,
                 away, bufa, bufb, bufc, bufl, bufs, sa, sb, sl, tot, gown, gsum, gall, gdp,
                 send_z, recv_z, send_y, recv_y, send_s, recv_s, fsend_l, frecv_l,
                 send_a, recv_a, send_b, recv_b, send_c, recv_c, send_l, recv_l, send_g, recv_g):
    dp = lax.axis_index("dp")
    me = lax.axis_index("ctx")
    z = me // 4
    y = lax.rem(me // 2, 2)
    c = lax.rem(me, 2)
    n = me // 2
    first = me * 4
    sib = me + 1 - 2 * c
    yny = me + 2 - 4 * y
    arriving = [pltpu.make_async_copy(src, dst, in_sem.at[j])
                for j, (src, dst) in enumerate(((k_in, k_ref), (v_in, v_ref), (q_in, q_ref), (do_in, do_ref)))]
    for copy in arriving:
        copy.start()
    kv_ref[PROMPT * BLK:OWN * BLK, :] = jnp.zeros((REACH * BLK, 2 * BLK), BF)
    announce(dp, me)
    arriving[0].wait()
    arriving[1].wait()
    x = k_ref[...].astype(F32)
    r = lax.rsqrt(jnp.mean(x * x, axis=-1, keepdims=True) + 1e-6)
    kv_ref[OWN * BLK:, 0:BLK] = (x * r * kg_ref[...]).astype(BF)
    kv_ref[OWN * BLK:, BLK:2 * BLK] = v_ref[...]

    @pl.when(z == 0)
    def _():
        kv_ref[pl.ds(pl.multiple_of(me * GRP, GRP), GRP), :] = kv_ref[OWN * BLK:, :]

    pl.semaphore_wait(pltpu.get_barrier_semaphore(), 22)
    chain = 2 * y + c
    other = 2 * (1 - y) + c

    def krows(g, h):
        return kv_ref.at[pl.ds(pl.multiple_of(g * GRP + h * BLK, BLK), BLK)]

    def kblocks(first, count):
        return kv_ref.at[pl.ds(first * BLK, count * BLK)]

    def kv_z(h, zz, k):
        return copy_to(krows(chain, h), krows(chain, h), send_z.at[k], recv_z.at[h], dp, zz * 4 + chain)

    def kv_y(h):
        return copy_to(krows(chain, h), krows(chain, h), send_y.at[h], recv_y.at[h], dp, yny)

    def kv_s(j, h):
        g = chain if j == 0 else other
        return copy_to(krows(g, h), krows(g, h), send_s.at[4 * j + h], recv_s.at[4 * j + h], dp, sib)

    has_next = (n >= 2) & (n + 1 <= 7)
    has_prev = n >= 3
    ahead = copy_to(kblocks(OWN, 4),kblocks(PROMPT + 2, 4), fsend_l.at[0], frecv_l.at[0], dp, lax.rem(me + 2, 16))
    own_sib = copy_to(kblocks(OWN, 4),kblocks(PROMPT + 6, 4), fsend_l.at[1], frecv_l.at[1], dp, sib)
    kfar = copy_to(kblocks(OWN + 2, 2),kblocks(PROMPT, 2), fsend_l.at[2], frecv_l.at[2], dp, lax.rem(me + 3, 16))
    relay_full = copy_to(kblocks(PROMPT + 2, 4),kblocks(PROMPT + 6, 4), fsend_l.at[3], frecv_l.at[1], dp, sib)
    relay_half = copy_to(kblocks(PROMPT + 4, 2),kblocks(PROMPT, 2), fsend_l.at[4], frecv_l.at[2], dp, sib)
    sends_kfar = (c == 1) & (n >= 2) & (n + 2 <= 7)
    gets_kfar = (c == 0) & (n >= 4)

    shift = jnp.where(z >= 2, 2, 0)
    pieces = [lax.rem(p + shift, 4) for p in range(4)]

    @pl.when(z == 0)
    def _():
        for p in range(4):
            kv_z(p, 1, 2 * p).start()
            kv_z((p + 2) % 4, 3, 2 * p + 1).start()
        for p in range(4):
            kv_y(p).start()
            kv_s(0, p).start()

    @pl.when((c == 0) & (n >= 2))
    def _():
        own_sib.start()

    @pl.when(has_next)
    def _():
        ahead.start()

    @pl.when(sends_kfar)
    def _():
        kfar.start()

    early = jnp.where(z == 1, 1, 0)
    order = (early, 1 - early)
    sums = (dv_ref, dk_ref)

    def half(h):
        return pl.ds(pl.multiple_of(h * 256, 256), 256)

    def rows(g, h):
        return pl.ds(pl.multiple_of(g * GRP + h * 256, 256), 256)

    def group(g):
        return pl.ds(pl.multiple_of(g * GRP, GRP), GRP)

    def blocks(first, count):
        return pl.ds(first * BLK, count * BLK)

    def cp_a(x, j):
        return copy_to(away.at[x, group(2 * j + 1 - c)], bufa.at[x, j],
                       send_a.at[2 * x + j], recv_a.at[2 * x + j], dp, sib)

    def cp_b(x, h):
        return copy_to(sa.at[x, half(h)], bufb.at[x, half(h)], send_b.at[2 * x + h], recv_b.at[2 * x + h], dp, yny)

    def cp_c(x, h, slot, zz):
        return copy_to(sb.at[x, half(h)], bufc.at[slot, x, half(h)], send_c.at[2 * x + h],
                       recv_c.at[4 * slot + 2 * x + h], dp, zz * 4 + 2 * y + c)

    from_next = (n >= 2) & (n + 1 <= 7)
    sends_near = (c == 1) & (n >= 2)
    gets_near = (c == 0) & (n >= 2)
    sends_far = (c == 0) & (n >= 4)
    gets_far = (c == 1) & (n >= 2) & (n + 2 <= 7)
    two_blocks = pl.ds(0, 2 * BLK)

    def leg(src, dst, k, x, to):
        return copy_to(src, dst, send_l.at[2 * k + x], recv_l.at[2 * k + x], dp, to)

    def hand_full(x):
        return leg(away.at[x, blocks(PROMPT + 6, 4)], bufs.at[x], 0, x, sib)

    def hand_half(x):
        return leg(away.at[x, blocks(PROMPT, 2)], bufs.at[x, two_blocks], 0, x, sib)

    def back(x):
        return leg(sl.at[x], bufl.at[0, x], 1, x, lax.rem(me + 14, 16))

    def near_back(x):
        return leg(away.at[x, blocks(PROMPT + 6, 4)], bufl.at[1, x], 2, x, sib)

    def far_back(x):
        return leg(away.at[x, blocks(PROMPT, 2)], bufl.at[2, x, two_blocks], 3, x, lax.rem(me + 13, 16))

    def hand_over(x, lo, hi):
        def one(s, _):
            rr = pl.ds(pl.multiple_of(s * BLK, BLK), BLK)
            away[x, rr, :] = sums[x][rr, :].astype(BF)
            return 0

        lax.fori_loop(lo, hi, one, 0)

    def local_start(x):
        @pl.when(has_prev & (c == 0))
        def _():
            hand_full(x).start()

        @pl.when(has_prev & (c == 1))
        def _():
            hand_half(x).start()

        @pl.when(sends_near)
        def _():
            near_back(x).start()

        @pl.when(sends_far)
        def _():
            far_back(x).start()

    def local_mid(x):
        @pl.when(has_prev & (c == 1))
        def _():
            hand_full(x).wait_recv()
            sl[x] = (away[x, blocks(PROMPT + 2, 4), :].astype(F32) + bufs[x].astype(F32)).astype(BF)
            back(x).start()

        @pl.when(has_prev & (c == 0))
        def _():
            hand_half(x).wait_recv()
            sl[x, 0:2 * BLK, :] = away[x, blocks(PROMPT + 2, 2), :]
            sl[x, 2 * BLK:, :] = (away[x, blocks(PROMPT + 4, 2), :].astype(F32)
                                  + bufs[x, 0:2 * BLK].astype(F32)).astype(BF)
            back(x).start()

    def local_end(x):
        @pl.when(from_next)
        def _():
            back(x).wait_recv()
            tot[x] += bufl[0, x].astype(F32)

        @pl.when(gets_near)
        def _():
            near_back(x).wait_recv()
            tot[x] += bufl[1, x].astype(F32)

        @pl.when(gets_far)
        def _():
            far_back(x).wait_recv()
            tot[x, 2 * BLK:, :] += bufl[2, x, 0:2 * BLK].astype(F32)

    def stage_b(x):
        cp_a(x, 1 - y).wait_recv()
        for h in order:
            sa[x, half(h), :] = (away[x, rows(2 * (1 - y) + c, h), :].astype(F32)
                                 + bufa[x, 1 - y, half(h), :].astype(F32)).astype(BF)
            cp_b(x, h).start()

    def stage_c(x):
        cp_a(x, y).wait_recv()
        for step, h in enumerate(order):
            tot[x, half(h), :] = (away[x, rows(2 * y + c, h), :].astype(F32)
                                  + bufa[x, y, half(h), :].astype(F32))
            cp_b(x, h).wait_recv()
            tot[x, half(h), :] += bufb[x, half(h), :].astype(F32)

            @pl.when(z == 2)
            def _(h=h):
                sb[x, half(h), :] = tot[x, half(h), :].astype(BF)
                cp_c(x, h, 0, 1 + 2 * h).start()

            if step == 0:
                @pl.when((z == 1) | (z == 3))
                def _(h=h):
                    sb[x, half(h), :] = tot[x, half(h), :].astype(BF)
                    cp_c(x, h, (z - 1) // 2, 0).start()

    def stage_d(x):
        h = 1 - early

        @pl.when((z == 1) | (z == 3))
        def _():
            cp_c(x, h, 0, 0).wait_recv()
            tot[x, half(h), :] += bufc[0, x, half(h), :].astype(F32)
            sb[x, half(h), :] = tot[x, half(h), :].astype(BF)
            cp_c(x, h, (z - 1) // 2, 0).start()

    def stage_e(x):
        own = sums[x][OWN * BLK:, :]

        @pl.when(z != 0)
        def _():
            tot[x] = own

        @pl.when(z == 0)
        def _():
            tot[x] += own
            for h in order:
                for slot in (0, 1):
                    cp_c(x, h, slot, 1).wait_recv()
                    tot[x, half(h), :] += bufc[slot, x, half(h), :].astype(F32)

    dk_ref[...] = jnp.zeros_like(dk_ref)
    dv_ref[...] = jnp.zeros_like(dv_ref)
    m_s[...] = jnp.full_like(m_s, LOW)
    s_s[...] = jnp.zeros_like(s_s)
    qpart[...] = jnp.zeros_like(qpart)
    gain = qg_ref[...]

    def facts(i):
        b = first + i
        start = jnp.int32(PROMPT)
        off = jnp.int32(0)
        live = jnp.int32(BLK)
        for r in range(8):
            n = len_ref[r]
            c = (n + BLK - 1) // BLK
            inside = (b >= start) & (b < start + c)
            off = jnp.where(inside, b - start, off)
            live = jnp.where(inside, jnp.minimum(n - (b - start) * BLK, BLK), live)
            start = start + c
        return b, off, live

    def prep(i, _):
        b, off, live = facts(i)
        src = jnp.int32(0)
        for j in range(4):
            src = jnp.where(from_ref[j] == b, j, src)
        rows = pl.ds(pl.multiple_of(i * BLK, BLK), BLK)
        srcv = jnp.full((BLK, BLK), src, jnp.int32)
        alive = (lax.broadcasted_iota(jnp.int32, (BLK, BLK), 0) < live).astype(F32)
        for h in range(HEADS):
            cols = pl.ds(h * BLK, BLK)
            x = q_ref[rows, cols].astype(F32)
            r = lax.rsqrt(jnp.mean(x * x, axis=-1, keepdims=True) + 1e-6)
            y = (x * r * gain).astype(BF)
            z = do_ref[0:BLK, cols].astype(F32)
            for j in range(1, 4):
                z = jnp.where(srcv == j, do_ref[j * BLK:(j + 1) * BLK, cols].astype(F32), z)
            z = (z * alive).astype(BF)
            t = i * TPB + h // HT
            e = pl.ds((h % HT) * BLK, BLK)
            qn[t, e, :] = y
            qt[t, :, e] = y.T
            dn[t, e, :] = z
            dt[t, :, e] = z.T
        return 0

    arriving[2].wait()
    arriving[3].wait()
    lax.fori_loop(0, 2, prep, 0)
    @pl.when(z != 0)
    def _():
        for p in range(4):
            h = pieces[p]
            kv_z(h, 0, 0).wait_recv()
            if p < 2:
                @pl.when(z != 2)
                def _():
                    kv_z(h, 2, p).start()
            kv_y(h).start()
            kv_s(0, h).start()

    lax.fori_loop(2, 4, prep, 0)
    @pl.when(has_prev)
    def _():
        ahead.wait_recv()

    @pl.when(has_prev & (c == 1))
    def _():
        relay_full.start()

    @pl.when(has_prev & (c == 0))
    def _():
        relay_half.start()

    def chain_arrive():
        g = 2 * y + 1 - c
        for h in pieces:
            copy_to(krows(g, h), krows(g, h), send_s.at[h], recv_s.at[h], dp, sib).wait_recv()

    def rest_arrive():
        for h in pieces:
            copy_to(krows(other, h), krows(other, h), send_y.at[h], recv_y.at[h], dp, yny).wait_recv()
            kv_s(1, h).start()
        g = 2 * (1 - y) + 1 - c
        for h in pieces:
            copy_to(krows(g, h), krows(g, h), send_s.at[4 + h], recv_s.at[4 + h], dp, sib).wait_recv()
        lax.fori_loop(0, PROMPT, slot_t, 0)

    def slot_t(s, _):
        kt[s] = kv_ref[pl.ds(pl.multiple_of(s * BLK, BLK), BLK), 0:BLK].T
        return 0

    lax.fori_loop(OWN, SLOTS, slot_t, 0)

    def local_arrive():
        @pl.when(((c == 1) & (n >= 2)) | ((c == 0) & has_prev))
        def _():
            own_sib.wait_recv()

        @pl.when(gets_kfar | ((c == 1) & has_prev))
        def _():
            kfar.wait_recv()

        lax.fori_loop(PROMPT, OWN, slot_t, 0)

    def per_block(i, _):
        b, off, live = facts(i)
        n_prompt = jnp.minimum(b, PROMPT)
        n_prev = jnp.clip(b - PROMPT, 0, REACH)
        pc = (n_prompt + CBP - 1) // CBP
        lc = (REACH - n_prev) // CBL
        whole = jnp.minimum(n_prompt, 1)
        keyi = lax.broadcasted_iota(jnp.int32, (BLK, RT), 0)
        toki = lax.rem(lax.broadcasted_iota(jnp.int32, (BLK, RT), 1), BLK)
        bias = jnp.where((keyi <= toki) & (keyi < live), 0.0, LOW)

        offv = jnp.full((8, CS), off, jnp.int32)

        def seen(pos):
            prompt = pos < PROMPT
            spare = jnp.where(prompt, n_prompt - 1 - pos, pos - PROMPT - REACH)
            return spare + offv * jnp.where(prompt, 0, 1) >= 0

        def per_tile(g, _):
            t = i * TPB + g

            def row0(pos):
                return pl.multiple_of(jnp.where(pos < PROMPT, pos, pos + i) * BLK, BLK)

            def first_pass(pos, nb, diag):
                r0 = row0(pos)
                kc = kv_ref[pl.ds(r0, nb * BLK), 0:BLK]
                for x in range(0, RT, CS):
                    cs = slice(x, x + CS)
                    s = nn(kc, qt[t, :, cs])
                    for u in range(nb):
                        for q in range(NG):
                            lo = u * BLK + q * MG
                            su = s[lo:lo + MG]
                            if diag:
                                su = su + bias[q * MG:(q + 1) * MG, cs]
                            su = su.reshape(MG // 8, 8, CS)
                            m = jnp.max(su, axis=0) * SL2
                            w = jnp.exp2(su * SL2 - m[None])
                            s_s[(pos + u) * NG + q, :, cs] = jnp.sum(w, axis=0)
                            if diag:
                                m_s[(pos + u) * NG + q, :, cs] = m
                            else:
                                m_s[(pos + u) * NG + q, :, cs] = jnp.where(seen(pos + u), m, LOW)
                            w_s[pos + u, q * MG:(q + 1) * MG, cs] = w.reshape(MG, CS)

            def local(body, init):
                init = lax.fori_loop(lc, REACH // CBL, lambda c, x: body(PROMPT + c * CBL, CBL, False, x), init)
                return body(POS - 1, 1, True, init)

            def over(body, init):
                return local(body, lax.fori_loop(0, whole, lambda c, x: body(0, PROMPT, False, x), init))

            def p1(pos, nb, diag, x):
                first_pass(pos, nb, diag)
                return x

            @pl.when(i == 0)
            def _():
                local_arrive()
                local(p1, 0)
                chain_arrive()
                lax.fori_loop(0, whole, lambda c, x: p1(y * CBP, CBP, False, x), 0)
                rest_arrive()
                lax.fori_loop(0, whole, lambda c, x: p1((1 - y) * CBP, CBP, False, x), 0)

            @pl.when(i > 0)
            def _():
                over(p1, 0)

            m = m_s[...]
            top = jnp.max(jnp.max(m, axis=0), axis=0, keepdims=True)
            f = jnp.exp2(m - top[None])
            tot = jnp.sum(jnp.sum(f * s_s[...], axis=0), axis=0, keepdims=True)
            f_s[...] = f * (1.0 / tot)[None]

            drows = dn[t]
            def p3(pos, nb, diag, acc):
                r0 = row0(pos)
                vc = kv_ref[pl.ds(r0, nb * BLK), BLK:2 * BLK]
                accs, ps = [], []
                for x in range(0, RT, CS):
                    cs = slice(x, x + CS)
                    dp = nn(vc, dt[t, :, cs])
                    a = acc[:, cs]
                    pu = []
                    for u in range(nb):
                        du = dp[u * BLK:(u + 1) * BLK]
                        parts = []
                        for q in range(NG):
                            wq = w_s[pos + u, q * MG:(q + 1) * MG, cs].reshape(MG // 8, 8, CS)
                            parts.append((wq * f_s[(pos + u) * NG + q, :, cs][None]).reshape(MG, CS))
                        ch = jnp.concatenate(parts, axis=0)
                        chb = ch.astype(BF)
                        w_s[pos + u, :, cs] = ch
                        dp_s[pos + u, :, cs] = du
                        a = a + jnp.sum((chb.astype(F32) * du).reshape(BLK // 8, 8, CS), axis=0)
                        pu.append(chb)
                    accs.append(a)
                    ps.append(jnp.concatenate(pu, axis=0))
                p = jnp.concatenate(ps, axis=1)
                rows = pl.ds(r0, nb * BLK)
                dv_ref[rows, :] += nn(p, drows)
                return jnp.concatenate(accs, axis=1)

            delta = over(p3, jnp.zeros((8, RT), F32))
            @pl.when(i == 3)
            def _():
                hand_over(0, 0, OWN)
                for j in (0, 1):
                    cp_a(0, j).start()
                local_start(0)

            delta = jnp.sum(delta, axis=0, keepdims=True)
            qrows = qn[t]

            def key_side(pos, nb, keep):
                rr = pl.ds(row0(pos), nb * BLK)
                dss = []
                for u in range(nb):
                    ds = (w_s[pos + u] * (dp_s[pos + u] - delta)).astype(BF)
                    if keep:
                        w_s[pos + u] = ds.astype(F32)
                    dss.append(ds)
                ds = jnp.concatenate(dss, axis=0) if nb > 1 else dss[0]
                dk_ref[rr, :] += nn(ds, qrows)
                return ds

            def query_side(pos, nb, ds):
                slot = row0(pos) // BLK
                ktc = jnp.concatenate([kt[slot + u] for u in range(nb)], axis=1) if nb > 1 else kt[slot]
                dq_s[i] += nn(ktc, ds)

            def p4(pos, nb, diag, dq):
                query_side(pos, nb, key_side(pos, nb, False))
                return dq

            def p4_keys(pos, nb, diag, dq):
                key_side(pos, nb, True)
                return dq

            def p4_queries(pos, nb, diag, dq):
                parts = [w_s[pos + u].astype(BF) for u in range(nb)]
                query_side(pos, nb, jnp.concatenate(parts, axis=0) if nb > 1 else parts[0])
                return dq

            dq_s[i] = jnp.zeros((BLK, RT), F32)

            @pl.when(i < 3)
            def _():
                lax.fori_loop(0, pc, lambda c, x: p4(c * CBP, CBP, False, x), 0)
                local(p4, 0)

            @pl.when(i == 3)
            def _():
                for j in (0, 1):
                    @pl.when(j < pc)
                    def _(j=j):
                        p4_keys(j * CBP, CBP, False, 0)

                    hand_over(1, 8 * j, 8 * j + 8)
                    cp_a(1, j).start()
                stage_b(0)
                local(p4_keys, 0)
                hand_over(1, PROMPT, OWN)
                stage_b(1)
                local_start(1)
                lax.fori_loop(0, pc, lambda c, x: p4_queries(c * CBP, CBP, False, x), 0)
                local(p4_queries, 0)

            return 0

        lax.fori_loop(0, TPB, per_tile, 0)
        return 0

    lax.fori_loop(0, 4, per_block, 0)

    def finish(i, _):
        dqt = dq_s[i]
        dq = dqt.T * SCALE
        rows = pl.ds(pl.multiple_of(i * BLK, BLK), BLK)
        part = jnp.zeros((8, BLK), F32)
        for u in range(HT):
            cols = pl.ds(pl.multiple_of(u * BLK, BLK), BLK)
            x = q_ref[rows, cols].astype(F32)
            r = lax.rsqrt(jnp.mean(x * x, axis=-1, keepdims=True) + 1e-6)
            unit = x * r
            dqu = dq[u * BLK:(u + 1) * BLK]
            both = dqu * unit
            part = part + jnp.sum(both.reshape(BLK // 8, 8, BLK), axis=0)
            mean = jnp.mean(both * gain, axis=-1, keepdims=True)
            gq_ref[rows, cols] = (r * (dqu * gain - unit * mean)).astype(BF)
        qpart[...] += part
        return 0

    lax.fori_loop(0, 4, finish, 0)
    leaving = pltpu.make_async_copy(gq_ref, gq_out, out_sem.at[0])
    leaving.start()

    def key_part(k, acc):
        rr = pl.ds(pl.multiple_of(k * BLK, BLK), BLK)
        both = dk_ref[rr, :] * kv_ref[rr, 0:BLK].astype(F32)
        return acc + jnp.sum(both.reshape(BLK // 8, 8, BLK), axis=0)

    kpart = lax.fori_loop(0, SLOTS, key_part, jnp.zeros((8, BLK), F32))
    kgain = kg_ref[...]
    gown[...] = jnp.zeros_like(gown)
    gown[0:1, :] = jnp.sum(qpart[...], axis=0, keepdims=True)
    gown[1:2, :] = jnp.sum(kpart, axis=0, keepdims=True) * SCALE / kgain
    cg = [copy_to(gown, gall.at[me], send_g.at[o - 1], recv_g.at[me], dp, lax.rem(me + o, 16)) for o in range(1, 16)]
    ch = [copy_to(gsum, gdp.at[dp], send_g.at[14 + o], recv_g.at[16 + dp], lax.rem(dp + o, 8), me) for o in range(1, 8)]
    for q in cg:
        q.start()
    gall[me] = gown[...]
    for x in (0, 1):
        for h in (0, 1):
            cp_b(x, h).wait_send()
        local_mid(x)
    stage_c(0)
    stage_c(1)
    for o in range(1, 16):
        p = lax.rem(me + o, 16)
        copy_to(gown, gall.at[p], send_g.at[o - 1], recv_g.at[p], dp, p).wait_recv()
    total = gall[0]
    for o in range(1, 16):
        total = total + gall[o]
    gsum[...] = total
    for q in ch:
        q.start()
    gdp[dp] = total
    stage_d(0)
    stage_d(1)
    stage_e(0)
    local_end(0)
    gv_ref[...] = tot[0].astype(BF)
    stage_e(1)
    local_end(1)
    x = k_ref[...].astype(F32)
    r = lax.rsqrt(jnp.mean(x * x, axis=-1, keepdims=True) + 1e-6)
    unit = x * r
    dk = tot[1] * SCALE
    mean = jnp.mean(dk * unit * kgain, axis=-1, keepdims=True)
    gk_ref[...] = (r * (dk * kgain - unit * mean)).astype(BF)
    for o in range(1, 8):
        p = lax.rem(dp + o, 8)
        copy_to(gsum, gdp.at[p], send_g.at[14 + o], recv_g.at[16 + p], p, me).wait_recv()
    total = gdp[0]
    for o in range(1, 8):
        total = total + gdp[o]
    gain_ref[...] = total
    for q in cg + ch:
        q.wait_send()
    leaving.wait()
    for x in (0, 1):
        for h in (0, 1):
            cp_a(x, h).wait_send()

        @pl.when(z != 0)
        def _(x=x):
            for h in (0, 1):
                cp_c(x, h, 0, 0).wait_send()

        @pl.when(has_prev & (c == 0))
        def _(x=x):
            hand_full(x).wait_send()

        @pl.when(has_prev & (c == 1))
        def _(x=x):
            hand_half(x).wait_send()

        @pl.when(has_prev)
        def _(x=x):
            back(x).wait_send()

        @pl.when(sends_near)
        def _(x=x):
            near_back(x).wait_send()

        @pl.when(sends_far)
        def _(x=x):
            far_back(x).wait_send()

    @pl.when(z == 0)
    def _():
        for k in range(8):
            kv_z(0, 1, k).wait_send()

    @pl.when((z == 1) | (z == 3))
    def _():
        for k in range(2):
            kv_z(0, 1, k).wait_send()

    for h in range(4):
        kv_y(h).wait_send()
        kv_s(0, h).wait_send()
        kv_s(1, h).wait_send()

    @pl.when((c == 0) & (n >= 2))
    def _():
        own_sib.wait_send()

    @pl.when(has_next)
    def _():
        ahead.wait_send()

    @pl.when(sends_kfar)
    def _():
        kfar.wait_send()

    @pl.when(has_prev & (c == 1))
    def _():
        relay_full.wait_send()

    @pl.when(has_prev & (c == 0))
    def _():
        relay_half.wait_send()


def fused(lens, frm, qg, kg, q, do, k, v):
    dma = pltpu.SemaphoreType.DMA
    rows = SLOTS * BLK
    tiles = 4096 // RT
    pair = pltpu.VMEM((2, GRP, BLK), BF)
    anywhere = pl.BlockSpec(memory_space=pl.ANY)
    wide, narrow = pltpu.VMEM((GRP, 8 * BLK), BF), pltpu.VMEM((GRP, BLK), BF)
    two = pltpu.VMEM((2, 2, GRP, BLK), BF)
    return pl.pallas_call(
        fused_kernel,
        out_shape=(
            jax.ShapeDtypeStruct((512, 1024), BF),
            jax.ShapeDtypeStruct((GRP, BLK), BF),
            jax.ShapeDtypeStruct((GRP, BLK), BF),
            jax.ShapeDtypeStruct((8, BLK), F32),
        ),
        in_specs=[SM, SM, VM, VM] + [anywhere] * 4,
        out_specs=(anywhere, VM, VM, VM),
        scratch_shapes=[
            wide, wide, narrow, narrow, wide, dma((4,)), dma((1,)),
            pltpu.VMEM((rows, 2 * BLK), BF),
            pltpu.VMEM((tiles, RT, BLK), BF),
            pltpu.VMEM((tiles, BLK, RT), BF),
            pltpu.VMEM((tiles, RT, BLK), BF),
            pltpu.VMEM((tiles, BLK, RT), BF),
            pltpu.VMEM((SLOTS, BLK, BLK), BF),
            pltpu.VMEM((POS, BLK, RT), F32),
            pltpu.VMEM((POS, BLK, RT), F32),
            pltpu.VMEM((POS * NG, 8, RT), F32),
            pltpu.VMEM((POS * NG, 8, RT), F32),
            pltpu.VMEM((POS * NG, 8, RT), F32),
            pltpu.VMEM((tiles, BLK, RT), F32),
            pltpu.VMEM((rows, BLK), F32),
            pltpu.VMEM((rows, BLK), F32),
            pltpu.VMEM((8, BLK), F32),
            pltpu.VMEM((2, OWN * BLK, BLK), BF),
            two, pair, two, pltpu.VMEM((3, 2, GRP, BLK), BF), pair, pair, pair, pair,
            pltpu.VMEM((2, GRP, BLK), F32),
            pltpu.VMEM((8, BLK), F32),
            pltpu.VMEM((8, BLK), F32),
            pltpu.VMEM((16, 8, BLK), F32),
            pltpu.VMEM((8, 8, BLK), F32),
        ] + [dma((m,)) for m in (8, 4, 4, 4, 8, 8, 5, 3, 4, 4, 4, 4, 4, 8, 8, 8, 22, 24)],
        compiler_params=pltpu.CompilerParams(
            collective_id=0, has_side_effects=True, vmem_limit_bytes=60 * 1024 * 1024),
    )(lens, frm, qg, kg, q, do, k, v)


PIECES = 4


def hand_out_kernel(gains_ref, gq_ref, gk_ref, gv_ref, oq_ref, ok_ref, ov_ref, gq_gain_ref, gk_gain_ref,
                    bq, bk, bv, sin, sout):
    step = bq.shape[0] // PIECES
    legs = [(gq_ref.at[pl.ds(j * step, step)], bq.at[pl.ds(j * step, step)], oq_ref.at[pl.ds(j * step, step)])
            for j in range(PIECES)]
    legs += [(gk_ref, bk, ok_ref), (gv_ref, bv, ov_ref)]
    into = [pltpu.make_async_copy(x, m, sin.at[j]) for j, (x, m, _) in enumerate(legs)]
    out = [pltpu.make_async_copy(m, o, sout.at[j]) for j, (_, m, o) in enumerate(legs)]
    for copy in into:
        copy.start()
    gq_gain_ref[...] = gains_ref[0, :]
    gk_gain_ref[...] = gains_ref[1, :]
    for j in range(len(legs)):
        into[j].wait()
        out[j].start()
    for copy in out:
        copy.wait()


def hand_out(gains, gq, gk, gv):
    anywhere = pl.BlockSpec(memory_space=pl.ANY)
    flat = jax.ShapeDtypeStruct((BLK,), F32)
    dma = pltpu.SemaphoreType.DMA
    return pl.pallas_call(
        hand_out_kernel,
        out_shape=tuple(jax.ShapeDtypeStruct(t.shape, t.dtype) for t in (gq, gk, gv)) + (flat, flat),
        in_specs=[VM, anywhere, anywhere, anywhere],
        out_specs=(anywhere, anywhere, anywhere, VM, VM),
        scratch_shapes=[pltpu.VMEM(t.shape, t.dtype) for t in (gq, gk, gv)] + [dma((PIECES + 2,)), dma((PIECES + 2,))],
    )(gains, gq, gk, gv)


def body(q_raw, k_raw, values, d_out, q_gain, k_gain, resp_len, block_parent, block_from):
    gq, gk, gv, gains = fused(resp_len[0], block_from[0], q_gain.reshape(1, BLK), k_gain.reshape(1, BLK),
                              q_raw[0], d_out[0], k_raw[0], values[0])
    gq, gk, gv, q_gain_grad, k_gain_grad = hand_out(gains, gq, gk, gv)
    return gq[None], gk[None], gv[None], q_gain_grad, k_gain_grad


def solution(mesh):
    tok = P("dp", "ctx", None)
    return jax.shard_map(
        body,
        mesh=mesh,
        in_specs=(tok, tok, tok, tok, P(), P(), P("dp", None), P("dp", None), P("dp", "ctx")),
        out_specs=(tok, tok, tok, P(), P()),
        check_vma=False,
    )
```

```python
import functools, math
import jax, jax.numpy as jnp
from jax import lax
from jax.experimental import pallas as pl
from jax.experimental.pallas import tpu as pltpu
from jax.sharding import PartitionSpec as P

BLK = 128
HEADS = 8
PROMPT = 16
REACH = 10
SLOTS = 30
OWN = PROMPT + REACH
POS = 27
RT = 1024
CBP = 8
MG = 64
NG = BLK // MG
HT = RT // BLK
CS = 256
TPB = HEADS // HT
LOW = -1e30
F32 = jnp.float32
BF = jnp.bfloat16
SCALE = 1.0 / math.sqrt(128.0)
LOG2E = 1.4426950408889634
SL2 = SCALE * LOG2E
VM = pl.BlockSpec(memory_space=pltpu.VMEM)
SM = pl.BlockSpec(memory_space=pltpu.SMEM)


def nt(a, b):
    return lax.dot_general(a, b, (((1,), (1,)), ((), ())), preferred_element_type=F32)


def nn(a, b):
    return jnp.dot(a, b, preferred_element_type=F32)


MESH = pl.DeviceIdType.MESH
GRP = 512


def copy_to(src, dst, send, recv, dp, ctx):
    return pltpu.make_async_remote_copy(
        src_ref=src, dst_ref=dst, send_sem=send, recv_sem=recv,
        device_id=(dp, ctx), device_id_type=MESH)


def announce(dp, me):
    barrier = pltpu.get_barrier_semaphore()
    targets = [(dp, lax.rem(me + o, 16)) for o in range(1, 16)]
    targets += [(lax.rem(dp + o, 8), me) for o in range(1, 8)]
    for t in targets:
        pl.semaphore_signal(barrier, inc=1, device_id=t, device_id_type=MESH)


def fused_kernel(len_ref, from_ref, qg_ref, kg_ref, q_in, do_in, k_in, v_in,
                 gq_out, gk_ref, gv_ref, gain_ref,
                 q_ref, do_ref, k_ref, v_ref, gq_ref, in_sem, out_sem, kv_ref, qn, qt, dn, dt, kt, w_s, dp_s, m_s, s_s, dq_s, dk_ref, dv_ref, qpart,
                 away, bufa, bufb, bufc, bufl, bufs, sa, sb, sl, tot, gown, gsum, gall, gdp,
                 send_z, recv_z, send_y, recv_y, send_s, recv_s, fsend_l, frecv_l,
                 send_a, recv_a, send_b, recv_b, send_c, recv_c, send_l, recv_l, send_g, recv_g):
    dp = lax.axis_index("dp")
    me = lax.axis_index("ctx")
    z = me // 4
    y = lax.rem(me // 2, 2)
    c = lax.rem(me, 2)
    n = me // 2
    first = me * 4
    sib = me + 1 - 2 * c
    yny = me + 2 - 4 * y
    arriving = [pltpu.make_async_copy(src, dst, in_sem.at[j])
                for j, (src, dst) in enumerate(((k_in, k_ref), (v_in, v_ref), (q_in, q_ref), (do_in, do_ref)))]
    for copy in arriving:
        copy.start()
    kv_ref[PROMPT * BLK:OWN * BLK, :] = jnp.zeros((REACH * BLK, 2 * BLK), BF)
    announce(dp, me)
    arriving[0].wait()
    arriving[1].wait()
    x = k_ref[...].astype(F32)
    r = lax.rsqrt(jnp.mean(x * x, axis=-1, keepdims=True) + 1e-6)
    kv_ref[OWN * BLK:, 0:BLK] = (x * r * kg_ref[...]).astype(BF)
    kv_ref[OWN * BLK:, BLK:2 * BLK] = v_ref[...]

    @pl.when(z == 0)
    def _():
        kv_ref[pl.ds(pl.multiple_of(me * GRP, GRP), GRP), :] = kv_ref[OWN * BLK:, :]

    pl.semaphore_wait(pltpu.get_barrier_semaphore(), 22)
    chain = 2 * y + c
    other = 2 * (1 - y) + c

    def krows(g, h):
        return kv_ref.at[pl.ds(pl.multiple_of(g * GRP + h * BLK, BLK), BLK)]

    def kblocks(first, count):
        return kv_ref.at[pl.ds(first * BLK, count * BLK)]

    def kv_z(h, zz, k):
        return copy_to(krows(chain, h), krows(chain, h), send_z.at[k], recv_z.at[h], dp, zz * 4 + chain)

    def kv_y(h):
        return copy_to(krows(chain, h), krows(chain, h), send_y.at[h], recv_y.at[h], dp, yny)

    def kv_s(j, h):
        g = chain if j == 0 else other
        return copy_to(krows(g, h), krows(g, h), send_s.at[4 * j + h], recv_s.at[4 * j + h], dp, sib)

    has_next = (n >= 2) & (n + 1 <= 7)
    has_prev = n >= 3
    ahead = copy_to(kblocks(OWN, 4),kblocks(PROMPT + 2, 4), fsend_l.at[0], frecv_l.at[0], dp, lax.rem(me + 2, 16))
    own_sib = copy_to(kblocks(OWN, 4),kblocks(PROMPT + 6, 4), fsend_l.at[1], frecv_l.at[1], dp, sib)
    kfar = copy_to(kblocks(OWN + 2, 2),kblocks(PROMPT, 2), fsend_l.at[2], frecv_l.at[2], dp, lax.rem(me + 3, 16))
    relay_full = copy_to(kblocks(PROMPT + 2, 4),kblocks(PROMPT + 6, 4), fsend_l.at[3], frecv_l.at[1], dp, sib)
    relay_half = copy_to(kblocks(PROMPT + 4, 2),kblocks(PROMPT, 2), fsend_l.at[4], frecv_l.at[2], dp, sib)
    sends_kfar = (c == 1) & (n >= 2) & (n + 2 <= 7)
    gets_kfar = (c == 0) & (n >= 4)

    shift = jnp.where(z >= 2, 2, 0)
    pieces = [lax.rem(p + shift, 4) for p in range(4)]

    @pl.when(z == 0)
    def _():
        for p in range(4):
            kv_z(p, 1, 2 * p).start()
            kv_z((p + 2) % 4, 3, 2 * p + 1).start()
        for p in range(4):
            kv_y(p).start()
            kv_s(0, p).start()

    @pl.when((c == 0) & (n >= 2))
    def _():
        own_sib.start()

    @pl.when(has_next)
    def _():
        ahead.start()

    @pl.when(sends_kfar)
    def _():
        kfar.start()

    early = jnp.where(z == 1, 1, 0)
    order = (early, 1 - early)
    sums = (dv_ref, dk_ref)

    def half(h):
        return pl.ds(pl.multiple_of(h * 256, 256), 256)

    def rows(g, h):
        return pl.ds(pl.multiple_of(g * GRP + h * 256, 256), 256)

    def group(g):
        return pl.ds(pl.multiple_of(g * GRP, GRP), GRP)

    def blocks(first, count):
        return pl.ds(first * BLK, count * BLK)

    def cp_a(x, j):
        return copy_to(away.at[x, group(2 * j + 1 - c)], bufa.at[x, j],
                       send_a.at[2 * x + j], recv_a.at[2 * x + j], dp, sib)

    def cp_b(x, h):
        return copy_to(sa.at[x, half(h)], bufb.at[x, half(h)], send_b.at[2 * x + h], recv_b.at[2 * x + h], dp, yny)

    def cp_c(x, h, slot, zz):
        return copy_to(sb.at[x, half(h)], bufc.at[slot, x, half(h)], send_c.at[2 * x + h],
                       recv_c.at[4 * slot + 2 * x + h], dp, zz * 4 + 2 * y + c)

    from_next = (n >= 2) & (n + 1 <= 7)
    sends_near = (c == 1) & (n >= 2)
    gets_near = (c == 0) & (n >= 2)
    sends_far = (c == 0) & (n >= 4)
    gets_far = (c == 1) & (n >= 2) & (n + 2 <= 7)
    two_blocks = pl.ds(0, 2 * BLK)

    def leg(src, dst, k, x, to):
        return copy_to(src, dst, send_l.at[2 * k + x], recv_l.at[2 * k + x], dp, to)

    def hand_full(x):
        return leg(away.at[x, blocks(PROMPT + 6, 4)], bufs.at[x], 0, x, sib)

    def hand_half(x):
        return leg(away.at[x, blocks(PROMPT, 2)], bufs.at[x, two_blocks], 0, x, sib)

    def back(x):
        return leg(sl.at[x], bufl.at[0, x], 1, x, lax.rem(me + 14, 16))

    def near_back(x):
        return leg(away.at[x, blocks(PROMPT + 6, 4)], bufl.at[1, x], 2, x, sib)

    def far_back(x):
        return leg(away.at[x, blocks(PROMPT, 2)], bufl.at[2, x, two_blocks], 3, x, lax.rem(me + 13, 16))

    def hand_over(x, lo, hi):
        def one(s, _):
            rr = pl.ds(pl.multiple_of(s * BLK, BLK), BLK)
            away[x, rr, :] = sums[x][rr, :].astype(BF)
            return 0

        lax.fori_loop(lo, hi, one, 0)

    def local_start(x):
        @pl.when(has_prev & (c == 0))
        def _():
            hand_full(x).start()

        @pl.when(has_prev & (c == 1))
        def _():
            hand_half(x).start()

        @pl.when(sends_near)
        def _():
            near_back(x).start()

        @pl.when(sends_far)
        def _():
            far_back(x).start()

    def local_mid(x):
        @pl.when(has_prev & (c == 1))
        def _():
            hand_full(x).wait_recv()
            sl[x] = (away[x, blocks(PROMPT + 2, 4), :].astype(F32) + bufs[x].astype(F32)).astype(BF)
            back(x).start()

        @pl.when(has_prev & (c == 0))
        def _():
            hand_half(x).wait_recv()
            sl[x, 0:2 * BLK, :] = away[x, blocks(PROMPT + 2, 2), :]
            sl[x, 2 * BLK:, :] = (away[x, blocks(PROMPT + 4, 2), :].astype(F32)
                                  + bufs[x, 0:2 * BLK].astype(F32)).astype(BF)
            back(x).start()

    def local_end(x):
        @pl.when(from_next)
        def _():
            back(x).wait_recv()
            tot[x] += bufl[0, x].astype(F32)

        @pl.when(gets_near)
        def _():
            near_back(x).wait_recv()
            tot[x] += bufl[1, x].astype(F32)

        @pl.when(gets_far)
        def _():
            far_back(x).wait_recv()
            tot[x, 2 * BLK:, :] += bufl[2, x, 0:2 * BLK].astype(F32)

    def stage_b(x):
        cp_a(x, 1 - y).wait_recv()
        for h in order:
            sa[x, half(h), :] = (away[x, rows(2 * (1 - y) + c, h), :].astype(F32)
                                 + bufa[x, 1 - y, half(h), :].astype(F32)).astype(BF)
            cp_b(x, h).start()

    def stage_c(x):
        cp_a(x, y).wait_recv()
        for step, h in enumerate(order):
            tot[x, half(h), :] = (away[x, rows(2 * y + c, h), :].astype(F32)
                                  + bufa[x, y, half(h), :].astype(F32))
            cp_b(x, h).wait_recv()
            tot[x, half(h), :] += bufb[x, half(h), :].astype(F32)

            @pl.when(z == 2)
            def _(h=h):
                sb[x, half(h), :] = tot[x, half(h), :].astype(BF)
                cp_c(x, h, 0, 1 + 2 * h).start()

            if step == 0:
                @pl.when((z == 1) | (z == 3))
                def _(h=h):
                    sb[x, half(h), :] = tot[x, half(h), :].astype(BF)
                    cp_c(x, h, (z - 1) // 2, 0).start()

    def stage_d(x):
        h = 1 - early

        @pl.when((z == 1) | (z == 3))
        def _():
            cp_c(x, h, 0, 0).wait_recv()
            tot[x, half(h), :] += bufc[0, x, half(h), :].astype(F32)
            sb[x, half(h), :] = tot[x, half(h), :].astype(BF)
            cp_c(x, h, (z - 1) // 2, 0).start()

    def stage_e(x):
        own = sums[x][OWN * BLK:, :]

        @pl.when(z != 0)
        def _():
            tot[x] = own

        @pl.when(z == 0)
        def _():
            tot[x] += own
            for h in order:
                for slot in (0, 1):
                    cp_c(x, h, slot, 1).wait_recv()
                    tot[x, half(h), :] += bufc[slot, x, half(h), :].astype(F32)

    dk_ref[...] = jnp.zeros_like(dk_ref)
    dv_ref[...] = jnp.zeros_like(dv_ref)
    m_s[...] = jnp.full_like(m_s, LOW)
    s_s[...] = jnp.zeros_like(s_s)
    qpart[...] = jnp.zeros_like(qpart)
    gain = qg_ref[...]

    def facts(i):
        b = first + i
        start = jnp.int32(PROMPT)
        off = jnp.int32(0)
        live = jnp.int32(BLK)
        for r in range(8):
            n = len_ref[r]
            c = (n + BLK - 1) // BLK
            inside = (b >= start) & (b < start + c)
            off = jnp.where(inside, b - start, off)
            live = jnp.where(inside, jnp.minimum(n - (b - start) * BLK, BLK), live)
            start = start + c
        return b, off, live

    def prep(i, _):
        b, off, live = facts(i)
        src = jnp.int32(0)
        for j in range(4):
            src = jnp.where(from_ref[j] == b, j, src)
        rows = pl.ds(pl.multiple_of(i * BLK, BLK), BLK)
        srcv = jnp.full((BLK, BLK), src, jnp.int32)
        alive = (lax.broadcasted_iota(jnp.int32, (BLK, BLK), 0) < live).astype(F32)
        for h in range(HEADS):
            cols = pl.ds(h * BLK, BLK)
            x = q_ref[rows, cols].astype(F32)
            r = lax.rsqrt(jnp.mean(x * x, axis=-1, keepdims=True) + 1e-6)
            y = (x * r * gain).astype(BF)
            z = do_ref[0:BLK, cols].astype(F32)
            for j in range(1, 4):
                z = jnp.where(srcv == j, do_ref[j * BLK:(j + 1) * BLK, cols].astype(F32), z)
            z = (z * alive).astype(BF)
            t = i * TPB + h // HT
            e = pl.ds((h % HT) * BLK, BLK)
            qn[t, e, :] = y
            qt[t, :, e] = y.T
            dn[t, e, :] = z
            dt[t, :, e] = z.T
        return 0

    arriving[2].wait()
    arriving[3].wait()
    lax.fori_loop(0, 2, prep, 0)
    @pl.when(z != 0)
    def _():
        for p in range(4):
            h = pieces[p]
            kv_z(h, 0, 0).wait_recv()
            if p < 2:
                @pl.when(z != 2)
                def _():
                    kv_z(h, 2, p).start()
            kv_y(h).start()
            kv_s(0, h).start()

    lax.fori_loop(2, 4, prep, 0)
    @pl.when(has_prev)
    def _():
        ahead.wait_recv()

    @pl.when(has_prev & (c == 1))
    def _():
        relay_full.start()

    @pl.when(has_prev & (c == 0))
    def _():
        relay_half.start()

    def chain_arrive():
        g = 2 * y + 1 - c
        for h in pieces:
            copy_to(krows(g, h), krows(g, h), send_s.at[h], recv_s.at[h], dp, sib).wait_recv()

    def rest_arrive():
        for h in pieces:
            copy_to(krows(other, h), krows(other, h), send_y.at[h], recv_y.at[h], dp, yny).wait_recv()
            kv_s(1, h).start()
        g = 2 * (1 - y) + 1 - c
        for h in pieces:
            copy_to(krows(g, h), krows(g, h), send_s.at[4 + h], recv_s.at[4 + h], dp, sib).wait_recv()
        lax.fori_loop(0, PROMPT, slot_t, 0)

    def slot_t(s, _):
        kt[s] = kv_ref[pl.ds(pl.multiple_of(s * BLK, BLK), BLK), 0:BLK].T
        return 0

    lax.fori_loop(OWN, SLOTS, slot_t, 0)

    def local_arrive():
        @pl.when(((c == 1) & (n >= 2)) | ((c == 0) & has_prev))
        def _():
            own_sib.wait_recv()

        @pl.when(gets_kfar | ((c == 1) & has_prev))
        def _():
            kfar.wait_recv()

        lax.fori_loop(PROMPT, OWN, slot_t, 0)

    def per_block(i, _):
        b, off, live = facts(i)
        n_prompt = jnp.minimum(b, PROMPT)
        pc = (n_prompt + CBP - 1) // CBP
        whole = jnp.minimum(n_prompt, 1)
        keyi = lax.broadcasted_iota(jnp.int32, (BLK, RT), 0)
        toki = lax.rem(lax.broadcasted_iota(jnp.int32, (BLK, RT), 1), BLK)
        bias = jnp.where((keyi <= toki) & (keyi < live), 0.0, LOW)

        offv = jnp.full((8, CS), off, jnp.int32)

        def seen(pos):
            prompt = pos < PROMPT
            spare = jnp.where(prompt, n_prompt - 1 - pos, pos - PROMPT - REACH)
            return spare + offv * jnp.where(prompt, 0, 1) >= 0

        def per_tile(g, _):
            t = i * TPB + g

            def row0(pos):
                return pl.multiple_of(jnp.where(pos < PROMPT, pos, pos + i) * BLK, BLK)

            def first_pass(pos, nb, diag):
                r0 = row0(pos)
                kc = kv_ref[pl.ds(r0, nb * BLK), 0:BLK]
                for x in range(0, RT, CS):
                    cs = slice(x, x + CS)
                    s = nn(kc, qt[t, :, cs])
                    for u in range(nb):
                        for q in range(NG):
                            lo = u * BLK + q * MG
                            su = s[lo:lo + MG]
                            own = diag and u == nb - 1
                            if own:
                                su = su + bias[q * MG:(q + 1) * MG, cs]
                            su = su.reshape(MG // 8, 8, CS)
                            m = jnp.max(su, axis=0) * SL2
                            w = jnp.exp2(su * SL2 - m[None])
                            s_s[(pos + u) * NG + q, :, cs] = jnp.sum(w, axis=0)
                            if own:
                                m_s[(pos + u) * NG + q, :, cs] = m
                            else:
                                m_s[(pos + u) * NG + q, :, cs] = jnp.where(seen(pos + u), m, LOW)
                            w_s[pos + u, q * MG:(q + 1) * MG, cs] = w.reshape(MG, CS)

            def local(body, init):
                return body(PROMPT, REACH + 1, True, init)

            def over(body, init):
                return local(body, lax.fori_loop(0, whole, lambda c, x: body(0, PROMPT, False, x), init))

            def p1(pos, nb, diag, x):
                first_pass(pos, nb, diag)
                return x

            @pl.when(i == 0)
            def _():
                local_arrive()
                local(p1, 0)
                chain_arrive()
                lax.fori_loop(0, whole, lambda c, x: p1(y * CBP, CBP, False, x), 0)
                rest_arrive()
                lax.fori_loop(0, whole, lambda c, x: p1((1 - y) * CBP, CBP, False, x), 0)

            @pl.when(i > 0)
            def _():
                over(p1, 0)

            m = m_s[...]
            top = jnp.max(jnp.max(m, axis=0), axis=0, keepdims=True)
            f = jnp.exp2(m - top[None])
            tot = jnp.sum(jnp.sum(f * s_s[...], axis=0), axis=0, keepdims=True)
            m_s[...] = f * (1.0 / tot)[None]

            drows = dn[t]
            def p3(pos, nb, diag, acc):
                r0 = row0(pos)
                vc = kv_ref[pl.ds(r0, nb * BLK), BLK:2 * BLK]
                accs, ps = [], []
                for x in range(0, RT, CS):
                    cs = slice(x, x + CS)
                    dp = nn(vc, dt[t, :, cs])
                    a = acc[:, cs]
                    pu = []
                    for u in range(nb):
                        du = dp[u * BLK:(u + 1) * BLK]
                        parts = []
                        for q in range(NG):
                            wq = w_s[pos + u, q * MG:(q + 1) * MG, cs].reshape(MG // 8, 8, CS)
                            parts.append((wq * m_s[(pos + u) * NG + q, :, cs][None]).reshape(MG, CS))
                        ch = jnp.concatenate(parts, axis=0)
                        chb = ch.astype(BF)
                        w_s[pos + u, :, cs] = ch
                        dp_s[pos + u, :, cs] = du
                        a = a + jnp.sum((chb.astype(F32) * du).reshape(BLK // 8, 8, CS), axis=0)
                        pu.append(chb)
                    accs.append(a)
                    ps.append(jnp.concatenate(pu, axis=0))
                p = jnp.concatenate(ps, axis=1)
                rows = pl.ds(r0, nb * BLK)
                dv_ref[rows, :] += nn(p, drows)
                return jnp.concatenate(accs, axis=1)

            delta = over(p3, jnp.zeros((8, RT), F32))
            @pl.when(i == 3)
            def _():
                hand_over(0, 0, OWN)
                for j in (0, 1):
                    cp_a(0, j).start()
                local_start(0)

            delta = jnp.sum(delta, axis=0, keepdims=True)
            qrows = qn[t]

            def key_side(pos, nb, keep):
                rr = pl.ds(row0(pos), nb * BLK)
                dss = []
                for u in range(nb):
                    ds = (w_s[pos + u] * (dp_s[pos + u] - delta)).astype(BF)
                    if keep:
                        w_s[pos + u] = ds.astype(F32)
                    dss.append(ds)
                ds = jnp.concatenate(dss, axis=0) if nb > 1 else dss[0]
                dk_ref[rr, :] += nn(ds, qrows)
                return ds

            def query_side(pos, nb, ds):
                slot = row0(pos) // BLK
                ktc = jnp.concatenate([kt[slot + u] for u in range(nb)], axis=1) if nb > 1 else kt[slot]
                dq_s[i] += nn(ktc, ds)

            def p4(pos, nb, diag, dq):
                query_side(pos, nb, key_side(pos, nb, False))
                return dq

            def p4_keys(pos, nb, diag, dq):
                key_side(pos, nb, True)
                return dq

            def p4_queries(pos, nb, diag, dq):
                parts = [w_s[pos + u].astype(BF) for u in range(nb)]
                query_side(pos, nb, jnp.concatenate(parts, axis=0) if nb > 1 else parts[0])
                return dq

            dq_s[i] = jnp.zeros((BLK, RT), F32)

            @pl.when(i < 3)
            def _():
                lax.fori_loop(0, pc, lambda c, x: p4(c * CBP, CBP, False, x), 0)
                local(p4, 0)

            @pl.when(i == 3)
            def _():
                for j in (0, 1):
                    @pl.when(j < pc)
                    def _(j=j):
                        p4_keys(j * CBP, CBP, False, 0)

                    hand_over(1, 8 * j, 8 * j + 8)
                    cp_a(1, j).start()
                stage_b(0)
                local(p4_keys, 0)
                hand_over(1, PROMPT, OWN)
                stage_b(1)
                local_start(1)
                lax.fori_loop(0, pc, lambda c, x: p4_queries(c * CBP, CBP, False, x), 0)
                local(p4_queries, 0)

            return 0

        lax.fori_loop(0, TPB, per_tile, 0)
        return 0

    lax.fori_loop(0, 4, per_block, 0)

    def finish(i, _):
        dqt = dq_s[i]
        dq = dqt.T * SCALE
        rows = pl.ds(pl.multiple_of(i * BLK, BLK), BLK)
        part = jnp.zeros((8, BLK), F32)
        for u in range(HT):
            cols = pl.ds(pl.multiple_of(u * BLK, BLK), BLK)
            x = q_ref[rows, cols].astype(F32)
            r = lax.rsqrt(jnp.mean(x * x, axis=-1, keepdims=True) + 1e-6)
            unit = x * r
            dqu = dq[u * BLK:(u + 1) * BLK]
            both = dqu * unit
            part = part + jnp.sum(both.reshape(BLK // 8, 8, BLK), axis=0)
            mean = jnp.mean(both * gain, axis=-1, keepdims=True)
            gq_ref[rows, cols] = (r * (dqu * gain - unit * mean)).astype(BF)
        qpart[...] += part
        return 0

    lax.fori_loop(0, 4, finish, 0)
    leaving = pltpu.make_async_copy(gq_ref, gq_out, out_sem.at[0])
    leaving.start()

    def key_part(k, acc):
        rr = pl.ds(pl.multiple_of(k * BLK, BLK), BLK)
        both = dk_ref[rr, :] * kv_ref[rr, 0:BLK].astype(F32)
        return acc + jnp.sum(both.reshape(BLK // 8, 8, BLK), axis=0)

    kpart = lax.fori_loop(0, SLOTS, key_part, jnp.zeros((8, BLK), F32))
    kgain = kg_ref[...]
    gown[...] = jnp.zeros_like(gown)
    gown[0:1, :] = jnp.sum(qpart[...], axis=0, keepdims=True)
    gown[1:2, :] = jnp.sum(kpart, axis=0, keepdims=True) * SCALE / kgain
    cg = [copy_to(gown, gall.at[me], send_g.at[o - 1], recv_g.at[me], dp, lax.rem(me + o, 16)) for o in range(1, 16)]
    ch = [copy_to(gsum, gdp.at[dp], send_g.at[14 + o], recv_g.at[16 + dp], lax.rem(dp + o, 8), me) for o in range(1, 8)]
    for q in cg:
        q.start()
    gall[me] = gown[...]
    for x in (0, 1):
        for h in (0, 1):
            cp_b(x, h).wait_send()
        local_mid(x)
    stage_c(0)
    stage_c(1)
    for o in range(1, 16):
        p = lax.rem(me + o, 16)
        copy_to(gown, gall.at[p], send_g.at[o - 1], recv_g.at[p], dp, p).wait_recv()
    total = gall[0]
    for o in range(1, 16):
        total = total + gall[o]
    gsum[...] = total
    for q in ch:
        q.start()
    gdp[dp] = total
    stage_d(0)
    stage_d(1)
    stage_e(0)
    local_end(0)
    gv_ref[...] = tot[0].astype(BF)
    stage_e(1)
    local_end(1)
    x = k_ref[...].astype(F32)
    r = lax.rsqrt(jnp.mean(x * x, axis=-1, keepdims=True) + 1e-6)
    unit = x * r
    dk = tot[1] * SCALE
    mean = jnp.mean(dk * unit * kgain, axis=-1, keepdims=True)
    gk_ref[...] = (r * (dk * kgain - unit * mean)).astype(BF)
    for o in range(1, 8):
        p = lax.rem(dp + o, 8)
        copy_to(gsum, gdp.at[p], send_g.at[14 + o], recv_g.at[16 + p], p, me).wait_recv()
    total = gdp[0]
    for o in range(1, 8):
        total = total + gdp[o]
    gain_ref[...] = total
    for q in cg + ch:
        q.wait_send()
    leaving.wait()
    for x in (0, 1):
        for h in (0, 1):
            cp_a(x, h).wait_send()

        @pl.when(z != 0)
        def _(x=x):
            for h in (0, 1):
                cp_c(x, h, 0, 0).wait_send()

        @pl.when(has_prev & (c == 0))
        def _(x=x):
            hand_full(x).wait_send()

        @pl.when(has_prev & (c == 1))
        def _(x=x):
            hand_half(x).wait_send()

        @pl.when(has_prev)
        def _(x=x):
            back(x).wait_send()

        @pl.when(sends_near)
        def _(x=x):
            near_back(x).wait_send()

        @pl.when(sends_far)
        def _(x=x):
            far_back(x).wait_send()

    @pl.when(z == 0)
    def _():
        for k in range(8):
            kv_z(0, 1, k).wait_send()

    @pl.when((z == 1) | (z == 3))
    def _():
        for k in range(2):
            kv_z(0, 1, k).wait_send()

    for h in range(4):
        kv_y(h).wait_send()
        kv_s(0, h).wait_send()
        kv_s(1, h).wait_send()

    @pl.when((c == 0) & (n >= 2))
    def _():
        own_sib.wait_send()

    @pl.when(has_next)
    def _():
        ahead.wait_send()

    @pl.when(sends_kfar)
    def _():
        kfar.wait_send()

    @pl.when(has_prev & (c == 1))
    def _():
        relay_full.wait_send()

    @pl.when(has_prev & (c == 0))
    def _():
        relay_half.wait_send()


def fused(lens, frm, qg, kg, q, do, k, v):
    dma = pltpu.SemaphoreType.DMA
    rows = SLOTS * BLK
    tiles = 4096 // RT
    pair = pltpu.VMEM((2, GRP, BLK), BF)
    anywhere = pl.BlockSpec(memory_space=pl.ANY)
    wide, narrow = pltpu.VMEM((GRP, 8 * BLK), BF), pltpu.VMEM((GRP, BLK), BF)
    two = pltpu.VMEM((2, 2, GRP, BLK), BF)
    return pl.pallas_call(
        fused_kernel,
        out_shape=(
            jax.ShapeDtypeStruct((512, 1024), BF),
            jax.ShapeDtypeStruct((GRP, BLK), BF),
            jax.ShapeDtypeStruct((GRP, BLK), BF),
            jax.ShapeDtypeStruct((8, BLK), F32),
        ),
        in_specs=[SM, SM, VM, VM] + [anywhere] * 4,
        out_specs=(anywhere, VM, VM, VM),
        scratch_shapes=[
            wide, wide, narrow, narrow, wide, dma((4,)), dma((1,)),
            pltpu.VMEM((rows, 2 * BLK), BF),
            pltpu.VMEM((tiles, RT, BLK), BF),
            pltpu.VMEM((tiles, BLK, RT), BF),
            pltpu.VMEM((tiles, RT, BLK), BF),
            pltpu.VMEM((tiles, BLK, RT), BF),
            pltpu.VMEM((SLOTS, BLK, BLK), BF),
            pltpu.VMEM((POS, BLK, RT), F32),
            pltpu.VMEM((POS, BLK, RT), F32),
            pltpu.VMEM((POS * NG, 8, RT), F32),
            pltpu.VMEM((POS * NG, 8, RT), F32),
            pltpu.VMEM((tiles, BLK, RT), F32),
            pltpu.VMEM((rows, BLK), F32),
            pltpu.VMEM((rows, BLK), F32),
            pltpu.VMEM((8, BLK), F32),
            pltpu.VMEM((2, OWN * BLK, BLK), BF),
            two, pair, two, pltpu.VMEM((3, 2, GRP, BLK), BF), pair, pair, pair, pair,
            pltpu.VMEM((2, GRP, BLK), F32),
            pltpu.VMEM((8, BLK), F32),
            pltpu.VMEM((8, BLK), F32),
            pltpu.VMEM((16, 8, BLK), F32),
            pltpu.VMEM((8, 8, BLK), F32),
        ] + [dma((m,)) for m in (8, 4, 4, 4, 8, 8, 5, 3, 4, 4, 4, 4, 4, 8, 8, 8, 22, 24)],
        compiler_params=pltpu.CompilerParams(
            collective_id=0, has_side_effects=True, vmem_limit_bytes=62 * 1024 * 1024),
    )(lens, frm, qg, kg, q, do, k, v)


PIECES = 4


def hand_out_kernel(gains_ref, gq_ref, gk_ref, gv_ref, oq_ref, ok_ref, ov_ref, gq_gain_ref, gk_gain_ref,
                    bq, bk, bv, sin, sout):
    step = bq.shape[0] // PIECES
    legs = [(gq_ref.at[pl.ds(j * step, step)], bq.at[pl.ds(j * step, step)], oq_ref.at[pl.ds(j * step, step)])
            for j in range(PIECES)]
    legs += [(gk_ref, bk, ok_ref), (gv_ref, bv, ov_ref)]
    into = [pltpu.make_async_copy(x, m, sin.at[j]) for j, (x, m, _) in enumerate(legs)]
    out = [pltpu.make_async_copy(m, o, sout.at[j]) for j, (_, m, o) in enumerate(legs)]
    for copy in into:
        copy.start()
    gq_gain_ref[...] = gains_ref[0, :]
    gk_gain_ref[...] = gains_ref[1, :]
    for j in range(len(legs)):
        into[j].wait()
        out[j].start()
    for copy in out:
        copy.wait()


def hand_out(gains, gq, gk, gv):
    anywhere = pl.BlockSpec(memory_space=pl.ANY)
    flat = jax.ShapeDtypeStruct((BLK,), F32)
    dma = pltpu.SemaphoreType.DMA
    return pl.pallas_call(
        hand_out_kernel,
        out_shape=tuple(jax.ShapeDtypeStruct(t.shape, t.dtype) for t in (gq, gk, gv)) + (flat, flat),
        in_specs=[VM, anywhere, anywhere, anywhere],
        out_specs=(anywhere, anywhere, anywhere, VM, VM),
        scratch_shapes=[pltpu.VMEM(t.shape, t.dtype) for t in (gq, gk, gv)] + [dma((PIECES + 2,)), dma((PIECES + 2,))],
    )(gains, gq, gk, gv)


def body(q_raw, k_raw, values, d_out, q_gain, k_gain, resp_len, block_parent, block_from):
    gq, gk, gv, gains = fused(resp_len[0], block_from[0], q_gain.reshape(1, BLK), k_gain.reshape(1, BLK),
                              q_raw[0], d_out[0], k_raw[0], values[0])
    gq, gk, gv, q_gain_grad, k_gain_grad = hand_out(gains, gq, gk, gv)
    return gq[None], gk[None], gv[None], q_gain_grad, k_gain_grad


def solution(mesh):
    tok = P("dp", "ctx", None)
    return jax.shard_map(
        body,
        mesh=mesh,
        in_specs=(tok, tok, tok, tok, P(), P(), P("dp", None), P("dp", None), P("dp", "ctx")),
        out_specs=(tok, tok, tok, P(), P()),
        check_vma=False,
    )
```

```python
import functools, math
import jax, jax.numpy as jnp
from jax import lax
from jax.experimental import pallas as pl
from jax.experimental.pallas import tpu as pltpu
from jax.sharding import PartitionSpec as P

BLK = 128
HEADS = 8
PROMPT = 16
REACH = 10
SLOTS = 30
OWN = PROMPT + REACH
POS = 27
RT = 1024
CBP = 8
MG = 64
NG = BLK // MG
HT = RT // BLK
CS = 256
TPB = HEADS // HT
LOW = -1e30
F32 = jnp.float32
BF = jnp.bfloat16
SCALE = 1.0 / math.sqrt(128.0)
LOG2E = 1.4426950408889634
SL2 = SCALE * LOG2E
VM = pl.BlockSpec(memory_space=pltpu.VMEM)
SM = pl.BlockSpec(memory_space=pltpu.SMEM)


def nt(a, b):
    return lax.dot_general(a, b, (((1,), (1,)), ((), ())), preferred_element_type=F32)


def nn(a, b):
    return jnp.dot(a, b, preferred_element_type=F32)


MESH = pl.DeviceIdType.MESH
GRP = 512


def copy_to(src, dst, send, recv, dp, ctx):
    return pltpu.make_async_remote_copy(
        src_ref=src, dst_ref=dst, send_sem=send, recv_sem=recv,
        device_id=(dp, ctx), device_id_type=MESH)


def announce(dp, me):
    barrier = pltpu.get_barrier_semaphore()
    targets = [(dp, lax.rem(me + o, 16)) for o in range(1, 16)]
    targets += [(lax.rem(dp + o, 8), me) for o in range(1, 8)]
    for t in targets:
        pl.semaphore_signal(barrier, inc=1, device_id=t, device_id_type=MESH)


def fused_kernel(len_ref, from_ref, qg_ref, kg_ref, q_in, do_in, k_in, v_in,
                 gq_out, gk_ref, gv_ref, gain_ref,
                 q_ref, do_ref, k_ref, v_ref, gq_ref, in_sem, out_sem, kv_ref, qn, qt, dn, dt, kt, w_s, dp_s, m_s, s_s, dl_s, dq_s, dk_ref, dv_ref, qpart,
                 away, bufa, bufb, bufc, bufl, bufs, sa, sb, sl, tot, gown, gsum, gall, gdp,
                 send_z, recv_z, send_y, recv_y, send_s, recv_s, fsend_l, frecv_l,
                 send_a, recv_a, send_b, recv_b, send_c, recv_c, send_l, recv_l, send_g, recv_g):
    dp = lax.axis_index("dp")
    me = lax.axis_index("ctx")
    z = me // 4
    y = lax.rem(me // 2, 2)
    c = lax.rem(me, 2)
    n = me // 2
    first = me * 4
    sib = me + 1 - 2 * c
    yny = me + 2 - 4 * y
    arriving = [pltpu.make_async_copy(src, dst, in_sem.at[j])
                for j, (src, dst) in enumerate(((k_in, k_ref), (v_in, v_ref), (q_in, q_ref), (do_in, do_ref)))]
    for copy in arriving:
        copy.start()
    kv_ref[PROMPT * BLK:OWN * BLK, :] = jnp.zeros((REACH * BLK, 2 * BLK), BF)
    announce(dp, me)
    arriving[0].wait()
    arriving[1].wait()
    x = k_ref[...].astype(F32)
    r = lax.rsqrt(jnp.mean(x * x, axis=-1, keepdims=True) + 1e-6)
    kv_ref[OWN * BLK:, 0:BLK] = (x * r * kg_ref[...]).astype(BF)
    kv_ref[OWN * BLK:, BLK:2 * BLK] = v_ref[...]

    @pl.when(z == 0)
    def _():
        kv_ref[pl.ds(pl.multiple_of(me * GRP, GRP), GRP), :] = kv_ref[OWN * BLK:, :]

    pl.semaphore_wait(pltpu.get_barrier_semaphore(), 22)
    chain = 2 * y + c
    other = 2 * (1 - y) + c

    def krows(g, h):
        return kv_ref.at[pl.ds(pl.multiple_of(g * GRP + h * BLK, BLK), BLK)]

    def kblocks(first, count):
        return kv_ref.at[pl.ds(first * BLK, count * BLK)]

    def kv_z(h, zz, k):
        return copy_to(krows(chain, h), krows(chain, h), send_z.at[k], recv_z.at[h], dp, zz * 4 + chain)

    def kv_y(h):
        return copy_to(krows(chain, h), krows(chain, h), send_y.at[h], recv_y.at[h], dp, yny)

    def kv_s(j, h):
        g = chain if j == 0 else other
        return copy_to(krows(g, h), krows(g, h), send_s.at[4 * j + h], recv_s.at[4 * j + h], dp, sib)

    has_next = (n >= 2) & (n + 1 <= 7)
    has_prev = n >= 3
    ahead = copy_to(kblocks(OWN, 4),kblocks(PROMPT + 2, 4), fsend_l.at[0], frecv_l.at[0], dp, lax.rem(me + 2, 16))
    own_sib = copy_to(kblocks(OWN, 4),kblocks(PROMPT + 6, 4), fsend_l.at[1], frecv_l.at[1], dp, sib)
    kfar = copy_to(kblocks(OWN + 2, 2),kblocks(PROMPT, 2), fsend_l.at[2], frecv_l.at[2], dp, lax.rem(me + 3, 16))
    relay_full = copy_to(kblocks(PROMPT + 2, 4),kblocks(PROMPT + 6, 4), fsend_l.at[3], frecv_l.at[1], dp, sib)
    relay_half = copy_to(kblocks(PROMPT + 4, 2),kblocks(PROMPT, 2), fsend_l.at[4], frecv_l.at[2], dp, sib)
    sends_kfar = (c == 1) & (n >= 2) & (n + 2 <= 7)
    gets_kfar = (c == 0) & (n >= 4)

    shift = jnp.where(z >= 2, 2, 0)
    pieces = [lax.rem(p + shift, 4) for p in range(4)]

    @pl.when(z == 0)
    def _():
        for p in range(4):
            kv_z(p, 1, 2 * p).start()
            kv_z((p + 2) % 4, 3, 2 * p + 1).start()
        for p in range(4):
            kv_y(p).start()
            kv_s(0, p).start()

    @pl.when((c == 0) & (n >= 2))
    def _():
        own_sib.start()

    @pl.when(has_next)
    def _():
        ahead.start()

    @pl.when(sends_kfar)
    def _():
        kfar.start()

    early = jnp.where(z == 1, 1, 0)
    order = (early, 1 - early)
    sums = (dv_ref, dk_ref)

    def half(h):
        return pl.ds(pl.multiple_of(h * 256, 256), 256)

    def rows(g, h):
        return pl.ds(pl.multiple_of(g * GRP + h * 256, 256), 256)

    def group(g):
        return pl.ds(pl.multiple_of(g * GRP, GRP), GRP)

    def blocks(first, count):
        return pl.ds(first * BLK, count * BLK)

    def cp_a(x, j):
        return copy_to(away.at[x, group(2 * j + 1 - c)], bufa.at[x, j],
                       send_a.at[2 * x + j], recv_a.at[2 * x + j], dp, sib)

    def cp_b(x, h):
        return copy_to(sa.at[x, half(h)], bufb.at[x, half(h)], send_b.at[2 * x + h], recv_b.at[2 * x + h], dp, yny)

    def cp_c(x, h, slot, zz):
        return copy_to(sb.at[x, half(h)], bufc.at[slot, x, half(h)], send_c.at[2 * x + h],
                       recv_c.at[4 * slot + 2 * x + h], dp, zz * 4 + 2 * y + c)

    from_next = (n >= 2) & (n + 1 <= 7)
    sends_near = (c == 1) & (n >= 2)
    gets_near = (c == 0) & (n >= 2)
    sends_far = (c == 0) & (n >= 4)
    gets_far = (c == 1) & (n >= 2) & (n + 2 <= 7)
    two_blocks = pl.ds(0, 2 * BLK)

    def leg(src, dst, k, x, to):
        return copy_to(src, dst, send_l.at[2 * k + x], recv_l.at[2 * k + x], dp, to)

    def hand_full(x):
        return leg(away.at[x, blocks(PROMPT + 6, 4)], bufs.at[x], 0, x, sib)

    def hand_half(x):
        return leg(away.at[x, blocks(PROMPT, 2)], bufs.at[x, two_blocks], 0, x, sib)

    def back(x):
        return leg(sl.at[x], bufl.at[0, x], 1, x, lax.rem(me + 14, 16))

    def near_back(x):
        return leg(away.at[x, blocks(PROMPT + 6, 4)], bufl.at[1, x], 2, x, sib)

    def far_back(x):
        return leg(away.at[x, blocks(PROMPT, 2)], bufl.at[2, x, two_blocks], 3, x, lax.rem(me + 13, 16))

    def hand_over(x, lo, hi):
        def one(s, _):
            rr = pl.ds(pl.multiple_of(s * BLK, BLK), BLK)
            away[x, rr, :] = sums[x][rr, :].astype(BF)
            return 0

        lax.fori_loop(lo, hi, one, 0)

    def local_start(x):
        @pl.when(has_prev & (c == 0))
        def _():
            hand_full(x).start()

        @pl.when(has_prev & (c == 1))
        def _():
            hand_half(x).start()

        @pl.when(sends_near)
        def _():
            near_back(x).start()

        @pl.when(sends_far)
        def _():
            far_back(x).start()

    def local_mid(x):
        @pl.when(has_prev & (c == 1))
        def _():
            hand_full(x).wait_recv()
            sl[x] = (away[x, blocks(PROMPT + 2, 4), :].astype(F32) + bufs[x].astype(F32)).astype(BF)
            back(x).start()

        @pl.when(has_prev & (c == 0))
        def _():
            hand_half(x).wait_recv()
            sl[x, 0:2 * BLK, :] = away[x, blocks(PROMPT + 2, 2), :]
            sl[x, 2 * BLK:, :] = (away[x, blocks(PROMPT + 4, 2), :].astype(F32)
                                  + bufs[x, 0:2 * BLK].astype(F32)).astype(BF)
            back(x).start()

    def local_end(x):
        @pl.when(from_next)
        def _():
            back(x).wait_recv()
            tot[x] += bufl[0, x].astype(F32)

        @pl.when(gets_near)
        def _():
            near_back(x).wait_recv()
            tot[x] += bufl[1, x].astype(F32)

        @pl.when(gets_far)
        def _():
            far_back(x).wait_recv()
            tot[x, 2 * BLK:, :] += bufl[2, x, 0:2 * BLK].astype(F32)

    def stage_b(x):
        cp_a(x, 1 - y).wait_recv()
        for h in order:
            sa[x, half(h), :] = (away[x, rows(2 * (1 - y) + c, h), :].astype(F32)
                                 + bufa[x, 1 - y, half(h), :].astype(F32)).astype(BF)
            cp_b(x, h).start()

    def stage_c(x):
        cp_a(x, y).wait_recv()
        for step, h in enumerate(order):
            tot[x, half(h), :] = (away[x, rows(2 * y + c, h), :].astype(F32)
                                  + bufa[x, y, half(h), :].astype(F32))
            cp_b(x, h).wait_recv()
            tot[x, half(h), :] += bufb[x, half(h), :].astype(F32)

            @pl.when(z == 2)
            def _(h=h):
                sb[x, half(h), :] = tot[x, half(h), :].astype(BF)
                cp_c(x, h, 0, 1 + 2 * h).start()

            if step == 0:
                @pl.when((z == 1) | (z == 3))
                def _(h=h):
                    sb[x, half(h), :] = tot[x, half(h), :].astype(BF)
                    cp_c(x, h, (z - 1) // 2, 0).start()

    def stage_d(x):
        h = 1 - early

        @pl.when((z == 1) | (z == 3))
        def _():
            cp_c(x, h, 0, 0).wait_recv()
            tot[x, half(h), :] += bufc[0, x, half(h), :].astype(F32)
            sb[x, half(h), :] = tot[x, half(h), :].astype(BF)
            cp_c(x, h, (z - 1) // 2, 0).start()

    def stage_e(x):
        own = sums[x][OWN * BLK:, :]

        @pl.when(z != 0)
        def _():
            tot[x] = own

        @pl.when(z == 0)
        def _():
            tot[x] += own
            for h in order:
                for slot in (0, 1):
                    cp_c(x, h, slot, 1).wait_recv()
                    tot[x, half(h), :] += bufc[slot, x, half(h), :].astype(F32)

    dk_ref[...] = jnp.zeros_like(dk_ref)
    dv_ref[...] = jnp.zeros_like(dv_ref)
    m_s[...] = jnp.full_like(m_s, LOW)
    s_s[...] = jnp.zeros_like(s_s)
    qpart[...] = jnp.zeros_like(qpart)
    gain = qg_ref[...]

    def facts(i):
        b = first + i
        start = jnp.int32(PROMPT)
        off = jnp.int32(0)
        live = jnp.int32(BLK)
        for r in range(8):
            n = len_ref[r]
            c = (n + BLK - 1) // BLK
            inside = (b >= start) & (b < start + c)
            off = jnp.where(inside, b - start, off)
            live = jnp.where(inside, jnp.minimum(n - (b - start) * BLK, BLK), live)
            start = start + c
        return b, off, live

    def prep(i, _):
        b, off, live = facts(i)
        src = jnp.int32(0)
        for j in range(4):
            src = jnp.where(from_ref[j] == b, j, src)
        rows = pl.ds(pl.multiple_of(i * BLK, BLK), BLK)
        srcv = jnp.full((BLK, BLK), src, jnp.int32)
        alive = (lax.broadcasted_iota(jnp.int32, (BLK, BLK), 0) < live).astype(F32)
        for h in range(HEADS):
            cols = pl.ds(h * BLK, BLK)
            x = q_ref[rows, cols].astype(F32)
            r = lax.rsqrt(jnp.mean(x * x, axis=-1, keepdims=True) + 1e-6)
            y = (x * r * gain).astype(BF)
            z = do_ref[0:BLK, cols].astype(F32)
            for j in range(1, 4):
                z = jnp.where(srcv == j, do_ref[j * BLK:(j + 1) * BLK, cols].astype(F32), z)
            z = (z * alive).astype(BF)
            t = i * TPB + h // HT
            e = pl.ds((h % HT) * BLK, BLK)
            qn[t, e, :] = y
            qt[t, :, e] = y.T
            dn[t, e, :] = z
            dt[t, :, e] = z.T
        return 0

    arriving[2].wait()
    arriving[3].wait()
    lax.fori_loop(0, 2, prep, 0)
    @pl.when(z != 0)
    def _():
        for p in range(4):
            h = pieces[p]
            kv_z(h, 0, 0).wait_recv()
            if p < 2:
                @pl.when(z != 2)
                def _():
                    kv_z(h, 2, p).start()
            kv_y(h).start()
            kv_s(0, h).start()

    lax.fori_loop(2, 4, prep, 0)
    @pl.when(has_prev)
    def _():
        ahead.wait_recv()

    @pl.when(has_prev & (c == 1))
    def _():
        relay_full.start()

    @pl.when(has_prev & (c == 0))
    def _():
        relay_half.start()

    def chain_arrive():
        g = 2 * y + 1 - c
        for h in pieces:
            copy_to(krows(g, h), krows(g, h), send_s.at[h], recv_s.at[h], dp, sib).wait_recv()

    def rest_arrive():
        for h in pieces:
            copy_to(krows(other, h), krows(other, h), send_y.at[h], recv_y.at[h], dp, yny).wait_recv()
            kv_s(1, h).start()
        g = 2 * (1 - y) + 1 - c
        for h in pieces:
            copy_to(krows(g, h), krows(g, h), send_s.at[4 + h], recv_s.at[4 + h], dp, sib).wait_recv()
        lax.fori_loop(0, PROMPT, slot_t, 0)

    def slot_t(s, _):
        kt[s] = kv_ref[pl.ds(pl.multiple_of(s * BLK, BLK), BLK), 0:BLK].T
        return 0

    lax.fori_loop(OWN, SLOTS, slot_t, 0)

    def local_arrive():
        @pl.when(((c == 1) & (n >= 2)) | ((c == 0) & has_prev))
        def _():
            own_sib.wait_recv()

        @pl.when(gets_kfar | ((c == 1) & has_prev))
        def _():
            kfar.wait_recv()

        lax.fori_loop(PROMPT, OWN, slot_t, 0)

    def per_block(i, _):
        b, off, live = facts(i)
        n_prompt = jnp.minimum(b, PROMPT)
        pc = (n_prompt + CBP - 1) // CBP
        whole = jnp.minimum(n_prompt, 1)
        keyi = lax.broadcasted_iota(jnp.int32, (BLK, RT), 0)
        toki = lax.rem(lax.broadcasted_iota(jnp.int32, (BLK, RT), 1), BLK)
        bias = jnp.where((keyi <= toki) & (keyi < live), 0.0, LOW)

        offv = jnp.full((8, CS), off, jnp.int32)

        def seen(pos):
            prompt = pos < PROMPT
            spare = jnp.where(prompt, n_prompt - 1 - pos, pos - PROMPT - REACH)
            return spare + offv * jnp.where(prompt, 0, 1) >= 0

        def per_tile(g, _):
            t = i * TPB + g

            def row0(pos):
                return pl.multiple_of(jnp.where(pos < PROMPT, pos, pos + i) * BLK, BLK)

            def first_pass(pos, nb, diag, ahead_dp):
                r0 = row0(pos)
                kc = kv_ref[pl.ds(r0, nb * BLK), 0:BLK]
                vc = kv_ref[pl.ds(r0, nb * BLK), BLK:2 * BLK]
                for x in range(0, RT, CS):
                    cs = slice(x, x + CS)
                    s = nn(kc, qt[t, :, cs])
                    if ahead_dp:
                        dp_s[pl.ds(pos, nb), :, cs] = nn(vc, dt[t, :, cs]).reshape(nb, BLK, CS)
                    for u in range(nb):
                        for q in range(NG):
                            lo = u * BLK + q * MG
                            su = s[lo:lo + MG]
                            own = diag and u == nb - 1
                            if own:
                                su = su + bias[q * MG:(q + 1) * MG, cs]
                            su = su.reshape(MG // 8, 8, CS)
                            m = jnp.max(su, axis=0) * SL2
                            w = jnp.exp2(su * SL2 - m[None])
                            s_s[(pos + u) * NG + q, :, cs] = jnp.sum(w, axis=0)
                            if own:
                                m_s[(pos + u) * NG + q, :, cs] = m
                            else:
                                m_s[(pos + u) * NG + q, :, cs] = jnp.where(seen(pos + u), m, LOW)
                            w_s[pos + u, q * MG:(q + 1) * MG, cs] = w.reshape(MG, CS)

            def local(body, init):
                return body(PROMPT, REACH + 1, True, init)

            def over(body, init):
                return local(body, lax.fori_loop(0, whole, lambda c, x: body(0, PROMPT, False, x), init))

            def p1(pos, nb, diag, x):
                first_pass(pos, nb, diag, False)
                return x

            def p1_both(pos, nb, diag, x):
                first_pass(pos, nb, diag, True)
                return x

            @pl.when(i == 0)
            def _():
                local_arrive()
                local(p1_both, 0)
                chain_arrive()
                lax.fori_loop(0, whole, lambda c, x: p1_both(y * CBP, CBP, False, x), 0)
                rest_arrive()
                lax.fori_loop(0, whole, lambda c, x: p1_both((1 - y) * CBP, CBP, False, x), 0)

            @pl.when(i > 0)
            def _():
                over(p1, 0)

            m = m_s[...]
            top = jnp.max(jnp.max(m, axis=0), axis=0, keepdims=True)
            f = jnp.exp2(m - top[None])
            tot = jnp.sum(jnp.sum(f * s_s[...], axis=0), axis=0, keepdims=True)
            m_s[...] = f * (1.0 / tot)[None]

            drows = dn[t]
            def p3_with(have_dp, pos, nb, acc):
                r0 = row0(pos)
                vc = kv_ref[pl.ds(r0, nb * BLK), BLK:2 * BLK]
                accs, ps = [], []
                for x in range(0, RT, CS):
                    cs = slice(x, x + CS)
                    dp = None if have_dp else nn(vc, dt[t, :, cs])
                    a = acc[:, cs]
                    pu = []
                    for u in range(nb):
                        du = dp_s[pos + u, :, cs] if have_dp else dp[u * BLK:(u + 1) * BLK]
                        parts = []
                        for q in range(NG):
                            wq = w_s[pos + u, q * MG:(q + 1) * MG, cs].reshape(MG // 8, 8, CS)
                            parts.append((wq * m_s[(pos + u) * NG + q, :, cs][None]).reshape(MG, CS))
                        ch = jnp.concatenate(parts, axis=0)
                        chb = ch.astype(BF)
                        w_s[pos + u, :, cs] = ch
                        if not have_dp:
                            dp_s[pos + u, :, cs] = du
                        a = a + jnp.sum((chb.astype(F32) * du).reshape(BLK // 8, 8, CS), axis=0)
                        pu.append(chb)
                    accs.append(a)
                    ps.append(jnp.concatenate(pu, axis=0))
                p = jnp.concatenate(ps, axis=1)
                rows = pl.ds(r0, nb * BLK)
                dv_ref[rows, :] += nn(p, drows)
                return jnp.concatenate(accs, axis=1)

            @pl.when(i == 0)
            def _():
                dl_s[...] = over(lambda pos, nb, diag, acc: p3_with(True, pos, nb, acc), jnp.zeros((8, RT), F32))

            @pl.when(i > 0)
            def _():
                dl_s[...] = over(lambda pos, nb, diag, acc: p3_with(False, pos, nb, acc), jnp.zeros((8, RT), F32))

            delta = dl_s[...]
            @pl.when(i == 3)
            def _():
                hand_over(0, 0, OWN)
                for j in (0, 1):
                    cp_a(0, j).start()
                local_start(0)

            delta = jnp.sum(delta, axis=0, keepdims=True)
            qrows = qn[t]

            def key_side(pos, nb, keep):
                rr = pl.ds(row0(pos), nb * BLK)
                dss = []
                for u in range(nb):
                    ds = (w_s[pos + u] * (dp_s[pos + u] - delta)).astype(BF)
                    if keep:
                        w_s[pos + u] = ds.astype(F32)
                    dss.append(ds)
                ds = jnp.concatenate(dss, axis=0) if nb > 1 else dss[0]
                dk_ref[rr, :] += nn(ds, qrows)
                return ds

            def query_side(pos, nb, ds):
                slot = row0(pos) // BLK
                ktc = jnp.concatenate([kt[slot + u] for u in range(nb)], axis=1) if nb > 1 else kt[slot]
                dq_s[i] += nn(ktc, ds)

            def p4(pos, nb, diag, dq):
                query_side(pos, nb, key_side(pos, nb, False))
                return dq

            def p4_keys(pos, nb, diag, dq):
                key_side(pos, nb, True)
                return dq

            def p4_queries(pos, nb, diag, dq):
                parts = [w_s[pos + u].astype(BF) for u in range(nb)]
                query_side(pos, nb, jnp.concatenate(parts, axis=0) if nb > 1 else parts[0])
                return dq

            dq_s[i] = jnp.zeros((BLK, RT), F32)

            @pl.when(i < 3)
            def _():
                lax.fori_loop(0, pc, lambda c, x: p4(c * CBP, CBP, False, x), 0)
                local(p4, 0)

            @pl.when(i == 3)
            def _():
                for j in (0, 1):
                    @pl.when(j < pc)
                    def _(j=j):
                        p4_keys(j * CBP, CBP, False, 0)

                    hand_over(1, 8 * j, 8 * j + 8)
                    cp_a(1, j).start()
                stage_b(0)
                local(p4_keys, 0)
                hand_over(1, PROMPT, OWN)
                stage_b(1)
                local_start(1)
                lax.fori_loop(0, pc, lambda c, x: p4_queries(c * CBP, CBP, False, x), 0)
                local(p4_queries, 0)

            return 0

        lax.fori_loop(0, TPB, per_tile, 0)
        return 0

    lax.fori_loop(0, 4, per_block, 0)

    def finish(i, _):
        dqt = dq_s[i]
        dq = dqt.T * SCALE
        rows = pl.ds(pl.multiple_of(i * BLK, BLK), BLK)
        part = jnp.zeros((8, BLK), F32)
        for u in range(HT):
            cols = pl.ds(pl.multiple_of(u * BLK, BLK), BLK)
            x = q_ref[rows, cols].astype(F32)
            r = lax.rsqrt(jnp.mean(x * x, axis=-1, keepdims=True) + 1e-6)
            unit = x * r
            dqu = dq[u * BLK:(u + 1) * BLK]
            both = dqu * unit
            part = part + jnp.sum(both.reshape(BLK // 8, 8, BLK), axis=0)
            mean = jnp.mean(both * gain, axis=-1, keepdims=True)
            gq_ref[rows, cols] = (r * (dqu * gain - unit * mean)).astype(BF)
        qpart[...] += part
        return 0

    lax.fori_loop(0, 4, finish, 0)
    leaving = pltpu.make_async_copy(gq_ref, gq_out, out_sem.at[0])
    leaving.start()

    def key_part(k, acc):
        rr = pl.ds(pl.multiple_of(k * BLK, BLK), BLK)
        both = dk_ref[rr, :] * kv_ref[rr, 0:BLK].astype(F32)
        return acc + jnp.sum(both.reshape(BLK // 8, 8, BLK), axis=0)

    kpart = lax.fori_loop(0, SLOTS, key_part, jnp.zeros((8, BLK), F32))
    kgain = kg_ref[...]
    gown[...] = jnp.zeros_like(gown)
    gown[0:1, :] = jnp.sum(qpart[...], axis=0, keepdims=True)
    gown[1:2, :] = jnp.sum(kpart, axis=0, keepdims=True) * SCALE / kgain
    cg = [copy_to(gown, gall.at[me], send_g.at[o - 1], recv_g.at[me], dp, lax.rem(me + o, 16)) for o in range(1, 16)]
    ch = [copy_to(gsum, gdp.at[dp], send_g.at[14 + o], recv_g.at[16 + dp], lax.rem(dp + o, 8), me) for o in range(1, 8)]
    for q in cg:
        q.start()
    gall[me] = gown[...]
    for x in (0, 1):
        for h in (0, 1):
            cp_b(x, h).wait_send()
        local_mid(x)
    stage_c(0)
    stage_c(1)
    for o in range(1, 16):
        p = lax.rem(me + o, 16)
        copy_to(gown, gall.at[p], send_g.at[o - 1], recv_g.at[p], dp, p).wait_recv()
    total = gall[0]
    for o in range(1, 16):
        total = total + gall[o]
    gsum[...] = total
    for q in ch:
        q.start()
    gdp[dp] = total
    stage_d(0)
    stage_d(1)
    stage_e(0)
    local_end(0)
    gv_ref[...] = tot[0].astype(BF)
    stage_e(1)
    local_end(1)
    x = k_ref[...].astype(F32)
    r = lax.rsqrt(jnp.mean(x * x, axis=-1, keepdims=True) + 1e-6)
    unit = x * r
    dk = tot[1] * SCALE
    mean = jnp.mean(dk * unit * kgain, axis=-1, keepdims=True)
    gk_ref[...] = (r * (dk * kgain - unit * mean)).astype(BF)
    for o in range(1, 8):
        p = lax.rem(dp + o, 8)
        copy_to(gsum, gdp.at[p], send_g.at[14 + o], recv_g.at[16 + p], p, me).wait_recv()
    total = gdp[0]
    for o in range(1, 8):
        total = total + gdp[o]
    gain_ref[...] = total
    for q in cg + ch:
        q.wait_send()
    leaving.wait()
    for x in (0, 1):
        for h in (0, 1):
            cp_a(x, h).wait_send()

        @pl.when(z != 0)
        def _(x=x):
            for h in (0, 1):
                cp_c(x, h, 0, 0).wait_send()

        @pl.when(has_prev & (c == 0))
        def _(x=x):
            hand_full(x).wait_send()

        @pl.when(has_prev & (c == 1))
        def _(x=x):
            hand_half(x).wait_send()

        @pl.when(has_prev)
        def _(x=x):
            back(x).wait_send()

        @pl.when(sends_near)
        def _(x=x):
            near_back(x).wait_send()

        @pl.when(sends_far)
        def _(x=x):
            far_back(x).wait_send()

    @pl.when(z == 0)
    def _():
        for k in range(8):
            kv_z(0, 1, k).wait_send()

    @pl.when((z == 1) | (z == 3))
    def _():
        for k in range(2):
            kv_z(0, 1, k).wait_send()

    for h in range(4):
        kv_y(h).wait_send()
        kv_s(0, h).wait_send()
        kv_s(1, h).wait_send()

    @pl.when((c == 0) & (n >= 2))
    def _():
        own_sib.wait_send()

    @pl.when(has_next)
    def _():
        ahead.wait_send()

    @pl.when(sends_kfar)
    def _():
        kfar.wait_send()

    @pl.when(has_prev & (c == 1))
    def _():
        relay_full.wait_send()

    @pl.when(has_prev & (c == 0))
    def _():
        relay_half.wait_send()


def fused(lens, frm, qg, kg, q, do, k, v):
    dma = pltpu.SemaphoreType.DMA
    rows = SLOTS * BLK
    tiles = 4096 // RT
    pair = pltpu.VMEM((2, GRP, BLK), BF)
    anywhere = pl.BlockSpec(memory_space=pl.ANY)
    wide, narrow = pltpu.VMEM((GRP, 8 * BLK), BF), pltpu.VMEM((GRP, BLK), BF)
    two = pltpu.VMEM((2, 2, GRP, BLK), BF)
    return pl.pallas_call(
        fused_kernel,
        out_shape=(
            jax.ShapeDtypeStruct((512, 1024), BF),
            jax.ShapeDtypeStruct((GRP, BLK), BF),
            jax.ShapeDtypeStruct((GRP, BLK), BF),
            jax.ShapeDtypeStruct((8, BLK), F32),
        ),
        in_specs=[SM, SM, VM, VM] + [anywhere] * 4,
        out_specs=(anywhere, VM, VM, VM),
        scratch_shapes=[
            wide, wide, narrow, narrow, wide, dma((4,)), dma((1,)),
            pltpu.VMEM((rows, 2 * BLK), BF),
            pltpu.VMEM((tiles, RT, BLK), BF),
            pltpu.VMEM((tiles, BLK, RT), BF),
            pltpu.VMEM((tiles, RT, BLK), BF),
            pltpu.VMEM((tiles, BLK, RT), BF),
            pltpu.VMEM((SLOTS, BLK, BLK), BF),
            pltpu.VMEM((POS, BLK, RT), F32),
            pltpu.VMEM((POS, BLK, RT), F32),
            pltpu.VMEM((POS * NG, 8, RT), F32),
            pltpu.VMEM((POS * NG, 8, RT), F32),
            pltpu.VMEM((8, RT), F32),
            pltpu.VMEM((tiles, BLK, RT), F32),
            pltpu.VMEM((rows, BLK), F32),
            pltpu.VMEM((rows, BLK), F32),
            pltpu.VMEM((8, BLK), F32),
            pltpu.VMEM((2, OWN * BLK, BLK), BF),
            two, pair, two, pltpu.VMEM((3, 2, GRP, BLK), BF), pair, pair, pair, pair,
            pltpu.VMEM((2, GRP, BLK), F32),
            pltpu.VMEM((8, BLK), F32),
            pltpu.VMEM((8, BLK), F32),
            pltpu.VMEM((16, 8, BLK), F32),
            pltpu.VMEM((8, 8, BLK), F32),
        ] + [dma((m,)) for m in (8, 4, 4, 4, 8, 8, 5, 3, 4, 4, 4, 4, 4, 8, 8, 8, 22, 24)],
        compiler_params=pltpu.CompilerParams(
            collective_id=0, has_side_effects=True, vmem_limit_bytes=62 * 1024 * 1024),
    )(lens, frm, qg, kg, q, do, k, v)


PIECES = 4


def hand_out_kernel(gains_ref, gq_ref, gk_ref, gv_ref, oq_ref, ok_ref, ov_ref, gq_gain_ref, gk_gain_ref,
                    bq, bk, bv, sin, sout):
    step = bq.shape[0] // PIECES
    legs = [(gq_ref.at[pl.ds(j * step, step)], bq.at[pl.ds(j * step, step)], oq_ref.at[pl.ds(j * step, step)])
            for j in range(PIECES)]
    legs += [(gk_ref, bk, ok_ref), (gv_ref, bv, ov_ref)]
    into = [pltpu.make_async_copy(x, m, sin.at[j]) for j, (x, m, _) in enumerate(legs)]
    out = [pltpu.make_async_copy(m, o, sout.at[j]) for j, (_, m, o) in enumerate(legs)]
    for copy in into:
        copy.start()
    gq_gain_ref[...] = gains_ref[0, :]
    gk_gain_ref[...] = gains_ref[1, :]
    for j in range(len(legs)):
        into[j].wait()
        out[j].start()
    for copy in out:
        copy.wait()


def hand_out(gains, gq, gk, gv):
    anywhere = pl.BlockSpec(memory_space=pl.ANY)
    flat = jax.ShapeDtypeStruct((BLK,), F32)
    dma = pltpu.SemaphoreType.DMA
    return pl.pallas_call(
        hand_out_kernel,
        out_shape=tuple(jax.ShapeDtypeStruct(t.shape, t.dtype) for t in (gq, gk, gv)) + (flat, flat),
        in_specs=[VM, anywhere, anywhere, anywhere],
        out_specs=(anywhere, anywhere, anywhere, VM, VM),
        scratch_shapes=[pltpu.VMEM(t.shape, t.dtype) for t in (gq, gk, gv)] + [dma((PIECES + 2,)), dma((PIECES + 2,))],
    )(gains, gq, gk, gv)


def body(q_raw, k_raw, values, d_out, q_gain, k_gain, resp_len, block_parent, block_from):
    gq, gk, gv, gains = fused(resp_len[0], block_from[0], q_gain.reshape(1, BLK), k_gain.reshape(1, BLK),
                              q_raw[0], d_out[0], k_raw[0], values[0])
    gq, gk, gv, q_gain_grad, k_gain_grad = hand_out(gains, gq, gk, gv)
    return gq[None], gk[None], gv[None], q_gain_grad, k_gain_grad


def solution(mesh):
    tok = P("dp", "ctx", None)
    return jax.shard_map(
        body,
        mesh=mesh,
        in_specs=(tok, tok, tok, tok, P(), P(), P("dp", None), P("dp", None), P("dp", "ctx")),
        out_specs=(tok, tok, tok, P(), P()),
        check_vma=False,
    )
```
